512 devices in a mesh: sec: 64 (over z, x), mpo: 8 (over y, core).
Axes of the slice: x: 4, y: 4, z: 16, core: 2. Of those that a mesh axis runs over, the one named last changes fastest.
Arguments:
- start_vector: float32 [512, 8192], P('sec'), may hold values from -6 to 6
- precond_diag: float32 [512, 8192], P('sec'), may hold values from 1 to 10
- left_env: float32 [24, 512, 8], P('mpo', 'sec'), may hold values from -2 to 2
- right_env: float32 [24, 8192, 128], P('mpo', 'sec'), may hold values from -0.109375 to 0.109375
- right_shift: int32 [24], P('mpo'), may hold values from 0 to 63
- sector_length: int32 [64], P('sec'), may hold values from 1 to 8, 384 in all
Outputs:
- basis_three: float32 [512, 8192], P('sec', 'mpo')
- image_three: float32 [512, 8192], P('sec', 'mpo')
The draws below stay inside these ranges and needn't reach their ends.
Inputs may be any that keep to these rules, and one draw needn't show every extreme that they name: `sector_length`: each sector has 1 to 8 live rows, and some sector has exactly 8; they add up to 384.
All inputs are finite; a program needn't handle non-finite values. No bound on the sum of `sector_length` on one device may be relied on, other than what follows from the above.
Results may differ from the reference program's by a relative error of at most 0.0003.
Values sent between devices are 32-bit elements; how exact they have to be, the bound alone decides.
A program may use at most 64 MiB of HBM per device.

```python
import math
import jax
import jax.numpy as jnp
import numpy as np
from jax import lax

ROWS_DEV = 8
DR = 8192
BR = 128
TERMS = 24
DL = 512
NRS = 64
N_SEC = 64


def plant(values, rng, smallest, largest):
    shape = values.shape
    spot = [jax.random.randint(jax.random.fold_in(rng, axis), (), 0, shape[axis]) for axis in range(len(shape))]
    values = values.at[tuple(spot)].set(smallest)
    longest = shape.index(max(shape))
    spot[longest] = (spot[longest] + 1) % shape[longest]
    return values.at[tuple(spot)].set(largest)


def shard_levels(key, extent, cuts, smallest, largest):
    gain, own = 1.0, jax.random.fold_in(key, 6)
    for axis_at, parts in cuts:
        heights = jnp.exp(jax.random.uniform(jax.random.fold_in(own, axis_at), (parts,), jnp.float32, smallest / len(cuts), largest / len(cuts)))
        gain = gain * jnp.repeat(heights, extent[axis_at] // parts).reshape([-1 if axis == axis_at else 1 for axis in range(len(extent))])
    return gain


def profile(amount, total, reach, skew):
    loads = [(1 << 20) // math.isqrt(standing ** skew) + 1 for standing in range(2, amount + 1)]
    spare, counts = total - reach - (amount - 1), [1] * (amount - 1)
    while spare > 0:
        candidates = [i for i in range(amount - 1) if counts[i] < reach]
        mass, left = sum([loads[i] for i in candidates]), spare
        for i in candidates:
            more = min(reach - counts[i], max(1, left * loads[i] // mass), spare)
            counts[i] = counts[i] + more
            spare = spare - more
    return np.array([reach] + counts)


def ragged_sizes(key, amount, total, most, skew):
    if amount == 2:
        one = jax.random.randint(key, (), max(1, total - most), min(most, total - 1) + 1)
        return jnp.stack([one, total - one])
    sizes = jnp.asarray(profile(amount, total, most, skew), jnp.int32)
    pairs = (amount - 1) // 2
    source_of, sink = sizes[1:1 + 2 * pairs:2], sizes[2:2 + 2 * pairs:2]
    slack = jnp.minimum(source_of - 1, most - sink)
    passed = jax.random.randint(jax.random.fold_in(key, 1), (pairs,), 0, 1 << 20) % (slack + 1)
    sizes = sizes.at[1:1 + 2 * pairs:2].set(source_of - passed).at[2:2 + 2 * pairs:2].set(sink + passed)
    return sizes[jax.random.permutation(jax.random.fold_in(key, 2), amount)]


def normal_values(stream_key, extent, width, most, cuts=(), kind=jnp.bfloat16):
    array = jax.random.normal(stream_key, extent, jnp.float32) * width
    if len(cuts) > 0:
        array = shard_levels(stream_key, extent, cuts, -0.22, 0.18) * array
    return jnp.clip(array, min=-most, max=most).astype(kind)


def setup_inputs(seed: int = 0) -> dict:
    splits = jax.random.split(jax.random.key(seed), 7)
    start_vector = normal_values(splits[0], (DL, DR), 1.0, 6.0, ((0, 64),), jnp.float32)
    precond_diag = jnp.clip(jnp.exp(math.log(10.0) - 2.3025851 * jax.random.uniform(splits[1], (DL, DR), jnp.float32) ** shard_levels(splits[1], (DL, DR), ((0, 64),), -0.2, 0.2)), 1.0, 10.0)
    left_env = normal_values(splits[2], (TERMS, DL, ROWS_DEV), ROWS_DEV ** -0.5, 2.0, ((0, 8), (1, 64)), jnp.float32)
    right_env = normal_values(splits[3], (TERMS, DR, BR), (BR * TERMS) ** -0.5, 0.109375, ((0, 8), (1, 64)), jnp.float32)
    right_shift = plant(jax.random.randint(splits[4], (TERMS,), 0, NRS), jax.random.fold_in(splits[4], 1), 0, NRS - 1).astype(jnp.int32)
    sector_length = ragged_sizes(splits[5], N_SEC, ROWS_DEV * N_SEC * 3 // 4, ROWS_DEV, 2).astype(jnp.int32)
    return {"start_vector": start_vector, "precond_diag": precond_diag, "left_env": left_env, "right_env": right_env, "right_shift": right_shift, "sector_length": sector_length}


epsilon = 1e-06

def inner_sum(left, right):
    return jnp.sum(left * right)

def image_of(vector, left_env, right_env, right_shift, live):
    sectors = DL // ROWS_DEV
    stacked = vector.reshape(sectors, ROWS_DEV, DR)
    left_blocks = left_env.reshape(TERMS, sectors, ROWS_DEV, ROWS_DEV)
    right_blocks = right_env.reshape(TERMS, NRS, BR, BR)

    def one_term(carry, pieces):
        left_part, right_part, offset = pieces
        mixed = jnp.einsum('sij,sjc->sic', left_part, stacked, precision=lax.Precision.HIGHEST)
        mixed = jnp.roll(mixed.reshape(sectors, ROWS_DEV, NRS, BR), -offset, axis=2)
        result = jnp.einsum('sinb,nbc->sinc', mixed, right_part, precision=lax.Precision.HIGHEST)
        return (carry + result.reshape(DL, DR), None)
    summed, _ = lax.scan(one_term, jnp.zeros((DL, DR), jnp.float32), (left_blocks, right_blocks, right_shift))
    return summed * live

def reference(start_vector, precond_diag, left_env, right_env, right_shift, sector_length):
    positions = jnp.arange(DL, dtype=jnp.int32)
    owners = jnp.repeat(sector_length, ROWS_DEV)
    live = (positions % ROWS_DEV < owners).astype(jnp.float32)[:, None]
    cells = jnp.float32(DL * DR)
    masked = start_vector * live
    basis_one = masked * jnp.sqrt(cells / (inner_sum(masked, masked) + epsilon))
    image_one = image_of(basis_one, left_env, right_env, right_shift, live)
    rayleigh = inner_sum(basis_one, image_one) / cells
    correction = (image_one - rayleigh * basis_one) / precond_diag
    coeff_one = inner_sum(basis_one, correction) / cells
    update = correction - coeff_one * basis_one
    basis_two = update * jnp.sqrt(cells / (inner_sum(update, update) + epsilon))
    image_two = image_of(basis_two, left_env, right_env, right_shift, live)
    coupling = (inner_sum(basis_one, image_two) + inner_sum(basis_two, image_one)) / (2.0 * cells)
    second = inner_sum(basis_two, image_two) / cells
    half_gap = (rayleigh - second) / 2.0
    ritz_value = (rayleigh + second) / 2.0 - jnp.sqrt(half_gap * half_gap + coupling * coupling)
    rotation = jnp.arctan2(coupling, half_gap) / 2.0
    weight_one = -jnp.sin(rotation)
    weight_two = jnp.cos(rotation)
    ritz_vector = weight_one * basis_one + weight_two * basis_two
    ritz_image = weight_one * image_one + weight_two * image_two
    correction_two = (ritz_image - ritz_value * ritz_vector) / precond_diag
    proj_one = inner_sum(basis_one, correction_two) / cells
    proj_two = inner_sum(basis_two, correction_two) / cells
    update_two = correction_two - proj_one * basis_one - proj_two * basis_two
    basis_three = update_two * jnp.sqrt(cells / (inner_sum(update_two, update_two) + epsilon))
    image_three = image_of(basis_three, left_env, right_env, right_shift, live)
    return (basis_three, image_three)
```

```python
import functools

import jax
import jax.numpy as jnp
from jax import lax
from jax.experimental import pallas as pl
from jax.experimental.pallas import tpu as pltpu
from jax.sharding import PartitionSpec as P

MESH = pl.DeviceIdType.MESH
F32 = jnp.float32
BF16 = jnp.bfloat16

NX, NY, NZ = 4, 4, 16
ROWS, BR, NBLK = 8, 128, 64
TPD = 3
KS = 4
CELLS = float(512 * 8192)
EPS = 1e-6


def kernel(
    start_ref,
    diag_ref,
    left_ref,
    right_ref,
    shift_ref,
    length_ref,
    basis_ref,
    image_ref,
    rbuf,
    r_hi,
    r_lo,
    v1,
    v2,
    v3,
    y_own,
    y_in1,
    y_in2,
    y_in3,
    piece,
    src_gd,
    got_gd,
    left_tile,
    left_row,
    left_all,
    shift_tile,
    shift_all,
    shift_sm,
    left_wide,
    mask,
    dz,
    dp,
    dc,
    out_src,
    out_got,
    w_send,
    w_recv,
    ag_send,
    ag_plus,
    ag_minus,
    ag_core,
    y_send,
    y_recv,
    dot_send,
    dot_recv,
    st_send,
    st_recv,
    sm_sem,
    out_send,
    out_recv,
):
    sec = lax.axis_index("sec")
    mpo = lax.axis_index("mpo")
    z, x = lax.div(sec, 4), lax.rem(sec, 4)
    y, c = lax.div(mpo, 2), lax.rem(mpo, 2)

    def dev(xx, yy, zz, cc):
        return (zz * 4 + xx, yy * 2 + cc)

    def send(src, dst, send_sem, recv_sem, where):
        pltpu.make_async_remote_copy(
            src_ref=src,
            dst_ref=dst,
            send_sem=send_sem,
            recv_sem=recv_sem,
            device_id=where,
            device_id_type=MESH,
        ).start()

    def wait(ref, sem):
        pltpu.make_async_copy(ref, ref, sem).wait()

    up, down = lax.rem(z + 1, NZ), lax.rem(z + NZ - 1, NZ)
    other = dev(x, y, z, 1 - c)
    zdevs = [dev(x, y, lax.rem(z + d, NZ), c) for d in range(1, NZ)]
    ydevs = [dev(x, lax.rem(y + d, NY), z, c) for d in range(1, NY)]

    barrier = pltpu.get_barrier_semaphore()
    partners = zdevs + ydevs + [dev(lax.rem(x + 1, NX), y, z, c), dev(lax.rem(x + 3, NX), y, z, c), other]
    for p in partners:
        pl.semaphore_signal(barrier, inc=1, device_id=p, device_id_type=MESH)

    sub = lax.broadcasted_iota(jnp.int32, (ROWS, BR), 0)
    live0 = jnp.where(sub < length_ref[0], 1.0, 0.0).astype(F32)
    for m in range(NBLK):
        src_gd[m, 0] = start_ref[:, m * BR : (m + 1) * BR] * live0
        src_gd[m, 1] = diag_ref[:, m * BR : (m + 1) * BR]
    left_tile[...] = jnp.zeros((ROWS, BR), F32)
    for t in range(TPD):
        left_tile[:, t * ROWS : (t + 1) * ROWS] = left_ref[t]
    left_tile[:, TPD * ROWS : TPD * ROWS + 1] = jnp.full((ROWS, 1), length_ref[0].astype(F32), F32)
    shift_tile[...] = jnp.where(sub == 0, shift_ref[0], jnp.where(sub == 1, shift_ref[1], shift_ref[2]))

    pl.semaphore_wait(barrier, len(partners))

    p1 = (1 - c) * x + c * y
    p2 = (1 - c) * y + c * x

    def axis1(d):
        return dev(lax.rem(x + d * (1 - c) + 4, 4), lax.rem(y + d * c + 4, 4), z, c)

    def axis2(d):
        return dev(lax.rem(x + d * c + 4, 4), lax.rem(y + d * (1 - c) + 4, 4), z, c)

    def slot(d1, d2):
        q1, q2 = lax.rem(p1 + d1 + 4, 4), lax.rem(p2 + d2 + 4, 4)
        return (1 - c) * (q1 * 4 + q2) + c * (q2 * 4 + q1)

    H = BR // 2

    def part(d1, d2, half):
        s = slot(d1, d2)
        if half is None:
            return rbuf.at[s]
        return rbuf.at[s, :, pl.ds(half * H, H), :]

    def send_axis1():
        own = slot(0, 0)
        send(right_ref, rbuf.at[own], w_send, w_recv.at[0], axis1(1))
        send(right_ref, rbuf.at[own], w_send, w_recv.at[1], axis1(-1))

    def send_axis2(d1):
        src = right_ref if d1 == 0 else part(d1, 0, None)
        i = d1 % 4
        s = slot(d1, 0)
        send(src, rbuf.at[s], w_send, w_recv.at[4 + 4 * i], axis2(1))
        send(src, rbuf.at[s], w_send, w_recv.at[5 + 4 * i], axis2(-1))

    def first_of_axis1():
        wait(part(-1, 0, None), w_recv.at[0])
        send(part(-1, 0, 0), part(-1, 0, 0), w_send, w_recv.at[2], axis1(1))
        send_axis2(-1)

    def second_of_axis1():
        wait(part(1, 0, None), w_recv.at[1])
        send(part(1, 0, 1), part(1, 0, 1), w_send, w_recv.at[3], axis1(-1))
        send_axis2(1)

    def third_of_axis1():
        wait(part(2, 0, 0), w_recv.at[2])
        wait(part(2, 0, 1), w_recv.at[3])
        send_axis2(2)

    def near_axis2(d1):
        i = d1 % 4
        wait(part(d1, -1, None), w_recv.at[4 + 4 * i])
        send(part(d1, -1, 0), part(d1, -1, 0), w_send, w_recv.at[6 + 4 * i], axis2(1))
        wait(part(d1, 1, None), w_recv.at[5 + 4 * i])
        send(part(d1, 1, 1), part(d1, 1, 1), w_send, w_recv.at[7 + 4 * i], axis2(-1))

    def far_axis2(d1):
        i = d1 % 4
        wait(part(d1, 2, 0), w_recv.at[6 + 4 * i])
        wait(part(d1, 2, 1), w_recv.at[7 + 4 * i])

    send_axis1()
    send_axis2(0)

    src_line = lax.rem(z, 4)
    is_src = src_line == y
    kown = lax.div(z, 4)
    for p in ydevs:
        send(shift_tile, shift_all.at[y], st_send.at[0], st_recv.at[0], p)
    shift_all[y] = shift_tile[...]

    def blocks_of(zz):
        return pl.ds(4 * zz + 2 * c, 2)

    @pl.when(is_src)
    def _():
        for d in range(1, NZ):
            zt = lax.rem(z + d, NZ)
            send(src_gd.at[blocks_of(zt)], got_gd.at[kown], st_send.at[1], st_recv.at[1], dev(x, y, zt, c))
        got_gd[kown] = src_gd[blocks_of(z)]
        left_row[y] = left_tile[...]
        wait(got_gd.at[pl.ds(0, 3)], st_recv.at[1])

    @pl.when(jnp.logical_not(is_src))
    def _():
        send(left_tile, left_row.at[y], st_send.at[2], st_recv.at[2], dev(x, src_line, z, c))
        wait(got_gd, st_recv.at[1])

    G, D, GD, HV, Q, HD, U, K, UD = range(9)
    mine = blocks_of(z)
    for b in range(2):
        for k in range(KS):
            g = got_gd[k, b, 0]
            d = got_gd[k, b, 1]
            gd = g / d
            piece[G, k, b] = g
            piece[D, k, b] = d
            piece[GD, k, b] = gd
    v1[pl.ds(0, 4), mine] = piece[G]
    v1[pl.ds(4, 4), mine] = piece[GD]

    def ring(phase, v, width):
        def at(ch, zz):
            return v.at[pl.ds(ch * width, width), blocks_of(zz)]

        def start():
            for ch in range(2):
                send(at(ch, z), at(ch, z), ag_send.at[phase], ag_plus.at[phase, ch, 0], dev(x, y, up, c))
                send(at(ch, z), at(ch, z), ag_send.at[phase], ag_minus.at[phase, ch, 0], dev(x, y, down, c))
            for ch in range(2):
                send(at(ch, z), at(ch, z), ag_send.at[phase], ag_core.at[phase], other)

        def step(i):
            zp, zm = lax.rem(z + NZ - i, NZ), lax.rem(z + i, NZ)
            for ch in range(2):
                wait(at(ch, zp), ag_plus.at[phase, ch, i - 1])
                if i < 8:
                    send(at(ch, zp), at(ch, zp), ag_send.at[phase], ag_plus.at[phase, ch, i], dev(x, y, up, c))
                send(at(ch, zp), at(ch, zp), ag_send.at[phase], ag_core.at[phase], other)
                if i < 8:
                    wait(at(ch, zm), ag_minus.at[phase, ch, i - 1])
                    if i < 7:
                        send(at(ch, zm), at(ch, zm), ag_send.at[phase], ag_minus.at[phase, ch, i], dev(x, y, down, c))
                    send(at(ch, zm), at(ch, zm), ag_send.at[phase], ag_core.at[phase], other)

        def finish():
            wait(v.at[:, pl.ds(0, 32)], ag_core.at[phase])

        def sent():
            wait(v.at[:, pl.ds(0, 62)], ag_send.at[phase])

        return start, step, finish, sent

    start, step, finish, sent1 = ring(0, v1, 4)
    start()

    @pl.when(is_src)
    def _():
        wait(left_row.at[pl.ds(0, 3)], st_recv.at[2])
        for d in range(1, NZ):
            send(left_row, left_all.at[kown], st_send.at[2], st_recv.at[3], dev(x, y, lax.rem(z + d, NZ), c))
        left_all[kown] = left_row[...]

    first_of_axis1()
    step(1)
    second_of_axis1()
    near_axis2(0)
    step(2)
    third_of_axis1()
    step(3)
    near_axis2(-1)
    step(4)
    near_axis2(1)
    step(5)
    far_axis2(0)
    step(6)
    near_axis2(2)
    step(7)
    far_axis2(-1)
    far_axis2(1)
    step(8)

    wait(shift_all.at[pl.ds(0, 3)], st_recv.at[0])
    to_sm = pltpu.make_async_copy(shift_all, shift_sm, sm_sem)
    to_sm.start()

    @pl.when(is_src)
    def _():
        wait(left_all.at[pl.ds(0, 3)], st_recv.at[3])

    @pl.when(jnp.logical_not(is_src))
    def _():
        wait(left_all, st_recv.at[3])

    def widen(i, carry):
        k, yy = lax.div(i, 4), lax.rem(i, 4)
        tile = left_all[k, yy]
        for t in range(TPD):
            for j in range(ROWS):
                lane = t * ROWS + j
                left_wide[yy * TPD + t, k, j] = jnp.broadcast_to(tile[:, lane : lane + 1], (ROWS, BR))
        return carry

    lax.fori_loop(0, 16, widen, 0)
    subf = sub.astype(F32)
    for k in range(KS):
        length = jnp.broadcast_to(left_all[k, 0][:, TPD * ROWS : TPD * ROWS + 1], (ROWS, BR))
        mask[k] = jnp.where(subf < length, 1.0, 0.0).astype(F32)

    rbuf[slot(0, 0)] = right_ref[...]
    far_axis2(2)

    def cut(i, carry):
        for t in range(TPD):
            r = rbuf[i, t]
            hi = r.astype(BF16)
            r_hi[i, t] = hi
            r_lo[i, t] = (r - hi.astype(F32)).astype(BF16)
        return carry

    lax.fori_loop(0, 16, cut, 0)
    to_sm.wait()
    finish()

    def product(v, nk):
        rows = nk * ROWS
        y_own[:, pl.ds(0, nk)] = jnp.zeros((4, nk, ROWS, BR), F32)

        def body(i, carry):
            yy, t = lax.div(i, TPD), lax.rem(i, TPD)
            shift = shift_sm[yy, t, 0]
            for n in range(4):
                m = 4 * z + n + shift
                m = jnp.where(m >= NBLK, m - NBLK, m)
                tiles = []
                for k in range(nk):
                    src = v[k, m]
                    total = None
                    for j in range(ROWS):
                        term = left_wide[i, k % KS, j] * src[j : j + 1, :]
                        total = term if total is None else total + term
                    tiles.append(total)
                p = jnp.concatenate(tiles, axis=0)
                hi = p.astype(BF16)
                lo = (p - hi.astype(F32)).astype(BF16)
                rh = r_hi[n * 4 + yy, t]
                rl = r_lo[n * 4 + yy, t]
                both = jnp.dot(jnp.concatenate([hi, lo], axis=0), rh, preferred_element_type=F32)
                more = jnp.dot(hi, rl, preferred_element_type=F32)
                res = both[:rows] + both[rows:] + more
                y_own[n, pl.ds(0, nk)] += res.reshape(nk, ROWS, BR)
            return carry

        lax.fori_loop(0, 4 * TPD, body, 0)

    def swap(phase, y_in, nk):
        send(
            y_own.at[pl.ds(2 * (1 - c), 2), pl.ds(0, nk)], y_in, y_send.at[phase], y_recv.at[phase], other
        )
        wait(y_in, y_recv.at[phase])

    def swapped(phase, y_in):
        wait(y_in, y_send.at[phase])

    product(v1, 8)
    swap(0, y_in1, 8)
    for b in range(2):
        for k in range(KS):
            h = (y_own[2 * c + b, k] + y_in1[b, k]) * mask[k]
            q = (y_own[2 * c + b, KS + k] + y_in1[b, KS + k]) * mask[k]
            piece[HV, k, b] = h
            piece[Q, k, b] = q
            piece[HD, k, b] = h / piece[D, k, b]
    v2[:, mine] = piece[HD]
    start, step, finish, sent2 = ring(1, v2, 2)
    start()

    def dot(a, b):
        prod = (piece[a] * piece[b]).reshape(KS * 2, ROWS, BR)
        return jnp.sum(jnp.sum(prod, axis=0), axis=0, keepdims=True)

    def dots_z(g, pairs):
        for r, (a, b) in enumerate(pairs):
            dz[g, z, r : r + 1, :] = dot(a, b)
        for p in zdevs:
            send(dz.at[g, z], dz.at[g, z], dot_send.at[g, 0], dot_recv.at[g, 0], p)

    def dots_plane(g):
        wait(dz.at[g, pl.ds(0, 15)], dot_recv.at[g, 0])
        here = x * 4 + y
        dp[g, here] = jnp.sum(dz[g], axis=0)
        for d in range(1, 16):
            there = dev(lax.rem(x + d // 4, 4), lax.rem(y + d % 4, 4), z, c)
            send(dp.at[g, here], dp.at[g, here], dot_send.at[g, 1], dot_recv.at[g, 1], there)

    def dots_core(g):
        wait(dp.at[g, pl.ds(0, 15)], dot_recv.at[g, 1])
        dc[g, c] = jnp.sum(dp[g], axis=0)
        send(dc.at[g, c], dc.at[g, c], dot_send.at[g, 2], dot_recv.at[g, 2], other)

    def dots_done(g, count):
        wait(dc.at[g, 1 - c], dot_recv.at[g, 2])
        total = jnp.sum(dc[g, 0] + dc[g, 1], axis=1, keepdims=True)
        return [jnp.broadcast_to(total[r : r + 1, :], (ROWS, BR)) for r in range(count)]

    def dots_sent(g):
        wait(dz.at[g, pl.ds(0, 15)], dot_send.at[g, 0])
        wait(dp.at[g, pl.ds(0, 15)], dot_send.at[g, 1])
        wait(dc.at[g, c], dot_send.at[g, 2])

    for g in range(3):
        dz[g, z] = jnp.zeros((16, BR), F32)
    dots_z(0, [(G, G), (G, HV), (G, HD), (G, GD)])
    step(1)
    step(2)
    step(3)
    dots_plane(0)
    step(4)
    step(5)
    dots_core(0)
    step(6)
    step(7)
    step(8)
    gg, gh, ghd, ggd = dots_done(0, 4)
    f1 = jnp.sqrt(CELLS / (gg + EPS))
    r1 = f1 * f1 * gh / CELLS
    c1 = f1 * f1 * (ghd - r1 * ggd) / CELLS
    finish()
    swapped(0, y_in1)

    product(v2, 4)
    swap(1, y_in2, 4)
    for b in range(2):
        for k in range(KS):
            w = (y_own[2 * c + b, k] + y_in2[b, k]) * mask[k]
            u = f1 * (piece[HD, k, b] - r1 * piece[GD, k, b] - c1 * piece[G, k, b])
            piece[U, k, b] = u
            piece[UD, k, b] = u / piece[D, k, b]
            piece[K, k, b] = f1 * (w - r1 * piece[Q, k, b] - c1 * piece[HV, k, b])
    dots_z(
        1,
        [(U, U), (G, K), (U, HV), (U, K), (GD, K), (G, UD), (U, HD), (UD, K), (U, UD)],
    )
    dots_plane(1)
    dots_core(1)
    uu, gk, uh, uk, gkd, gud, uhd, ukd, uud = dots_done(1, 9)
    f2 = jnp.sqrt(CELLS / (uu + EPS))
    a = r1
    b_ = f1 * f2 * (gk + uh) / (2.0 * CELLS)
    d_ = f2 * f2 * uk / CELLS
    h_ = (a - d_) / 2.0
    ritz = (a + d_) / 2.0 - jnp.sqrt(h_ * h_ + b_ * b_)
    big = jnp.maximum(jnp.abs(h_), jnp.abs(b_))
    safe = jnp.where(big > 0.0, big, 1.0)
    hs = jnp.where(big > 0.0, h_ / safe, 1.0)
    bs = b_ / safe
    rs = jnp.sqrt(hs * hs + bs * bs)
    larger = jnp.sqrt((rs + jnp.abs(hs)) / (2.0 * rs))
    smaller = jnp.abs(bs) / (2.0 * rs * larger)
    sign = jnp.where(bs < 0.0, -1.0, 1.0)
    co = jnp.where(hs >= 0.0, larger, smaller)
    si = sign * jnp.where(hs >= 0.0, smaller, larger)
    n1, n2 = -si * f1, co * f2
    e1 = f1 * (n1 * (ghd - ritz * ggd) + n2 * (gkd - ritz * gud)) / CELLS
    e2 = f2 * (n1 * (uhd - ritz * gud) + n2 * (ukd - ritz * uud)) / CELLS
    for b in range(2):
        for k in range(KS):
            g = piece[G, k, b]
            u = piece[U, k, b]
            t2 = (n1 * (piece[HV, k, b] - ritz * g) + n2 * (piece[K, k, b] - ritz * u)) / piece[D, k, b]
            piece[Q, k, b] = t2 - e1 * f1 * g - e2 * f2 * u
    v3[:, mine] = piece[Q]
    start, step, finish, sent3 = ring(2, v3, 2)
    start()
    dots_z(2, [(Q, Q)])
    step(1)
    step(2)
    step(3)
    dots_plane(2)
    step(4)
    step(5)
    dots_core(2)
    step(6)
    step(7)
    step(8)
    (qq,) = dots_done(2, 1)
    f3 = jnp.sqrt(CELLS / (qq + EPS))
    finish()
    swapped(1, y_in2)

    product(v3, 4)
    swap(2, y_in3, 4)
    for b in range(2):
        for k in range(KS):
            out_src[k, 0, b] = piece[Q, k, b] * f3
            out_src[k, 1, b] = (y_own[2 * c + b, k] + y_in3[b, k]) * mask[k] * f3

    yo, co_ = lax.div(z, 4), lax.rem(lax.div(z, 2), 2)
    part_out = lax.rem(z, 2) * 2 + c
    stays = jnp.logical_and(jnp.logical_and(yo == y, src_line == y), co_ == c)
    for k in range(KS):
        here = jnp.logical_and(stays, kown == k)

        @pl.when(here)
        def _():
            out_got[part_out] = out_src[k]

        @pl.when(jnp.logical_not(here))
        def _():
            send(out_src.at[k], out_got.at[part_out], out_send, out_recv, dev(x, yo, y + 4 * k, co_))

    @pl.when(stays)
    def _():
        wait(out_got.at[pl.ds(0, 3)], out_recv)
        wait(out_got.at[pl.ds(0, 3)], out_send)

    @pl.when(jnp.logical_not(stays))
    def _():
        wait(out_got, out_recv)
        wait(out_got, out_send)

    for s in range(4):
        for b in range(2):
            col = (s * 2 + b) * BR
            basis_ref[:, col : col + BR] = out_got[s, 0, b]
            image_ref[:, col : col + BR] = out_got[s, 1, b]

    wait(rbuf.at[pl.ds(0, 15)], w_send)
    sent1()
    sent2()
    sent3()
    swapped(2, y_in3)
    for g in range(3):
        dots_sent(g)
    wait(shift_all.at[pl.ds(0, 3)], st_send.at[0])

    @pl.when(is_src)
    def _():
        wait(src_gd.at[pl.ds(0, 30)], st_send.at[1])
        wait(src_gd.at[pl.ds(0, 30)], st_send.at[2])

    @pl.when(jnp.logical_not(is_src))
    def _():
        wait(left_tile, st_send.at[2])


def per_device(start_vector, precond_diag, left_env, right_env, right_shift, sector_length):
    vmem = pl.BlockSpec(memory_space=pltpu.VMEM)
    smem = pl.BlockSpec(memory_space=pltpu.SMEM)
    DMA = pltpu.SemaphoreType.DMA
    tile = (ROWS, BR)
    return pl.pallas_call(
        kernel,
        out_shape=[jax.ShapeDtypeStruct((ROWS, 1024), F32)] * 2,
        in_specs=[vmem, vmem, vmem, vmem, smem, smem],
        out_specs=[vmem, vmem],
        scratch_shapes=[
            pltpu.VMEM((16, TPD, BR, BR), F32),
            pltpu.VMEM((16, TPD, BR, BR), BF16),
            pltpu.VMEM((16, TPD, BR, BR), BF16),
            pltpu.VMEM((8, NBLK) + tile, F32),
            pltpu.VMEM((4, NBLK) + tile, F32),
            pltpu.VMEM((4, NBLK) + tile, F32),
            pltpu.VMEM((4, 8) + tile, F32),
            pltpu.VMEM((2, 8) + tile, F32),
            pltpu.VMEM((2, 4) + tile, F32),
            pltpu.VMEM((2, 4) + tile, F32),
            pltpu.VMEM((9, KS, 2) + tile, F32),
            pltpu.VMEM((NBLK, 2) + tile, F32),
            pltpu.VMEM((KS, 2, 2) + tile, F32),
            pltpu.VMEM(tile, F32),
            pltpu.VMEM((4,) + tile, F32),
            pltpu.VMEM((KS, 4) + tile, F32),
            pltpu.VMEM(tile, jnp.int32),
            pltpu.VMEM((4,) + tile, jnp.int32),
            pltpu.SMEM((4,) + tile, jnp.int32),
            pltpu.VMEM((4 * TPD, KS, ROWS) + tile, F32),
            pltpu.VMEM((KS,) + tile, F32),
            pltpu.VMEM((3, 16, 16, BR), F32),
            pltpu.VMEM((3, 16, 16, BR), F32),
            pltpu.VMEM((3, 2, 16, BR), F32),
            pltpu.VMEM((KS, 2, 2) + tile, F32),
            pltpu.VMEM((4, 2, 2) + tile, F32),
            DMA,
            DMA((20,)),
            DMA((3,)),
            DMA((3, 2, 8)),
            DMA((3, 2, 7)),
            DMA((3,)),
            DMA((3,)),
            DMA((3,)),
            DMA((3, 3)),
            DMA((3, 3)),
            DMA((3,)),
            DMA((4,)),
            DMA,
            DMA,
            DMA,
        ],
        compiler_params=pltpu.CompilerParams(
            collective_id=0, has_side_effects=True, vmem_limit_bytes=48 * 1024 * 1024
        ),
        cost_estimate=pl.CostEstimate(flops=600_000_000, bytes_accessed=2_000_000, transcendentals=0),
    )(start_vector, precond_diag, left_env, right_env, right_shift, sector_length)


def solution(mesh):
    placed = (
        P("sec", None),
        P("sec", None),
        P("mpo", "sec", None),
        P("mpo", "sec", None),
        P("mpo"),
        P("sec"),
    )
    return jax.shard_map(
        per_device,
        mesh=mesh,
        in_specs=placed,
        out_specs=(P("sec", "mpo"), P("sec", "mpo")),
        check_vma=False,
    )
```

```python
import jax
import jax.numpy as jnp
from jax import lax
from jax.experimental import pallas as pl
from jax.experimental.pallas import tpu as pltpu
from jax.sharding import PartitionSpec as P

MESH = pl.DeviceIdType.MESH
F32 = jnp.float32
BF16 = jnp.bfloat16

NZ = 16
ROWS, BR, NBLK = 8, 128, 64
TPD = 3
TERMS = 24
KS = 4
CELLS = float(512 * 8192)
EPS = 1e-6
TILE = (ROWS, BR)

G, B, E, H_, Q, S, A_, AA, AQ, P_, T, W, AP = range(13)
EARLY = [
    (G, G), (G, B), (G, A_), (B, B), (A_, B), (A_, A_), (G, H_), (G, Q), (B, Q), (A_, H_), (A_, Q),
    (E, B), (E, A_), (AA, A_), (E, Q), (AA, Q), (E, E), (E, AA), (AA, AA), (E, AQ), (AA, AQ), (AQ, AQ),
]
LATE = [(G, P_), (B, P_), (A_, P_), (E, P_), (AA, P_), (E, AP), (AA, AP), (AQ, AP), (AP, AP)]


def kernel(
    start_hbm,
    diag_hbm,
    left_ref,
    right_hbm,
    shift_ref,
    length_ref,
    basis_ref,
    image_ref,
    start_ref,
    diag_ref,
    zbuf,
    rbuf,
    r_hi,
    r_lo,
    gd,
    v1,
    v2,
    v2b,
    v3,
    y_sum,
    piece,
    inv,
    left_all,
    shift_all,
    shift_sm,
    left_wide,
    mask,
    dz0,
    dp0,
    dc0,
    dz1,
    dp1,
    dc1,
    out_src,
    out_got,
    in_sem,
    z_send,
    z_plus,
    z_minus,
    r_send,
    r_recv,
    x_send,
    x_recv,
    x_core,
    l_send,
    l_recv,
    s_send,
    s_recv,
    sm_sem,
    ag_send,
    ag_recv,
    ag_core,
    dot_send,
    dot_recv,
    out_send,
    out_recv,
):
    sec = lax.axis_index("sec")
    mpo = lax.axis_index("mpo")
    z, x = lax.div(sec, 4), lax.rem(sec, 4)
    y, c = lax.div(mpo, 2), lax.rem(mpo, 2)
    here = 4 * y + x

    def dev(xx, yy, zz, cc):
        return (zz * 4 + xx, yy * 2 + cc)

    def send(src, dst, send_sem, recv_sem, where):
        pltpu.make_async_remote_copy(
            src_ref=src,
            dst_ref=dst,
            send_sem=send_sem,
            recv_sem=recv_sem,
            device_id=where,
            device_id_type=MESH,
        ).start()

    def wait(ref, sem):
        pltpu.make_async_copy(ref, ref, sem).wait()

    up = dev(x, y, lax.rem(z + 1, NZ), c)
    down = dev(x, y, lax.rem(z + NZ - 1, NZ), c)
    other = dev(x, y, z, 1 - c)
    zdevs = [dev(x, y, lax.rem(z + d, NZ), c) for d in range(1, NZ)]
    offsets = sorted(range(1, 16), key=lambda o: -(min(o // 4, 4 - o // 4) + min(o % 4, 4 - o % 4)))

    def peer(o):
        return dev(lax.rem(x + o // 4, 4), lax.rem(y + o % 4, 4), z, c)

    def sender(o):
        return 4 * lax.rem(y + 4 - o % 4, 4) + lax.rem(x + 4 - o // 4, 4)

    loads = [
        pltpu.make_async_copy(right_hbm, zbuf.at[z], in_sem.at[0]),
        pltpu.make_async_copy(start_hbm, start_ref, in_sem.at[1]),
        pltpu.make_async_copy(diag_hbm, diag_ref, in_sem.at[2]),
    ]
    for load in loads:
        load.start()
    barrier = pltpu.get_barrier_semaphore()
    partners = [up, down, other] + [peer(o) for o in offsets]
    partners += [dev(x, lax.rem(y + d, 4), z, 1 - c) for d in range(1, 4)]
    for p in partners:
        pl.semaphore_signal(barrier, inc=1, device_id=p, device_id_type=MESH)

    sub = lax.broadcasted_iota(jnp.int32, TILE, 0)
    left_all[c, here] = jnp.zeros(TILE, F32)
    for t in range(TPD):
        left_all[c, here, :, t * ROWS : (t + 1) * ROWS] = left_ref[t]
    left_all[c, here, :, TPD * ROWS : TPD * ROWS + 1] = jnp.full((ROWS, 1), length_ref[0].astype(F32), F32)
    shift_all[c, y] = jnp.where(sub == 0, shift_ref[0], jnp.where(sub == 1, shift_ref[1], shift_ref[2]))
    live0 = jnp.where(sub < length_ref[0], 1.0, 0.0).astype(F32)
    loads[1].wait()
    loads[2].wait()
    for m in range(NBLK):
        gd[x, m % 16, m // 16, 0] = start_ref[:, m * BR : (m + 1) * BR] * live0
        gd[x, m % 16, m // 16, 1] = diag_ref[:, m * BR : (m + 1) * BR]
    loads[0].wait()
    pl.semaphore_wait(barrier, len(partners))

    def deliver(zz, t):
        nn = lax.rem(lax.div(zz, 4), 2)
        yd, cd = lax.rem(zz, 4), lax.div(zz, 8)
        dst = rbuf.at[nn, y, c, t]
        stays = jnp.logical_and(yd == y, cd == c)

        @pl.when(stays)
        def _():
            pltpu.make_async_copy(zbuf.at[zz, t], dst, r_recv).start()

        @pl.when(jnp.logical_not(stays))
        def _():
            send(zbuf.at[zz, t], dst, r_send, r_recv, dev(x, yd, z, cd))

    for t in range(TPD):
        send(zbuf.at[z, t], zbuf.at[z, t], z_send, z_plus.at[t, 0], up)
        send(zbuf.at[z, t], zbuf.at[z, t], z_send, z_minus.at[t, 0], down)

    def half(k, cc):
        return gd.at[k, :, pl.ds(2 * cc, 2)]

    for d in (2, 1, 3):
        send(half(x, c), half(x, c), x_send, x_recv.at[d - 1], dev(lax.rem(x + d, 4), y, z, c))
    for d in range(1, 4):
        send(shift_all.at[c, y], shift_all.at[c, y], s_send.at[0], s_recv.at[0], dev(x, lax.rem(y + d, 4), z, c))
    for o in offsets:
        send(left_all.at[c, here], left_all.at[c, here], l_send.at[0], l_recv.at[0], peer(o))
    for t in range(TPD):
        deliver(z, t)

    def ring_step(i, t):
        zp, zm = lax.rem(z + NZ - i, NZ), lax.rem(z + i, NZ)
        wait(zbuf.at[zp, t], z_plus.at[t, i - 1])
        if i < 8:
            send(zbuf.at[zp, t], zbuf.at[zp, t], z_send, z_plus.at[t, i], up)
        deliver(zp, t)
        if i < 8:
            wait(zbuf.at[zm, t], z_minus.at[t, i - 1])
            if i < 7:
                send(zbuf.at[zm, t], zbuf.at[zm, t], z_send, z_minus.at[t, i], down)
            deliver(zm, t)

    def pass_rows(d):
        k = lax.rem(x + 4 - d, 4)
        wait(half(k, c), x_recv.at[d - 1])
        send(half(k, c), half(k, c), x_send, x_core, other)

    def pass_small():
        wait(shift_all.at[c, pl.ds(0, 3)], s_recv.at[0])
        send(shift_all.at[c], shift_all.at[c], s_send.at[1], s_recv.at[1], other)
        wait(left_all.at[c, pl.ds(0, 15)], l_recv.at[0])
        send(left_all.at[c], left_all.at[c], l_send.at[1], l_recv.at[1], other)

    to_sm = pltpu.make_async_copy(shift_all, shift_sm, sm_sem)

    def take_small():
        wait(shift_all.at[1 - c], s_recv.at[1])
        to_sm.start()
        wait(left_all.at[1 - c], l_recv.at[1])
        for k in range(KS):
            length = jnp.broadcast_to(left_all[c, 4 * y + k][:, TPD * ROWS : TPD * ROWS + 1], TILE)
            mask[k] = jnp.where(sub.astype(F32) < length, 1.0, 0.0).astype(F32)

    def widen(first, count):
        def body(i, carry):
            cc, r = lax.div(i, 16), lax.rem(i, 16)
            yy, k = lax.div(r, 4), lax.rem(r, 4)
            tile = left_all[cc, r]
            for t in range(TPD):
                for j in range(ROWS):
                    lane = t * ROWS + j
                    left_wide[(yy * 2 + cc) * TPD + t, k, j] = jnp.broadcast_to(tile[:, lane : lane + 1], TILE)
            return carry

        lax.fori_loop(first, first + count, body, 0)

    def take_rows():
        wait(gd.at[pl.ds(0, 3), :, pl.ds(0, 2)], x_core)

    def vectors(first, count):
        def body(r, carry):
            for k in range(KS):
                for j in range(4):
                    g = gd[k, r, j, 0]
                    a = 1.0 / gd[k, r, j, 1]
                    b = g * a
                    v1[k, r, j] = g
                    v1[KS + k, r, j] = b
                    v1[2 * KS + k, r, j] = b * a
            return carry

        lax.fori_loop(first, first + count, body, 0)

    idle = [lambda: None]
    tasks = idle * 3 + [pass_small] + idle + [take_small]
    tasks += [lambda i=i: widen(4 * i, 4) for i in range(8)]
    tasks += [lambda: pass_rows(1), lambda: pass_rows(3), lambda: pass_rows(2), take_rows]
    tasks += [lambda i=i: vectors(3 * i, 3) for i in range(5)] + [lambda: vectors(15, 1)]
    tasks = tasks[::-1]
    for i in range(1, 9):
        for t in range(TPD):
            ring_step(i, t)
            if tasks:
                tasks.pop()()
    while tasks:
        tasks.pop()()

    for nn in range(2):
        for k in range(KS):
            j = 2 * c + nn
            inv[k, nn] = 1.0 / gd[k, here, j, 1]
            piece[G, k, nn] = v1[k, here, j]
            piece[B, k, nn] = v1[KS + k, here, j]
            piece[E, k, nn] = v1[2 * KS + k, here, j]
    to_sm.wait()
    wait(rbuf, r_recv)

    def product(v, nk, cut):
        rows = nk * ROWS
        y_sum[:, pl.ds(0, nk)] = jnp.zeros((2, nk) + TILE, F32)

        def body(i, carry):
            yy, rest = lax.div(i, 2 * TPD), lax.rem(i, 2 * TPD)
            cc, t = lax.div(rest, TPD), lax.rem(rest, TPD)
            shift = shift_sm[cc, yy, t, 0]
            for nn in range(2):
                m = 16 * (2 * c + nn) + here + shift
                m = jnp.where(m >= NBLK, m - NBLK, m)
                r, j4 = lax.rem(m, 16), lax.div(m, 16)
                tiles = []
                for k in range(nk):
                    src = v[k, r, j4]
                    total = None
                    for j in range(ROWS):
                        term = left_wide[i, k % KS, j] * src[j : j + 1, :]
                        total = term if total is None else total + term
                    tiles.append(total)
                p = jnp.concatenate(tiles, axis=0)
                hi = p.astype(BF16)
                lo = (p - hi.astype(F32)).astype(BF16)
                if cut:
                    full = rbuf[nn, yy, cc, t]
                    rh = full.astype(BF16)
                    rl = (full - rh.astype(F32)).astype(BF16)
                    r_hi[nn, yy, cc, t] = rh
                    r_lo[nn, yy, cc, t] = rl
                else:
                    rh = r_hi[nn, yy, cc, t]
                    rl = r_lo[nn, yy, cc, t]
                both = jnp.dot(jnp.concatenate([hi, lo], axis=0), rh, preferred_element_type=F32)
                more = jnp.dot(hi, rl, preferred_element_type=F32)
                y_sum[nn, pl.ds(0, nk)] += (both[:rows] + both[rows:] + more).reshape((nk,) + TILE)
            return carry

        lax.fori_loop(0, TERMS, body, 0)

    def gather(phase, v):
        def at(r, cc):
            return v.at[:, r, pl.ds(2 * cc, 2)]

        def start():
            for o in offsets:
                send(at(here, c), at(here, c), ag_send.at[phase, 0], ag_recv.at[phase, o], peer(o))
            send(at(here, c), at(here, c), ag_send.at[phase, 1], ag_core.at[phase], other)

        def pass_on():
            for o in offsets[::-1]:
                r = sender(o)
                wait(at(r, c), ag_recv.at[phase, o])
                send(at(r, c), at(r, c), ag_send.at[phase, 1], ag_core.at[phase], other)

        def finish():
            wait(v.at[:, :, pl.ds(0, 2)], ag_core.at[phase])

        def sent():
            wait(v.at[:, pl.ds(0, 15), pl.ds(0, 2)], ag_send.at[phase, 0])
            wait(v.at[:, :, pl.ds(0, 2)], ag_send.at[phase, 1])

        return start, pass_on, finish, sent

    def dots(g, dz, dp, dc):
        def start(pairs):
            dz[z] = jnp.zeros(dz.shape[1:], F32)
            for r, (a, b) in enumerate(pairs):
                prod = (piece[a] * piece[b]).reshape((2 * KS,) + TILE)
                dz[z, r : r + 1, :] = jnp.sum(jnp.sum(prod, axis=0), axis=0, keepdims=True)
            for p in zdevs:
                send(dz.at[z], dz.at[z], dot_send.at[g, 0], dot_recv.at[g, 0], p)

        def plane():
            wait(dz.at[pl.ds(0, 15)], dot_recv.at[g, 0])
            dp[here] = jnp.sum(dz[...], axis=0)
            for o in offsets:
                send(dp.at[here], dp.at[here], dot_send.at[g, 1], dot_recv.at[g, 1], peer(o))

        def core():
            wait(dp.at[pl.ds(0, 15)], dot_recv.at[g, 1])
            dc[c] = jnp.sum(dp[...], axis=0)
            send(dc.at[c], dc.at[c], dot_send.at[g, 2], dot_recv.at[g, 2], other)

        def done(pairs):
            wait(dc.at[1 - c], dot_recv.at[g, 2])
            total = jnp.sum(dc[0] + dc[1], axis=1, keepdims=True)
            return {p: jnp.broadcast_to(total[r : r + 1, :], TILE) for r, p in enumerate(pairs)}

        def sent():
            wait(dz.at[pl.ds(0, 15)], dot_send.at[g, 0])
            wait(dp.at[pl.ds(0, 15)], dot_send.at[g, 1])
            wait(dc.at[c], dot_send.at[g, 2])

        return start, plane, core, done, sent

    product(v1, 3 * KS, True)
    mine = pl.ds(2 * c, 2)
    for nn in range(2):
        for k in range(KS):
            h = y_sum[nn, k] * mask[k]
            q = y_sum[nn, KS + k] * mask[k]
            a = h * inv[k, nn]
            piece[H_, k, nn] = h
            piece[Q, k, nn] = q
            piece[S, k, nn] = y_sum[nn, 2 * KS + k] * mask[k]
            piece[A_, k, nn] = a
            piece[AA, k, nn] = a * inv[k, nn]
            piece[AQ, k, nn] = q * inv[k, nn]
    v2[:, here, mine] = piece[A_]
    v2b[pl.ds(0, KS), here, mine] = piece[AA]
    v2b[pl.ds(KS, KS), here, mine] = piece[AQ]
    ag2, ag2b, ag3 = gather(0, v2), gather(1, v2b), gather(2, v3)
    early, late = dots(0, dz0, dp0, dc0), dots(1, dz1, dp1, dc1)
    ag2[0]()
    early[0](EARLY)
    ag2b[0]()
    ag2[1]()
    ag2[2]()

    product(v2, KS, False)
    for nn in range(2):
        for k in range(KS):
            p = y_sum[nn, k] * mask[k]
            piece[P_, k, nn] = p
            piece[AP, k, nn] = p * inv[k, nn]
    v3[:, here, mine] = piece[AP]
    ag3[0]()
    late[0](LATE)
    early[1]()
    ag2b[1]()
    ag2b[2]()
    product(v2b, 2 * KS, False)
    for nn in range(2):
        for k in range(KS):
            piece[T, k, nn] = y_sum[nn, k] * mask[k]
            piece[W, k, nn] = y_sum[nn, KS + k] * mask[k]
    early[2]()
    ag3[1]()
    late[1]()
    ag3[2]()

    product(v3, KS, False)
    late[2]()
    dot = early[3](EARLY)
    dot.update(late[3](LATE))
    dot.update({(b, a): value for (a, b), value in dot.items()})

    f1 = jnp.sqrt(CELLS / (dot[G, G] + EPS))
    r1 = f1 * f1 * dot[G, H_] / CELLS
    c1 = f1 * f1 * (dot[G, A_] - r1 * dot[G, B]) / CELLS
    w = (-f1 * c1, -f1 * r1, f1)
    x_x = [[dot[i, j] for j in (G, B, A_)] for i in (G, B, A_)]
    x_y = [
        [dot[G, H_], dot[G, Q], dot[G, P_]],
        [dot[G, A_], dot[B, Q], dot[B, P_]],
        [dot[A_, H_], dot[A_, Q], dot[A_, P_]],
    ]
    ax_y = [
        [dot[G, A_], dot[B, Q], dot[B, P_]],
        [dot[A_, B], dot[E, Q], dot[E, P_]],
        [dot[A_, A_], dot[AA, Q], dot[AA, P_]],
    ]
    ax_x = [
        [dot[G, B], dot[B, B], dot[A_, B]],
        [dot[B, B], dot[E, B], dot[E, A_]],
        [dot[A_, B], dot[E, A_], dot[AA, A_]],
    ]

    def along(row):
        return w[0] * row[0] + w[1] * row[1] + w[2] * row[2]

    def form(m):
        return along([along(row) for row in m])

    def column(m, j):
        return [row[j] for row in m]

    uu, uk, uak, uau = form(x_x), form(x_y), form(ax_y), form(ax_x)
    gu, gk, uh = along(x_x[0]), along(x_y[0]), along(column(x_y, 0))
    gak, gau, uah = along(x_y[1]), along(x_x[1]), along(column(x_x, 2))
    f2 = jnp.sqrt(CELLS / (jnp.maximum(uu, 0.0) + EPS))
    b_ = f1 * f2 * (gk + uh) / (2.0 * CELLS)
    d_ = f2 * f2 * uk / CELLS
    h_ = (r1 - d_) / 2.0
    ritz = (r1 + d_) / 2.0 - jnp.sqrt(h_ * h_ + b_ * b_)
    big = jnp.maximum(jnp.abs(h_), jnp.abs(b_))
    safe = jnp.where(big > 0.0, big, 1.0)
    hs = jnp.where(big > 0.0, h_ / safe, 1.0)
    bs = b_ / safe
    rs = jnp.sqrt(hs * hs + bs * bs)
    larger = jnp.sqrt((rs + jnp.abs(hs)) / (2.0 * rs))
    smaller = jnp.abs(bs) / (2.0 * rs * larger)
    co = jnp.where(hs >= 0.0, larger, smaller)
    si = jnp.where(bs < 0.0, -1.0, 1.0) * jnp.where(hs >= 0.0, smaller, larger)
    n1, n2 = -si * f1, co * f2
    e1 = f1 * (n1 * (dot[G, A_] - ritz * dot[G, B]) + n2 * (gak - ritz * gau)) / CELLS
    e2 = f2 * (n1 * (uah - ritz * gau) + n2 * (uak - ritz * uau)) / CELLS
    t2 = {
        A_: n1 + n2 * w[0],
        B: -ritz * (n1 + n2 * w[0]),
        E: -ritz * n2 * w[1],
        AA: -ritz * n2 * w[2],
        AQ: n2 * w[1],
        AP: n2 * w[2],
    }
    dot[A_, AQ], dot[A_, AP], dot[B, AQ], dot[B, AP] = dot[AA, Q], dot[AA, P_], dot[E, Q], dot[E, P_]
    dot[B, AA] = dot[E, A_]
    dot.update({(b, a): value for (a, b), value in dot.items()})
    tt = jnp.zeros(TILE, F32)
    for i in t2:
        row = jnp.zeros(TILE, F32)
        for j in t2:
            row = row + t2[j] * dot[i, j]
        tt = tt + t2[i] * row
    square = tt - 2.0 * CELLS * (e1 * e1 + e2 * e2)
    square = square + e1 * e1 * f1 * f1 * dot[G, G] + e2 * e2 * f2 * f2 * uu + 2.0 * e1 * e2 * f1 * f2 * gu
    f3 = jnp.sqrt(CELLS / (jnp.maximum(square, 0.0) + EPS))
    coef = dict(t2)
    coef[G] = -e1 * f1 - e2 * f2 * w[0]
    coef[B] = coef[B] - e2 * f2 * w[1]
    coef[A_] = coef[A_] - e2 * f2 * w[2]
    coef = {i: f3 * value for i, value in coef.items()}
    image_of = {A_: P_, B: Q, E: S, AA: T, AQ: W, G: H_}
    for nn in range(2):
        for k in range(KS):
            basis = coef[AP] * piece[AP, k, nn]
            image = coef[AP] * (y_sum[nn, k] * mask[k])
            for i in image_of:
                basis = basis + coef[i] * piece[i, k, nn]
                image = image + coef[i] * piece[image_of[i], k, nn]
            out_src[k, nn, 0] = basis
            out_src[k, nn, 1] = image

    spot = 4 * lax.rem(y, 2) + x
    cd = lax.div(y, 2)
    keeps = cd == c
    for k in range(KS):
        for nn in range(2):
            stays = jnp.logical_and(jnp.logical_and(x == k, y == 2 * c + nn), keeps)

            @pl.when(stays)
            def _():
                out_got[spot] = out_src[k, nn]

            @pl.when(jnp.logical_not(stays))
            def _():
                send(out_src.at[k, nn], out_got.at[spot], out_send, out_recv, dev(k, 2 * c + nn, z, cd))

    @pl.when(keeps)
    def _():
        wait(out_got.at[pl.ds(0, 7)], out_recv)
        wait(out_got.at[pl.ds(0, 7)], out_send)

    @pl.when(jnp.logical_not(keeps))
    def _():
        wait(out_got, out_recv)
        wait(out_got, out_send)

    for s in range(8):
        basis_ref[:, s * BR : (s + 1) * BR] = out_got[s, 0]
        image_ref[:, s * BR : (s + 1) * BR] = out_got[s, 1]

    wait(zbuf.at[pl.ds(0, 15)], z_send)
    wait(zbuf.at[pl.ds(0, 14)], r_send)
    wait(gd.at[pl.ds(0, 3)], x_send)
    wait(left_all.at[c, pl.ds(0, 15)], l_send.at[0])
    wait(left_all.at[c], l_send.at[1])
    wait(shift_all.at[c, pl.ds(0, 3)], s_send.at[0])
    wait(shift_all.at[c], s_send.at[1])
    for ag in (ag2, ag2b, ag3):
        ag[3]()
    early[4]()
    late[4]()


def per_device(start_vector, precond_diag, left_env, right_env, right_shift, sector_length):
    vmem = pl.BlockSpec(memory_space=pltpu.VMEM)
    smem = pl.BlockSpec(memory_space=pltpu.SMEM)
    hbm = pl.BlockSpec(memory_space=pl.ANY)
    DMA = pltpu.SemaphoreType.DMA
    return pl.pallas_call(
        kernel,
        out_shape=[jax.ShapeDtypeStruct((ROWS, 1024), F32)] * 2,
        in_specs=[hbm, hbm, vmem, hbm, smem, smem],
        out_specs=[vmem, vmem],
        scratch_shapes=[
            pltpu.VMEM((ROWS, NBLK * BR), F32),
            pltpu.VMEM((ROWS, NBLK * BR), F32),
            pltpu.VMEM((NZ, TPD, BR, BR), F32),
            pltpu.VMEM((2, 4, 2, TPD, BR, BR), F32),
            pltpu.VMEM((2, 4, 2, TPD, BR, BR), BF16),
            pltpu.VMEM((2, 4, 2, TPD, BR, BR), BF16),
            pltpu.VMEM((KS, 16, 4, 2) + TILE, F32),
            pltpu.VMEM((3 * KS, 16, 4) + TILE, F32),
            pltpu.VMEM((KS, 16, 4) + TILE, F32),
            pltpu.VMEM((2 * KS, 16, 4) + TILE, F32),
            pltpu.VMEM((KS, 16, 4) + TILE, F32),
            pltpu.VMEM((2, 3 * KS) + TILE, F32),
            pltpu.VMEM((13, KS, 2) + TILE, F32),
            pltpu.VMEM((KS, 2) + TILE, F32),
            pltpu.VMEM((2, 16) + TILE, F32),
            pltpu.VMEM((2, 4) + TILE, jnp.int32),
            pltpu.SMEM((2, 4) + TILE, jnp.int32),
            pltpu.VMEM((TERMS, KS, ROWS) + TILE, F32),
            pltpu.VMEM((KS,) + TILE, F32),
            pltpu.VMEM((16, 24, BR), F32),
            pltpu.VMEM((16, 24, BR), F32),
            pltpu.VMEM((2, 24, BR), F32),
            pltpu.VMEM((16, 16, BR), F32),
            pltpu.VMEM((16, 16, BR), F32),
            pltpu.VMEM((2, 16, BR), F32),
            pltpu.VMEM((KS, 2, 2) + TILE, F32),
            pltpu.VMEM((8, 2) + TILE, F32),
            DMA((3,)),
            DMA,
            DMA((TPD, 8)),
            DMA((TPD, 7)),
            DMA,
            DMA,
            DMA,
            DMA((3,)),
            DMA,
            DMA((2,)),
            DMA((2,)),
            DMA((2,)),
            DMA((2,)),
            DMA,
            DMA((3, 2)),
            DMA((3, 16)),
            DMA((3,)),
            DMA((2, 3)),
            DMA((2, 3)),
            DMA,
            DMA,
        ],
        compiler_params=pltpu.CompilerParams(
            collective_id=0, has_side_effects=True, vmem_limit_bytes=48 * 1024 * 1024
        ),
        cost_estimate=pl.CostEstimate(flops=600_000_000, bytes_accessed=2_000_000, transcendentals=0),
    )(start_vector, precond_diag, left_env, right_env, right_shift, sector_length)


def solution(mesh):
    placed = (
        P("sec", None),
        P("sec", None),
        P("mpo", "sec", None),
        P("mpo", "sec", None),
        P("mpo"),
        P("sec"),
    )
    return jax.shard_map(
        per_device,
        mesh=mesh,
        in_specs=placed,
        out_specs=(P("sec", "mpo"), P("sec", "mpo")),
        check_vma=False,
    )
```

```python
import jax
import jax.numpy as jnp
from jax import lax
from jax.experimental import pallas as pl
from jax.experimental.pallas import tpu as pltpu
from jax.sharding import PartitionSpec as P

MESH = pl.DeviceIdType.MESH
F32 = jnp.float32
BF16 = jnp.bfloat16

NZ = 16
ROWS, BR, NBLK = 8, 128, 64
TPD = 3
TERMS = 24
KS = 4
CELLS = float(512 * 8192)
EPS = 1e-6
TILE = (ROWS, BR)

G, B, E, H_, Q, S, A_, AA, P_, PP, T, AP = range(12)
EARLY = [
    (G, G), (G, H_), (G, B), (G, A_), (B, B), (A_, B), (A_, A_), (A_, H_),
    (E, B), (E, A_), (AA, A_), (E, E), (E, AA), (AA, AA),
]
LATE = [(G, PP), (B, PP), (A_, PP), (E, PP), (AA, PP), (E, AP), (AA, AP), (AP, AP)]


def kernel(
    start_hbm,
    diag_hbm,
    left_hbm,
    right_hbm,
    shift_hbm,
    length_hbm,
    basis_ref,
    image_ref,
    start_ref,
    diag_ref,
    left_ref,
    shift_ref,
    length_ref,
    zbuf,
    rbuf,
    r_hi,
    r_lo,
    gd,
    v1,
    v2,
    v2b,
    v3,
    y_sum,
    piece,
    inv,
    left_all,
    shift_all,
    shift_sm,
    left_wide,
    mask,
    d_rows,
    dz,
    dp,
    dc,
    out_src,
    out_got,
    in_sem,
    z_send,
    z_plus,
    z_minus,
    r_send,
    r_recv,
    x_send,
    x_recv,
    x_core,
    l_send,
    l_recv,
    s_send,
    s_recv,
    sm_sem,
    ag_send,
    ag_recv,
    ag_core,
    dot_send,
    dot_recv,
    out_send,
    out_recv,
):
    sec = lax.axis_index("sec")
    mpo = lax.axis_index("mpo")
    z, x = lax.div(sec, 4), lax.rem(sec, 4)
    y, c = lax.div(mpo, 2), lax.rem(mpo, 2)
    here = 4 * y + x

    def dev(xx, yy, zz, cc):
        return (zz * 4 + xx, yy * 2 + cc)

    def send(src, dst, send_sem, recv_sem, where):
        pltpu.make_async_remote_copy(
            src_ref=src,
            dst_ref=dst,
            send_sem=send_sem,
            recv_sem=recv_sem,
            device_id=where,
            device_id_type=MESH,
        ).start()

    def wait(ref, sem):
        pltpu.make_async_copy(ref, ref, sem).wait()

    up = dev(x, y, lax.rem(z + 1, NZ), c)
    down = dev(x, y, lax.rem(z + NZ - 1, NZ), c)
    other = dev(x, y, z, 1 - c)
    zdevs = [dev(x, y, lax.rem(z + d, NZ), c) for d in range(1, NZ)]
    offsets = sorted(range(1, 16), key=lambda o: -(min(o // 4, 4 - o // 4) + min(o % 4, 4 - o % 4)))

    def peer(o):
        return dev(lax.rem(x + o // 4, 4), lax.rem(y + o % 4, 4), z, c)

    def sender(o):
        return 4 * lax.rem(y + 4 - o % 4, 4) + lax.rem(x + 4 - o // 4, 4)

    loads = [
        pltpu.make_async_copy(right_hbm, zbuf.at[z], in_sem.at[0]),
        pltpu.make_async_copy(start_hbm, start_ref, in_sem.at[1]),
        pltpu.make_async_copy(diag_hbm, diag_ref, in_sem.at[2]),
        pltpu.make_async_copy(left_hbm, left_ref, in_sem.at[3]),
        pltpu.make_async_copy(shift_hbm, shift_ref, in_sem.at[4]),
        pltpu.make_async_copy(length_hbm, length_ref, in_sem.at[5]),
    ]
    for load in loads:
        load.start()
    barrier = pltpu.get_barrier_semaphore()
    partners = [up, down, other] + [peer(o) for o in offsets]
    partners += [dev(x, lax.rem(y + d, 4), z, 1 - c) for d in range(1, 4)]
    for p in partners:
        pl.semaphore_signal(barrier, inc=1, device_id=p, device_id_type=MESH)

    sub = lax.broadcasted_iota(jnp.int32, TILE, 0)
    for load in loads[3:]:
        load.wait()
    left_all[c, here] = jnp.zeros(TILE, F32)
    for t in range(TPD):
        left_all[c, here, :, t * ROWS : (t + 1) * ROWS] = left_ref[t]
    left_all[c, here, :, TPD * ROWS : TPD * ROWS + 1] = jnp.full((ROWS, 1), length_ref[0].astype(F32), F32)
    shift_all[c, y] = jnp.where(sub == 0, shift_ref[0], jnp.where(sub == 1, shift_ref[1], shift_ref[2]))
    live0 = jnp.where(sub < length_ref[0], 1.0, 0.0).astype(F32)
    loads[1].wait()
    loads[2].wait()
    for m in range(NBLK):
        gd[x, m % 16, m // 16, 0] = start_ref[:, m * BR : (m + 1) * BR] * live0
        gd[x, m % 16, m // 16, 1] = diag_ref[:, m * BR : (m + 1) * BR]
    loads[0].wait()
    pl.semaphore_wait(barrier, len(partners))

    def deliver(zz, t):
        nn = lax.rem(lax.div(zz, 4), 2)
        yd, cd = lax.rem(zz, 4), lax.div(zz, 8)
        dst = rbuf.at[nn, y, c, t]
        sem = r_recv.at[nn]
        stays = jnp.logical_and(yd == y, cd == c)

        @pl.when(stays)
        def _():
            pltpu.make_async_copy(zbuf.at[zz, t], dst, sem).start()

        @pl.when(jnp.logical_not(stays))
        def _():
            send(zbuf.at[zz, t], dst, r_send, sem, dev(x, yd, z, cd))

    for t in range(TPD):
        send(zbuf.at[z, t], zbuf.at[z, t], z_send, z_plus.at[t, 0], up)
        send(zbuf.at[z, t], zbuf.at[z, t], z_send, z_minus.at[t, 0], down)

    def half(k, cc):
        return gd.at[k, :, pl.ds(2 * cc, 2)]

    def send_rows(i):
        rows = gd.at[x, pl.ds(2 * i, 2), pl.ds(2 * c, 2)]
        for d in (2, 1, 3):
            send(rows, rows, x_send, x_recv.at[d - 1], dev(lax.rem(x + d, 4), y, z, c))

    for d in range(1, 4):
        send(shift_all.at[c, y], shift_all.at[c, y], s_send.at[0], s_recv.at[0], dev(x, lax.rem(y + d, 4), z, c))
    for o in offsets:
        send(left_all.at[c, here], left_all.at[c, here], l_send.at[0], l_recv.at[0], peer(o))
    for t in range(TPD):
        deliver(z, t)

    def ring_step(i, t):
        zp, zm = lax.rem(z + NZ - i, NZ), lax.rem(z + i, NZ)
        top, low = pl.ds(0, BR // 2), pl.ds(BR // 2, BR // 2)
        if i < 8:
            wait(zbuf.at[zp, t], z_plus.at[t, i - 1])
            block = zbuf.at[zp, t] if i < 7 else zbuf.at[zp, t, top]
            send(block, block, z_send, z_plus.at[t, i], up)
            wait(zbuf.at[zm, t], z_minus.at[t, i - 1])
            block = zbuf.at[zm, t] if i < 7 else zbuf.at[zm, t, low]
            send(block, block, z_send, z_minus.at[t, i], down)
            deliver(zp, t)
            deliver(zm, t)
        else:
            wait(zbuf.at[zp, t, top], z_plus.at[t, 7])
            wait(zbuf.at[zp, t, low], z_minus.at[t, 7])
            deliver(zp, t)

    def pass_rows(d):
        k = lax.rem(x + 4 - d, 4)
        wait(half(k, c), x_recv.at[d - 1])
        send(half(k, c), half(k, c), x_send, x_core, other)

    def pass_small():
        wait(shift_all.at[c, pl.ds(0, 3)], s_recv.at[0])
        send(shift_all.at[c], shift_all.at[c], s_send.at[1], s_recv.at[1], other)
        wait(left_all.at[c, pl.ds(0, 15)], l_recv.at[0])
        send(left_all.at[c], left_all.at[c], l_send.at[1], l_recv.at[1], other)

    to_sm = pltpu.make_async_copy(shift_all, shift_sm, sm_sem)

    def take_small():
        wait(shift_all.at[1 - c], s_recv.at[1])
        to_sm.start()
        wait(left_all.at[1 - c], l_recv.at[1])
        for k in range(KS):
            length = jnp.broadcast_to(left_all[c, 4 * y + k][:, TPD * ROWS : TPD * ROWS + 1], TILE)
            mask[k] = jnp.where(sub.astype(F32) < length, 1.0, 0.0).astype(F32)

    def widen(first, count):
        def body(i, carry):
            cc, r = lax.div(i, 16), lax.rem(i, 16)
            yy, k = lax.div(r, 4), lax.rem(r, 4)
            tile = left_all[cc, r]
            for t in range(TPD):
                for j in range(ROWS):
                    lane = t * ROWS + j
                    left_wide[(yy * 2 + cc) * TPD + t, k, j] = jnp.broadcast_to(tile[:, lane : lane + 1], TILE)
            return carry

        lax.fori_loop(first, first + count, body, 0)

    def take_rows():
        wait(gd.at[pl.ds(0, 3), :, pl.ds(0, 2)], x_core)

    def vectors(first, count):
        def body(r, carry):
            for k in range(KS):
                for j in range(4):
                    g = gd[k, r, j, 0]
                    a = 1.0 / gd[k, r, j, 1]
                    b = g * a
                    v1[k, r, j] = g
                    v1[KS + k, r, j] = b
                    v1[2 * KS + k, r, j] = b * a
            return carry

        lax.fori_loop(first, first + count, body, 0)

    tasks = {i: [lambda i=i: send_rows(i)] for i in range(8)}
    tasks[4].append(pass_small)
    tasks[6].append(take_small)
    for i in range(8):
        tasks.setdefault(i + 7, []).append(lambda i=i: widen(4 * i, 4))
    tasks[15] = [lambda: pass_rows(1)]
    tasks[16] = [lambda: pass_rows(3)]
    tasks[17] = [lambda: pass_rows(2)]
    tasks[18] = [take_rows, lambda: vectors(0, 2)]
    for i in range(19, 23):
        tasks[i] = [lambda i=i: vectors(3 * i - 55, 3)]
    tasks[23] = [lambda: vectors(14, 2)]
    for i in range(1, 9):
        for t in range(TPD):
            ring_step(i, t)
            for task in tasks.get((i - 1) * TPD + t, []):
                task()

    for nn in range(2):
        for k in range(KS):
            j = 2 * c + nn
            inv[k, nn] = 1.0 / gd[k, here, j, 1]
            piece[G, k, nn] = v1[k, here, j]
            piece[B, k, nn] = v1[KS + k, here, j]
            piece[E, k, nn] = v1[2 * KS + k, here, j]
    to_sm.wait()

    def product(v, nk, cut=False, only=None):
        rows = nk * ROWS
        blocks = range(2) if only is None else (only,)
        for nn in blocks:
            y_sum[nn, pl.ds(0, nk)] = jnp.zeros((nk,) + TILE, F32)

        def body(i, carry):
            yy, rest = lax.div(i, 2 * TPD), lax.rem(i, 2 * TPD)
            cc, t = lax.div(rest, TPD), lax.rem(rest, TPD)
            shift = shift_sm[cc, yy, t, 0]
            for nn in blocks:
                m = 16 * (2 * c + nn) + here + shift
                m = jnp.where(m >= NBLK, m - NBLK, m)
                r, j4 = lax.rem(m, 16), lax.div(m, 16)
                tiles = []
                for k in range(nk):
                    src = v[k, r, j4]
                    total = None
                    for j in range(ROWS):
                        term = left_wide[i, k % KS, j] * src[j : j + 1, :]
                        total = term if total is None else total + term
                    tiles.append(total)
                p = jnp.concatenate(tiles, axis=0)
                hi = p.astype(BF16)
                lo = (p - hi.astype(F32)).astype(BF16)
                if cut:
                    full = rbuf[nn, yy, cc, t]
                    rh = full.astype(BF16)
                    rl = (full - rh.astype(F32)).astype(BF16)
                    r_hi[nn, yy, cc, t] = rh
                    r_lo[nn, yy, cc, t] = rl
                else:
                    rh = r_hi[nn, yy, cc, t]
                    rl = r_lo[nn, yy, cc, t]
                both = jnp.dot(jnp.concatenate([hi, lo], axis=0), rh, preferred_element_type=F32)
                more = jnp.dot(hi, rl, preferred_element_type=F32)
                y_sum[nn, pl.ds(0, nk)] += (both[:rows] + both[rows:] + more).reshape((nk,) + TILE)
            return carry

        lax.fori_loop(0, TERMS, body, 0)

    def gather(phase, v):
        def at(r, cc):
            return v.at[:, r, pl.ds(2 * cc, 2)]

        def start():
            for o in offsets:
                send(at(here, c), at(here, c), ag_send.at[phase, 0], ag_recv.at[phase, o], peer(o))
            send(at(here, c), at(here, c), ag_send.at[phase, 1], ag_core.at[phase], other)

        def pass_on(first, last):
            for o in offsets[::-1][first:last]:
                r = sender(o)
                wait(at(r, c), ag_recv.at[phase, o])
                send(at(r, c), at(r, c), ag_send.at[phase, 1], ag_core.at[phase], other)

        def finish():
            wait(v.at[:, :, pl.ds(0, 2)], ag_core.at[phase])

        def sent():
            wait(v.at[:, pl.ds(0, 15), pl.ds(0, 2)], ag_send.at[phase, 0])
            wait(v.at[:, :, pl.ds(0, 2)], ag_send.at[phase, 1])

        return start, pass_on, finish, sent

    def dots(g):
        def start(pairs):
            d_rows[g] = jnp.zeros((16, BR), F32)
            for r, (a, b) in enumerate(pairs):
                prod = (piece[a] * piece[b]).reshape((2 * KS,) + TILE)
                d_rows[g, r : r + 1, :] = jnp.sum(jnp.sum(prod, axis=0), axis=0, keepdims=True)
            total = jnp.broadcast_to(jnp.sum(d_rows[g], axis=1, keepdims=True), (16, BR))
            at_row = lax.broadcasted_iota(jnp.int32, (16, BR), 0) == lax.broadcasted_iota(jnp.int32, (16, BR), 1)
            dz[g, z] = jnp.sum(jnp.where(at_row, total, 0.0), axis=0, keepdims=True)
            for p in zdevs:
                send(dz.at[g, z], dz.at[g, z], dot_send.at[g, 0], dot_recv.at[g, 0], p)

        def plane():
            wait(dz.at[g, pl.ds(0, 15)], dot_recv.at[g, 0])
            dp[g, here] = jnp.sum(dz[g], axis=0)
            for o in offsets:
                send(dp.at[g, here], dp.at[g, here], dot_send.at[g, 1], dot_recv.at[g, 1], peer(o))

        def core():
            wait(dp.at[g, pl.ds(0, 15)], dot_recv.at[g, 1])
            dc[g, c] = jnp.sum(dp[g], axis=0)
            send(dc.at[g, c], dc.at[g, c], dot_send.at[g, 2], dot_recv.at[g, 2], other)

        def done(pairs):
            wait(dc.at[g, 1 - c], dot_recv.at[g, 2])
            total = dc[g, 0] + dc[g, 1]
            return {p: jnp.broadcast_to(total[:, r : r + 1], TILE) for r, p in enumerate(pairs)}

        def sent():
            wait(dz.at[g, pl.ds(0, 15)], dot_send.at[g, 0])
            wait(dp.at[g, pl.ds(0, 15)], dot_send.at[g, 1])
            wait(dc.at[g, c], dot_send.at[g, 2])

        return start, plane, core, done, sent

    apart = lax.rem(y + 8 * c - z + NZ, NZ)
    near = 1 - lax.div(lax.rem(apart + 9, NZ) + 9, NZ)
    for nn in (near, 1 - near):
        wait(rbuf.at[nn], r_recv.at[nn])
        product(v1, 3 * KS, True, nn)
    mine = pl.ds(2 * c, 2)
    for nn in range(2):
        for k in range(KS):
            h = y_sum[nn, k] * mask[k]
            a = h * inv[k, nn]
            piece[H_, k, nn] = h
            piece[Q, k, nn] = y_sum[nn, KS + k] * mask[k]
            piece[S, k, nn] = y_sum[nn, 2 * KS + k] * mask[k]
            piece[A_, k, nn] = a
            piece[AA, k, nn] = a * inv[k, nn]
    v2[:, here, mine] = piece[A_]
    v2b[:, here, mine] = piece[AA]
    ag2, ag2b, ag3 = gather(0, v2), gather(1, v2b), gather(2, v3)
    early, late = dots(0), dots(1)
    ag2[0]()
    early[0](EARLY)
    ag2[1](0, 10)
    early[1]()
    ag2[1](10, 15)
    ag2b[0]()
    ag2[2]()

    product(v2, KS)
    early[2]()
    dot = early[3](EARLY)
    f1 = jnp.sqrt(CELLS / (dot[G, G] + EPS))
    r1 = f1 * f1 * dot[G, H_] / CELLS
    for nn in range(2):
        for k in range(KS):
            p = y_sum[nn, k] * mask[k]
            pp = p - r1 * piece[Q, k, nn]
            piece[P_, k, nn] = p
            piece[PP, k, nn] = pp
            piece[AP, k, nn] = pp * inv[k, nn]
    v3[:, here, mine] = piece[AP]
    ag3[0]()
    late[0](LATE)
    ag2b[1](0, 15)
    ag2b[2]()
    product(v2b, KS)
    for nn in range(2):
        for k in range(KS):
            piece[T, k, nn] = y_sum[nn, k] * mask[k]
    ag3[1](0, 10)
    late[1]()
    ag3[1](10, 15)
    ag3[2]()

    product(v3, KS)
    late[2]()
    dot.update(late[3](LATE))
    dot.update({(b, a): value for (a, b), value in dot.items()})

    c1 = f1 * f1 * (dot[G, A_] - r1 * dot[G, B]) / CELLS
    w = (-f1 * c1, -f1 * r1, f1)
    wy = (w[0], f1)
    x_x = [[dot[i, j] for j in (G, B, A_)] for i in (G, B, A_)]
    x_y = [[dot[G, H_], dot[G, PP]], [dot[G, A_], dot[B, PP]], [dot[A_, H_], dot[A_, PP]]]
    ax_y = [[dot[G, A_], dot[B, PP]], [dot[A_, B], dot[E, PP]], [dot[A_, A_], dot[AA, PP]]]
    ax_x = [
        [dot[G, B], dot[B, B], dot[A_, B]],
        [dot[B, B], dot[E, B], dot[E, A_]],
        [dot[A_, B], dot[E, A_], dot[AA, A_]],
    ]

    def along(weights, row):
        total = weights[0] * row[0]
        for weight, value in zip(weights[1:], row[1:], strict=True):
            total = total + weight * value
        return total

    def form(weights, m):
        return along(w, [along(weights, row) for row in m])

    def column(m, j):
        return [row[j] for row in m]

    uu, uk, uak, uau = form(w, x_x), form(wy, x_y), form(wy, ax_y), form(w, ax_x)
    gu, gk, uh = along(w, x_x[0]), along(wy, x_y[0]), along(w, column(x_y, 0))
    gak, gau, uah = along(wy, x_y[1]), along(w, x_x[1]), along(w, column(x_x, 2))
    f2 = jnp.sqrt(CELLS / (jnp.maximum(uu, 0.0) + EPS))
    b_ = f1 * f2 * (gk + uh) / (2.0 * CELLS)
    d_ = f2 * f2 * uk / CELLS
    h_ = (r1 - d_) / 2.0
    ritz = (r1 + d_) / 2.0 - jnp.sqrt(h_ * h_ + b_ * b_)
    big = jnp.maximum(jnp.abs(h_), jnp.abs(b_))
    safe = jnp.where(big > 0.0, big, 1.0)
    hs = jnp.where(big > 0.0, h_ / safe, 1.0)
    bs = b_ / safe
    rs = jnp.sqrt(hs * hs + bs * bs)
    larger = jnp.sqrt((rs + jnp.abs(hs)) / (2.0 * rs))
    smaller = jnp.abs(bs) / (2.0 * rs * larger)
    co = jnp.where(hs >= 0.0, larger, smaller)
    si = jnp.where(bs < 0.0, -1.0, 1.0) * jnp.where(hs >= 0.0, smaller, larger)
    n1, n2 = -si * f1, co * f2
    e1 = f1 * (n1 * (dot[G, A_] - ritz * dot[G, B]) + n2 * (gak - ritz * gau)) / CELLS
    e2 = f2 * (n1 * (uah - ritz * gau) + n2 * (uak - ritz * uau)) / CELLS
    t2 = {
        A_: n1 + n2 * w[0],
        B: -ritz * (n1 + n2 * w[0]),
        E: -ritz * n2 * w[1],
        AA: -ritz * n2 * w[2],
        AP: n2 * f1,
    }
    dot[A_, AP], dot[B, AP], dot[B, AA] = dot[AA, PP], dot[E, PP], dot[E, A_]
    dot.update({(b, a): value for (a, b), value in dot.items()})
    tt = jnp.zeros(TILE, F32)
    for i in t2:
        row = jnp.zeros(TILE, F32)
        for j in t2:
            row = row + t2[j] * dot[i, j]
        tt = tt + t2[i] * row
    square = tt - 2.0 * CELLS * (e1 * e1 + e2 * e2)
    square = square + e1 * e1 * f1 * f1 * dot[G, G] + e2 * e2 * f2 * f2 * uu + 2.0 * e1 * e2 * f1 * f2 * gu
    f3 = jnp.sqrt(CELLS / (jnp.maximum(square, 0.0) + EPS))
    coef = dict(t2)
    coef[G] = -e1 * f1 - e2 * f2 * w[0]
    coef[B] = coef[B] - e2 * f2 * w[1]
    coef[A_] = coef[A_] - e2 * f2 * w[2]
    coef = {i: f3 * value for i, value in coef.items()}
    image_of = {A_: P_, B: Q, E: S, AA: T, G: H_}
    for nn in range(2):
        for k in range(KS):
            basis = coef[AP] * piece[AP, k, nn]
            image = coef[AP] * (y_sum[nn, k] * mask[k])
            for i in image_of:
                basis = basis + coef[i] * piece[i, k, nn]
                image = image + coef[i] * piece[image_of[i], k, nn]
            out_src[k, nn, 0] = basis
            out_src[k, nn, 1] = image

    spot = 4 * lax.rem(y, 2) + x
    cd = lax.div(y, 2)
    keeps = cd == c
    for k in range(KS):
        for nn in range(2):
            stays = jnp.logical_and(jnp.logical_and(x == k, y == 2 * c + nn), keeps)

            @pl.when(stays)
            def _():
                out_got[spot] = out_src[k, nn]

            @pl.when(jnp.logical_not(stays))
            def _():
                send(out_src.at[k, nn], out_got.at[spot], out_send, out_recv, dev(k, 2 * c + nn, z, cd))

    @pl.when(keeps)
    def _():
        wait(out_got.at[pl.ds(0, 7)], out_recv)
        wait(out_got.at[pl.ds(0, 7)], out_send)

    @pl.when(jnp.logical_not(keeps))
    def _():
        wait(out_got, out_recv)
        wait(out_got, out_send)

    for s in range(8):
        basis_ref[:, s * BR : (s + 1) * BR] = out_got[s, 0]
        image_ref[:, s * BR : (s + 1) * BR] = out_got[s, 1]

    wait(zbuf.at[pl.ds(0, 15)], z_send)
    wait(zbuf.at[pl.ds(0, 14)], r_send)
    wait(gd.at[pl.ds(0, 3)], x_send)
    wait(left_all.at[c, pl.ds(0, 15)], l_send.at[0])
    wait(left_all.at[c], l_send.at[1])
    wait(shift_all.at[c, pl.ds(0, 3)], s_send.at[0])
    wait(shift_all.at[c], s_send.at[1])
    for ag in (ag2, ag2b, ag3):
        ag[3]()
    early[4]()
    late[4]()


def per_device(start_vector, precond_diag, left_env, right_env, right_shift, sector_length):
    vmem = pl.BlockSpec(memory_space=pltpu.VMEM)
    hbm = pl.BlockSpec(memory_space=pltpu.HBM)
    DMA = pltpu.SemaphoreType.DMA
    return pl.pallas_call(
        kernel,
        out_shape=[jax.ShapeDtypeStruct((ROWS, 1024), F32)] * 2,
        in_specs=[hbm] * 6,
        out_specs=[vmem, vmem],
        scratch_shapes=[
            pltpu.VMEM((ROWS, NBLK * BR), F32),
            pltpu.VMEM((ROWS, NBLK * BR), F32),
            pltpu.VMEM((TPD, ROWS, ROWS), F32),
            pltpu.SMEM((TPD,), jnp.int32),
            pltpu.SMEM((1,), jnp.int32),
            pltpu.VMEM((NZ, TPD, BR, BR), F32),
            pltpu.VMEM((2, 4, 2, TPD, BR, BR), F32),
            pltpu.VMEM((2, 4, 2, TPD, BR, BR), BF16),
            pltpu.VMEM((2, 4, 2, TPD, BR, BR), BF16),
            pltpu.VMEM((KS, 16, 4, 2) + TILE, F32),
            pltpu.VMEM((3 * KS, 16, 4) + TILE, F32),
            pltpu.VMEM((KS, 16, 4) + TILE, F32),
            pltpu.VMEM((KS, 16, 4) + TILE, F32),
            pltpu.VMEM((KS, 16, 4) + TILE, F32),
            pltpu.VMEM((2, 3 * KS) + TILE, F32),
            pltpu.VMEM((12, KS, 2) + TILE, F32),
            pltpu.VMEM((KS, 2) + TILE, F32),
            pltpu.VMEM((2, 16) + TILE, F32),
            pltpu.VMEM((2, 4) + TILE, jnp.int32),
            pltpu.SMEM((2, 4) + TILE, jnp.int32),
            pltpu.VMEM((TERMS, KS, ROWS) + TILE, F32),
            pltpu.VMEM((KS,) + TILE, F32),
            pltpu.VMEM((2, 16, BR), F32),
            pltpu.VMEM((2, 16, 1, BR), F32),
            pltpu.VMEM((2, 16, 1, BR), F32),
            pltpu.VMEM((2, 2, 1, BR), F32),
            pltpu.VMEM((KS, 2, 2) + TILE, F32),
            pltpu.VMEM((8, 2) + TILE, F32),
            DMA((6,)),
            DMA,
            DMA((TPD, 8)),
            DMA((TPD, 8)),
            DMA,
            DMA((2,)),
            DMA,
            DMA((3,)),
            DMA,
            DMA((2,)),
            DMA((2,)),
            DMA((2,)),
            DMA((2,)),
            DMA,
            DMA((3, 2)),
            DMA((3, 16)),
            DMA((3,)),
            DMA((2, 3)),
            DMA((2, 3)),
            DMA,
            DMA,
        ],
        compiler_params=pltpu.CompilerParams(
            collective_id=0, has_side_effects=True, vmem_limit_bytes=60 * 1024 * 1024
        ),
        cost_estimate=pl.CostEstimate(flops=600_000_000, bytes_accessed=2_000_000, transcendentals=0),
    )(start_vector, precond_diag, left_env, right_env, right_shift, sector_length)


def solution(mesh):
    placed = (
        P("sec", None),
        P("sec", None),
        P("mpo", "sec", None),
        P("mpo", "sec", None),
        P("mpo"),
        P("sec"),
    )
    return jax.shard_map(
        per_device,
        mesh=mesh,
        in_specs=placed,
        out_specs=(P("sec", "mpo"), P("sec", "mpo")),
        check_vma=False,
    )
```

```python
import jax
import jax.numpy as jnp
from jax import lax
from jax.experimental import pallas as pl
from jax.experimental.pallas import tpu as pltpu
from jax.sharding import PartitionSpec as P

MESH = pl.DeviceIdType.MESH
F32 = jnp.float32
BF16 = jnp.bfloat16

NZ = 16
ROWS, BR, NBLK = 8, 128, 64
TPD = 3
TERMS = 24
KS = 4
CELLS = float(512 * 8192)
EPS = 1e-6
TILE = (ROWS, BR)

G, B, E, H_, Q, A_, AA, PP, AP = range(9)
EARLY = [
    (G, G), (G, H_), (G, B), (G, A_), (B, B), (A_, B), (A_, A_), (A_, H_),
    (E, B), (E, A_), (AA, A_), (E, E), (E, AA), (AA, AA),
]
LATE = [(G, PP), (B, PP), (A_, PP), (E, PP), (AA, PP), (E, AP), (AA, AP), (AP, AP)]


def kernel(
    start_hbm,
    diag_hbm,
    left_hbm,
    right_hbm,
    shift_hbm,
    length_hbm,
    basis_ref,
    image_ref,
    start_ref,
    diag_ref,
    left_ref,
    shift_ref,
    length_ref,
    zbuf,
    rbuf,
    r_hi,
    r_lo,
    gd,
    v1,
    v2,
    v2b,
    v3,
    mixed,
    y_sum,
    piece,
    inv,
    left_all,
    shift_all,
    shift_sm,
    left_wide,
    mask,
    d_rows,
    dz,
    dp,
    dc,
    qs_src,
    qs_got,
    t_src,
    t_got,
    o_src,
    o_got,
    in_sem,
    z_send,
    z_plus,
    z_minus,
    r_send,
    r_recv,
    x_send,
    x_recv,
    x_core,
    l_send,
    l_recv,
    s_send,
    s_recv,
    sm_sem,
    ag_send,
    ag_recv,
    ag_core,
    dot_send,
    dot_recv,
    out_send,
    out_recv,
):
    sec = lax.axis_index("sec")
    mpo = lax.axis_index("mpo")
    z, x = lax.div(sec, 4), lax.rem(sec, 4)
    y, c = lax.div(mpo, 2), lax.rem(mpo, 2)
    here = 4 * y + x

    def dev(xx, yy, zz, cc):
        return (zz * 4 + xx, yy * 2 + cc)

    def send(src, dst, send_sem, recv_sem, where):
        pltpu.make_async_remote_copy(
            src_ref=src,
            dst_ref=dst,
            send_sem=send_sem,
            recv_sem=recv_sem,
            device_id=where,
            device_id_type=MESH,
        ).start()

    def wait(ref, sem):
        pltpu.make_async_copy(ref, ref, sem).wait()

    up = dev(x, y, lax.rem(z + 1, NZ), c)
    down = dev(x, y, lax.rem(z + NZ - 1, NZ), c)
    other = dev(x, y, z, 1 - c)
    zdevs = [dev(x, y, lax.rem(z + d, NZ), c) for d in range(1, NZ)]
    offsets = sorted(range(1, 16), key=lambda o: -(min(o // 4, 4 - o // 4) + min(o % 4, 4 - o % 4)))

    def peer(o):
        return dev(lax.rem(x + o // 4, 4), lax.rem(y + o % 4, 4), z, c)

    def sender(o):
        return 4 * lax.rem(y + 4 - o % 4, 4) + lax.rem(x + 4 - o // 4, 4)

    loads = [
        pltpu.make_async_copy(right_hbm, zbuf.at[z], in_sem.at[0]),
        pltpu.make_async_copy(start_hbm, start_ref, in_sem.at[1]),
        pltpu.make_async_copy(diag_hbm, diag_ref, in_sem.at[2]),
        pltpu.make_async_copy(left_hbm, left_ref, in_sem.at[3]),
        pltpu.make_async_copy(shift_hbm, shift_ref, in_sem.at[4]),
        pltpu.make_async_copy(length_hbm, length_ref, in_sem.at[5]),
    ]
    for load in loads:
        load.start()
    barrier = pltpu.get_barrier_semaphore()
    partners = [up, down, other] + [peer(o) for o in offsets]
    partners += [dev(x, lax.rem(y + d, 4), z, 1 - c) for d in range(1, 4)]
    for p in partners:
        pl.semaphore_signal(barrier, inc=1, device_id=p, device_id_type=MESH)

    sub = lax.broadcasted_iota(jnp.int32, TILE, 0)
    for load in loads[3:]:
        load.wait()
    left_all[c, here] = jnp.zeros(TILE, F32)
    for t in range(TPD):
        left_all[c, here, :, t * ROWS : (t + 1) * ROWS] = left_ref[t]
    left_all[c, here, :, TPD * ROWS : TPD * ROWS + 1] = jnp.full((ROWS, 1), length_ref[0].astype(F32), F32)
    shift_all[c, y] = jnp.where(sub == 0, shift_ref[0], jnp.where(sub == 1, shift_ref[1], shift_ref[2]))
    live0 = jnp.where(sub < length_ref[0], 1.0, 0.0).astype(F32)
    loads[1].wait()
    loads[2].wait()
    for m in range(NBLK):
        gd[x, m % 16, m // 16, 0] = start_ref[:, m * BR : (m + 1) * BR] * live0
        gd[x, m % 16, m // 16, 1] = diag_ref[:, m * BR : (m + 1) * BR]
    loads[0].wait()
    pl.semaphore_wait(barrier, len(partners))

    def deliver(zz, t):
        nn = lax.rem(lax.div(zz, 4), 2)
        yd, cd = lax.rem(zz, 4), lax.div(zz, 8)
        dst = rbuf.at[nn, y, c, t]
        sem = r_recv.at[nn, lax.rem(yd - y + 4, 4)]
        stays = jnp.logical_and(yd == y, cd == c)

        @pl.when(stays)
        def _():
            pltpu.make_async_copy(zbuf.at[zz, t], dst, sem).start()

        @pl.when(jnp.logical_not(stays))
        def _():
            send(zbuf.at[zz, t], dst, r_send, sem, dev(x, yd, z, cd))

    for t in range(TPD):
        send(zbuf.at[z, t], zbuf.at[z, t], z_send, z_plus.at[t, 0], up)
        send(zbuf.at[z, t], zbuf.at[z, t], z_send, z_minus.at[t, 0], down)

    def half(k, cc):
        return gd.at[k, :, pl.ds(2 * cc, 2)]

    def send_rows(i):
        rows = gd.at[x, pl.ds(2 * i, 2), pl.ds(2 * c, 2)]
        for d in (2, 1, 3):
            send(rows, rows, x_send, x_recv.at[d - 1], dev(lax.rem(x + d, 4), y, z, c))

    for d in range(1, 4):
        send(shift_all.at[c, y], shift_all.at[c, y], s_send.at[0], s_recv.at[0], dev(x, lax.rem(y + d, 4), z, c))
    for o in offsets:
        send(left_all.at[c, here], left_all.at[c, here], l_send.at[0], l_recv.at[0], peer(o))
    for t in range(TPD):
        deliver(z, t)

    def ring_step(i, t):
        zp, zm = lax.rem(z + NZ - i, NZ), lax.rem(z + i, NZ)
        top, low = pl.ds(0, BR // 2), pl.ds(BR // 2, BR // 2)
        if i < 8:
            wait(zbuf.at[zp, t], z_plus.at[t, i - 1])
            block = zbuf.at[zp, t] if i < 7 else zbuf.at[zp, t, top]
            send(block, block, z_send, z_plus.at[t, i], up)
            wait(zbuf.at[zm, t], z_minus.at[t, i - 1])
            block = zbuf.at[zm, t] if i < 7 else zbuf.at[zm, t, low]
            send(block, block, z_send, z_minus.at[t, i], down)
            deliver(zp, t)
            deliver(zm, t)
        else:
            wait(zbuf.at[zp, t, top], z_plus.at[t, 7])
            wait(zbuf.at[zp, t, low], z_minus.at[t, 7])
            deliver(zp, t)

    def pass_rows(d):
        k = lax.rem(x + 4 - d, 4)
        wait(half(k, c), x_recv.at[d - 1])
        send(half(k, c), half(k, c), x_send, x_core, other)

    def pass_small():
        wait(shift_all.at[c, pl.ds(0, 3)], s_recv.at[0])
        send(shift_all.at[c], shift_all.at[c], s_send.at[1], s_recv.at[1], other)
        wait(left_all.at[c, pl.ds(0, 15)], l_recv.at[0])
        send(left_all.at[c], left_all.at[c], l_send.at[1], l_recv.at[1], other)

    to_sm = pltpu.make_async_copy(shift_all, shift_sm, sm_sem)

    def take_small():
        wait(shift_all.at[1 - c], s_recv.at[1])
        to_sm.start()
        wait(left_all.at[1 - c], l_recv.at[1])
        for k in range(KS):
            length = jnp.broadcast_to(left_all[c, 4 * y + k][:, TPD * ROWS : TPD * ROWS + 1], TILE)
            mask[k] = jnp.where(sub.astype(F32) < length, 1.0, 0.0).astype(F32)

    def widen(first, count):
        def body(i, carry):
            cc, r = lax.div(i, 16), lax.rem(i, 16)
            yy, k = lax.div(r, 4), lax.rem(r, 4)
            tile = left_all[cc, r]
            for t in range(TPD):
                for j in range(ROWS):
                    lane = t * ROWS + j
                    left_wide[(yy * 2 + cc) * TPD + t, k, j] = jnp.broadcast_to(tile[:, lane : lane + 1], TILE)
            return carry

        lax.fori_loop(first, first + count, body, 0)

    def take_rows():
        wait(gd.at[pl.ds(0, 3), :, pl.ds(0, 2)], x_core)

    def vectors(first, count):
        def body(r, carry):
            for k in range(KS):
                for j in range(4):
                    g = gd[k, r, j, 0]
                    a = 1.0 / gd[k, r, j, 1]
                    b = g * a
                    v1[k, r, j] = g
                    v1[KS + k, r, j] = b
                    v1[2 * KS + k, r, j] = b * a
            return carry

        lax.fori_loop(first, first + count, body, 0)

    def mix(v, nk, first, count, step):
        rows = nk * ROWS

        def body(at, carry):
            for u in range(step):
                i = first + at * step + u
                yy, rest = lax.div(i, 2 * TPD), lax.rem(i, 2 * TPD)
                shift = shift_sm[lax.div(rest, TPD), yy, lax.rem(rest, TPD), 0]
                for nn in range(2):
                    m = 16 * (2 * c + nn) + here + shift
                    m = jnp.where(m >= NBLK, m - NBLK, m)
                    r, j4 = lax.rem(m, 16), lax.div(m, 16)
                    tiles = []
                    for k in range(nk):
                        src = v[k, r, j4]
                        total = None
                        for j in range(ROWS):
                            term = left_wide[i, k % KS, j] * src[j : j + 1, :]
                            total = term if total is None else total + term
                        tiles.append(total)
                    p = jnp.concatenate(tiles, axis=0)
                    hi = p.astype(BF16)
                    mixed[i, nn, 0:rows] = hi
                    mixed[i, nn, rows : 2 * rows] = (p - hi.astype(F32)).astype(BF16)
            return carry

        lax.fori_loop(0, count // step, body, 0)

    def terms_of(nn, yy, rows, cut):
        acc = None
        for q in range(2 * TPD):
            cc, t = q // TPD, q % TPD
            if cut:
                full = rbuf[nn, yy, cc, t]
                rh = full.astype(BF16)
                rl = (full - rh.astype(F32)).astype(BF16)
                r_hi[nn, yy, cc, t] = rh
                r_lo[nn, yy, cc, t] = rl
            else:
                rh = r_hi[nn, yy, cc, t]
                rl = r_lo[nn, yy, cc, t]
            i = yy * 2 * TPD + q
            both = jnp.dot(mixed[i, nn, 0 : 2 * rows], rh, preferred_element_type=F32)
            more = jnp.dot(mixed[i, nn, 0:rows], rl, preferred_element_type=F32)
            res = both[:rows] + both[rows:] + more
            acc = res if acc is None else acc + res
        return acc

    def product(v, nk):
        mix(v, nk, 0, TERMS, 4)
        for nn in range(2):
            acc = terms_of(nn, 0, nk * ROWS, False)
            for yy in range(1, 4):
                acc = acc + terms_of(nn, yy, nk * ROWS, False)
            y_sum[nn, pl.ds(0, nk)] = acc.reshape((nk,) + TILE)

    tasks = {i: [lambda i=i: send_rows(i)] for i in range(8)}
    tasks[4].append(pass_small)
    tasks[6].append(take_small)
    for i in range(4):
        tasks.setdefault(i + 7, []).append(lambda i=i: widen(8 * i, 8))
    tasks[11] = [lambda: pass_rows(1)]
    tasks[12] = [lambda: pass_rows(3)]
    tasks[13] = [lambda: pass_rows(2)]
    tasks[14] = [take_rows, lambda: vectors(0, 4)]
    for i in range(15, 18):
        tasks[i] = [lambda i=i: vectors(4 * i - 56, 4)]
    tasks[17].append(to_sm.wait)
    for i in range(18, 24):
        tasks[i] = [lambda i=i: mix(v1, 3 * KS, 4 * i - 72, 4, 1)]
    for i in range(1, 9):
        for t in range(TPD):
            ring_step(i, t)
            for task in tasks.get((i - 1) * TPD + t, []):
                task()

    for nn in range(2):
        for k in range(KS):
            j = 2 * c + nn
            inv[k, nn] = 1.0 / gd[k, here, j, 1]
            piece[G, k, nn] = v1[k, here, j]
            piece[B, k, nn] = v1[KS + k, here, j]
            piece[E, k, nn] = v1[2 * KS + k, here, j]

    def gather(phase, v):
        def at(r, cc):
            return v.at[:, r, pl.ds(2 * cc, 2)]

        def start(nn):
            half = v.at[:, here, pl.ds(2 * c + nn, 1)]
            for o in offsets:
                send(half, half, ag_send.at[phase, 0], ag_recv.at[phase, o], peer(o))
            send(half, half, ag_send.at[phase, 1], ag_core.at[phase], other)

        def pass_on(first, last):
            for o in offsets[::-1][first:last]:
                r = sender(o)
                wait(at(r, c), ag_recv.at[phase, o])
                send(at(r, c), at(r, c), ag_send.at[phase, 1], ag_core.at[phase], other)

        def finish():
            wait(v.at[:, :, pl.ds(0, 2)], ag_core.at[phase])

        def sent():
            wait(v.at[:, pl.ds(0, 15), pl.ds(0, 2)], ag_send.at[phase, 0])
            wait(v.at[:, :, pl.ds(0, 2)], ag_send.at[phase, 1])

        return start, pass_on, finish, sent

    def dots(g):
        def start(pairs):
            d_rows[g] = jnp.zeros((16, BR), F32)
            for r, (a, b) in enumerate(pairs):
                prod = (piece[a] * piece[b]).reshape((2 * KS,) + TILE)
                d_rows[g, r : r + 1, :] = jnp.sum(jnp.sum(prod, axis=0), axis=0, keepdims=True)
            total = jnp.broadcast_to(jnp.sum(d_rows[g], axis=1, keepdims=True), (16, BR))
            at_row = lax.broadcasted_iota(jnp.int32, (16, BR), 0) == lax.broadcasted_iota(jnp.int32, (16, BR), 1)
            dz[g, z] = jnp.sum(jnp.where(at_row, total, 0.0), axis=0, keepdims=True)
            for p in zdevs:
                send(dz.at[g, z], dz.at[g, z], dot_send.at[g, 0], dot_recv.at[g, 0], p)

        def plane():
            wait(dz.at[g, pl.ds(0, 15)], dot_recv.at[g, 0])
            dp[g, here] = jnp.sum(dz[g], axis=0)
            for o in offsets:
                send(dp.at[g, here], dp.at[g, here], dot_send.at[g, 1], dot_recv.at[g, 1], peer(o))

        def core():
            wait(dp.at[g, pl.ds(0, 15)], dot_recv.at[g, 1])
            dc[g, c] = jnp.sum(dp[g], axis=0)
            send(dc.at[g, c], dc.at[g, c], dot_send.at[g, 2], dot_recv.at[g, 2], other)

        def done(pairs):
            wait(dc.at[g, 1 - c], dot_recv.at[g, 2])
            total = dc[g, 0] + dc[g, 1]
            return {p: jnp.broadcast_to(total[:, r : r + 1], TILE) for r, p in enumerate(pairs)}

        def sent():
            wait(dz.at[g, pl.ds(0, 15)], dot_send.at[g, 0])
            wait(dp.at[g, pl.ds(0, 15)], dot_send.at[g, 1])
            wait(dc.at[g, c], dot_send.at[g, 2])

        return start, plane, core, done, sent

    spot = 4 * lax.rem(y, 2) + x
    cd = lax.div(y, 2)
    keeps = cd == c

    def exchange(i, src, got):
        def start():
            for k in range(KS):
                for nn in range(2):
                    stays = jnp.logical_and(jnp.logical_and(x == k, y == 2 * c + nn), keeps)

                    @pl.when(stays)
                    def _():
                        got[spot] = src[k, nn]

                    @pl.when(jnp.logical_not(stays))
                    def _():
                        where = dev(k, 2 * c + nn, z, cd)
                        send(src.at[k, nn], got.at[spot], out_send.at[i], out_recv.at[i], where)

        def arrived(sem):
            @pl.when(keeps)
            def _():
                wait(got.at[pl.ds(0, 7)], sem.at[i])

            @pl.when(jnp.logical_not(keeps))
            def _():
                wait(got, sem.at[i])

        return start, lambda: arrived(out_recv), lambda: arrived(out_send)

    ex_early, ex_t, ex_o = exchange(0, qs_src, qs_got), exchange(1, t_src, t_got), exchange(2, o_src, o_got)
    ag2, ag2b, ag3 = gather(0, v2), gather(1, v2b), gather(2, v3)
    early, late = dots(0), dots(1)

    apart = lax.rem(y + 8 * c - z + NZ, NZ)
    near = 1 - lax.div(lax.rem(apart + 9, NZ) + 9, NZ)
    for nn in (near, 1 - near):
        acc = None
        for d in (0, 1, 3, 2):
            yy = lax.rem(y - d + 4, 4)
            wait(rbuf.at[nn, yy], r_recv.at[nn, d])
            part = terms_of(nn, yy, 3 * KS * ROWS, True)
            acc = part if acc is None else acc + part
        acc = acc.reshape((3 * KS,) + TILE)
        for k in range(KS):
            h = acc[k] * mask[k]
            a = h * inv[k, nn]
            piece[H_, k, nn] = h
            piece[A_, k, nn] = a
            v2[k, here, 2 * c + nn] = a
            piece[AA, k, nn] = a * inv[k, nn]
            v2b[k, here, 2 * c + nn] = a * inv[k, nn]
            q = acc[KS + k] * mask[k]
            piece[Q, k, nn] = q
            qs_src[k, nn, 0] = q
            qs_src[k, nn, 1] = acc[2 * KS + k] * mask[k]
        ag2[0](nn)
    early[0](EARLY)
    ag2[1](0, 10)
    early[1]()
    ag2b[0](0)
    ag2b[0](1)
    ex_early[0]()
    ag2[1](10, 15)
    ag2[2]()

    product(v2, KS)
    early[2]()
    dot = early[3](EARLY)
    f1 = jnp.sqrt(CELLS / (dot[G, G] + EPS))
    r1 = f1 * f1 * dot[G, H_] / CELLS
    for nn in range(2):
        for k in range(KS):
            pp = y_sum[nn, k] * mask[k] - r1 * piece[Q, k, nn]
            piece[PP, k, nn] = pp
            piece[AP, k, nn] = pp * inv[k, nn]
            v3[k, here, 2 * c + nn] = pp * inv[k, nn]
        ag3[0](nn)
    late[0](LATE)
    ag2b[1](0, 15)
    ag2b[2]()
    product(v2b, KS)
    for nn in range(2):
        for k in range(KS):
            t_src[k, nn] = y_sum[nn, k] * mask[k]
    ex_t[0]()
    ag3[1](0, 10)
    late[1]()
    ag3[1](10, 15)
    ag3[2]()

    product(v3, KS)
    for nn in range(2):
        for k in range(KS):
            o_src[k, nn] = y_sum[nn, k] * mask[k]
    ex_o[0]()
    late[2]()
    dot.update(late[3](LATE))
    dot.update({(b, a): value for (a, b), value in dot.items()})

    c1 = f1 * f1 * (dot[G, A_] - r1 * dot[G, B]) / CELLS
    w = (-f1 * c1, -f1 * r1, f1)
    wy = (w[0], f1)
    x_x = [[dot[i, j] for j in (G, B, A_)] for i in (G, B, A_)]
    x_y = [[dot[G, H_], dot[G, PP]], [dot[G, A_], dot[B, PP]], [dot[A_, H_], dot[A_, PP]]]
    ax_y = [[dot[G, A_], dot[B, PP]], [dot[A_, B], dot[E, PP]], [dot[A_, A_], dot[AA, PP]]]
    ax_x = [
        [dot[G, B], dot[B, B], dot[A_, B]],
        [dot[B, B], dot[E, B], dot[E, A_]],
        [dot[A_, B], dot[E, A_], dot[AA, A_]],
    ]

    def along(weights, row):
        total = weights[0] * row[0]
        for weight, value in zip(weights[1:], row[1:], strict=True):
            total = total + weight * value
        return total

    def form(weights, m):
        return along(w, [along(weights, row) for row in m])

    def column(m, j):
        return [row[j] for row in m]

    uu, uk, uak, uau = form(w, x_x), form(wy, x_y), form(wy, ax_y), form(w, ax_x)
    gu, gk, uh = along(w, x_x[0]), along(wy, x_y[0]), along(w, column(x_y, 0))
    gak, gau, uah = along(wy, x_y[1]), along(w, x_x[1]), along(w, column(x_x, 2))
    f2 = jnp.sqrt(CELLS / (jnp.maximum(uu, 0.0) + EPS))
    b_ = f1 * f2 * (gk + uh) / (2.0 * CELLS)
    d_ = f2 * f2 * uk / CELLS
    h_ = (r1 - d_) / 2.0
    ritz = (r1 + d_) / 2.0 - jnp.sqrt(h_ * h_ + b_ * b_)
    big = jnp.maximum(jnp.abs(h_), jnp.abs(b_))
    safe = jnp.where(big > 0.0, big, 1.0)
    hs = jnp.where(big > 0.0, h_ / safe, 1.0)
    bs = b_ / safe
    rs = jnp.sqrt(hs * hs + bs * bs)
    larger = jnp.sqrt((rs + jnp.abs(hs)) / (2.0 * rs))
    smaller = jnp.abs(bs) / (2.0 * rs * larger)
    co = jnp.where(hs >= 0.0, larger, smaller)
    si = jnp.where(bs < 0.0, -1.0, 1.0) * jnp.where(hs >= 0.0, smaller, larger)
    n1, n2 = -si * f1, co * f2
    e1 = f1 * (n1 * (dot[G, A_] - ritz * dot[G, B]) + n2 * (gak - ritz * gau)) / CELLS
    e2 = f2 * (n1 * (uah - ritz * gau) + n2 * (uak - ritz * uau)) / CELLS
    t2 = {
        A_: n1 + n2 * w[0],
        B: -ritz * (n1 + n2 * w[0]),
        E: -ritz * n2 * w[1],
        AA: -ritz * n2 * w[2],
        AP: n2 * f1,
    }
    dot[A_, AP], dot[B, AP], dot[B, AA] = dot[AA, PP], dot[E, PP], dot[E, A_]
    dot.update({(b, a): value for (a, b), value in dot.items()})
    tt = jnp.zeros(TILE, F32)
    for i in t2:
        row = jnp.zeros(TILE, F32)
        for j in t2:
            row = row + t2[j] * dot[i, j]
        tt = tt + t2[i] * row
    square = tt - 2.0 * CELLS * (e1 * e1 + e2 * e2)
    square = square + e1 * e1 * f1 * f1 * dot[G, G] + e2 * e2 * f2 * f2 * uu + 2.0 * e1 * e2 * f1 * f2 * gu
    f3 = jnp.sqrt(CELLS / (jnp.maximum(square, 0.0) + EPS))
    coef = dict(t2)
    coef[G] = -e1 * f1 - e2 * f2 * w[0]
    coef[B] = coef[B] - e2 * f2 * w[1]
    coef[A_] = coef[A_] - e2 * f2 * w[2]
    coef = {i: f3 * value for i, value in coef.items()}
    coef_q = coef[B] + coef[A_] * r1
    for ex in (ex_early, ex_t, ex_o):
        ex[1]()
    for i in range(8):
        r = 8 * c + i
        a, ap, d = v2[x, r, y], v3[x, r, y], gd[x, r, y, 1]
        basis = coef[AP] * ap + coef[A_] * a + coef[AA] * v2b[x, r, y]
        basis = basis + coef[G] * v1[x, r, y] + coef[B] * v1[KS + x, r, y] + coef[E] * v1[2 * KS + x, r, y]
        image = coef[AP] * o_got[i] + (coef[A_] * ap + coef[G] * a) * d
        image = image + coef_q * qs_got[i, 0] + coef[E] * qs_got[i, 1] + coef[AA] * t_got[i]
        basis_ref[:, i * BR : (i + 1) * BR] = basis
        image_ref[:, i * BR : (i + 1) * BR] = image

    wait(zbuf.at[pl.ds(0, 15)], z_send)
    wait(zbuf.at[pl.ds(0, 14)], r_send)
    wait(gd.at[pl.ds(0, 3)], x_send)
    wait(left_all.at[c, pl.ds(0, 15)], l_send.at[0])
    wait(left_all.at[c], l_send.at[1])
    wait(shift_all.at[c, pl.ds(0, 3)], s_send.at[0])
    wait(shift_all.at[c], s_send.at[1])
    for ag in (ag2, ag2b, ag3):
        ag[3]()
    early[4]()
    late[4]()
    for ex in (ex_early, ex_t, ex_o):
        ex[2]()


def per_device(start_vector, precond_diag, left_env, right_env, right_shift, sector_length):
    vmem = pl.BlockSpec(memory_space=pltpu.VMEM)
    hbm = pl.BlockSpec(memory_space=pltpu.HBM)
    DMA = pltpu.SemaphoreType.DMA
    return pl.pallas_call(
        kernel,
        out_shape=[jax.ShapeDtypeStruct((ROWS, 1024), F32)] * 2,
        in_specs=[hbm] * 6,
        out_specs=[vmem, vmem],
        scratch_shapes=[
            pltpu.VMEM((ROWS, NBLK * BR), F32),
            pltpu.VMEM((ROWS, NBLK * BR), F32),
            pltpu.VMEM((TPD, ROWS, ROWS), F32),
            pltpu.SMEM((TPD,), jnp.int32),
            pltpu.SMEM((1,), jnp.int32),
            pltpu.VMEM((NZ, TPD, BR, BR), F32),
            pltpu.VMEM((2, 4, 2, TPD, BR, BR), F32),
            pltpu.VMEM((2, 4, 2, TPD, BR, BR), BF16),
            pltpu.VMEM((2, 4, 2, TPD, BR, BR), BF16),
            pltpu.VMEM((KS, 16, 4, 2) + TILE, F32),
            pltpu.VMEM((3 * KS, 16, 4) + TILE, F32),
            pltpu.VMEM((KS, 16, 4) + TILE, F32),
            pltpu.VMEM((KS, 16, 4) + TILE, F32),
            pltpu.VMEM((KS, 16, 4) + TILE, F32),
            pltpu.VMEM((TERMS, 2, 6 * KS * ROWS, BR), BF16),
            pltpu.VMEM((2, 3 * KS) + TILE, F32),
            pltpu.VMEM((9, KS, 2) + TILE, F32),
            pltpu.VMEM((KS, 2) + TILE, F32),
            pltpu.VMEM((2, 16) + TILE, F32),
            pltpu.VMEM((2, 4) + TILE, jnp.int32),
            pltpu.SMEM((2, 4) + TILE, jnp.int32),
            pltpu.VMEM((TERMS, KS, ROWS) + TILE, F32),
            pltpu.VMEM((KS,) + TILE, F32),
            pltpu.VMEM((2, 16, BR), F32),
            pltpu.VMEM((2, 16, 1, BR), F32),
            pltpu.VMEM((2, 16, 1, BR), F32),
            pltpu.VMEM((2, 2, 1, BR), F32),
            pltpu.VMEM((KS, 2, 2) + TILE, F32),
            pltpu.VMEM((8, 2) + TILE, F32),
            pltpu.VMEM((KS, 2) + TILE, F32),
            pltpu.VMEM((8,) + TILE, F32),
            pltpu.VMEM((KS, 2) + TILE, F32),
            pltpu.VMEM((8,) + TILE, F32),
            DMA((6,)),
            DMA,
            DMA((TPD, 8)),
            DMA((TPD, 8)),
            DMA,
            DMA((2, 4)),
            DMA,
            DMA((3,)),
            DMA,
            DMA((2,)),
            DMA((2,)),
            DMA((2,)),
            DMA((2,)),
            DMA,
            DMA((3, 2)),
            DMA((3, 16)),
            DMA((3,)),
            DMA((2, 3)),
            DMA((2, 3)),
            DMA((3,)),
            DMA((3,)),
        ],
        compiler_params=pltpu.CompilerParams(
            collective_id=0, has_side_effects=True, vmem_limit_bytes=60 * 1024 * 1024
        ),
        cost_estimate=pl.CostEstimate(flops=600_000_000, bytes_accessed=2_000_000, transcendentals=0),
    )(start_vector, precond_diag, left_env, right_env, right_shift, sector_length)


def solution(mesh):
    placed = (
        P("sec", None),
        P("sec", None),
        P("mpo", "sec", None),
        P("mpo", "sec", None),
        P("mpo"),
        P("sec"),
    )
    return jax.shard_map(
        per_device,
        mesh=mesh,
        in_specs=placed,
        out_specs=(P("sec", "mpo"), P("sec", "mpo")),
        check_vma=False,
    )
```

```python
import jax
import jax.numpy as jnp
from jax import lax
from jax.experimental import pallas as pl
from jax.experimental.pallas import tpu as pltpu
from jax.sharding import PartitionSpec as P

MESH = pl.DeviceIdType.MESH
F32 = jnp.float32
BF16 = jnp.bfloat16

NZ = 16
ROWS, BR, NBLK = 8, 128, 64
TPD = 3
TERMS = 24
KS = 4
CELLS = float(512 * 8192)
EPS = 1e-6
TILE = (ROWS, BR)

G, B, E, H_, Q, A_, AA, PP, AP = range(9)
EARLY = [
    (G, G), (G, H_), (G, B), (G, A_), (B, B), (A_, B), (A_, A_), (A_, H_),
    (E, B), (E, A_), (AA, A_), (E, E), (E, AA), (AA, AA),
]
LATE = [(G, PP), (B, PP), (A_, PP), (E, PP), (AA, PP), (E, AP), (AA, AP), (AP, AP)]


def kernel(
    start_hbm,
    diag_hbm,
    left_hbm,
    right_hbm,
    shift_hbm,
    length_hbm,
    basis_ref,
    image_ref,
    start_ref,
    diag_ref,
    left_ref,
    shift_ref,
    length_ref,
    zbuf,
    rbuf,
    r_hi,
    r_lo,
    gd,
    v1,
    v2,
    v2b,
    v3,
    mixed,
    y_sum,
    piece,
    inv,
    left_all,
    shift_all,
    shift_sm,
    left_wide,
    mask,
    d_rows,
    dz,
    dp,
    dc,
    qs_src,
    qs_got,
    t_src,
    t_got,
    o_src,
    o_got,
    in_sem,
    z_send,
    z_plus,
    z_minus,
    opp_send,
    opp_recv,
    r_send,
    r_recv,
    x_send,
    x_recv,
    x_core,
    l_send,
    l_recv,
    s_send,
    s_recv,
    sm_sem,
    ag_send,
    ag_recv,
    ag_core,
    dot_send,
    dot_recv,
    out_send,
    out_recv,
):
    sec = lax.axis_index("sec")
    mpo = lax.axis_index("mpo")
    z, x = lax.div(sec, 4), lax.rem(sec, 4)
    y, c = lax.div(mpo, 2), lax.rem(mpo, 2)
    here = 4 * y + x

    def dev(xx, yy, zz, cc):
        return (zz * 4 + xx, yy * 2 + cc)

    def send(src, dst, send_sem, recv_sem, where):
        pltpu.make_async_remote_copy(
            src_ref=src,
            dst_ref=dst,
            send_sem=send_sem,
            recv_sem=recv_sem,
            device_id=where,
            device_id_type=MESH,
        ).start()

    def wait(ref, sem):
        pltpu.make_async_copy(ref, ref, sem).wait()

    up = dev(x, y, lax.rem(z + 1, NZ), c)
    down = dev(x, y, lax.rem(z + NZ - 1, NZ), c)
    other = dev(x, y, z, 1 - c)
    zdevs = [dev(x, y, lax.rem(z + d, NZ), c) for d in range(1, NZ)]
    offsets = sorted(range(1, 16), key=lambda o: -(min(o // 4, 4 - o // 4) + min(o % 4, 4 - o % 4)))

    def peer(o):
        return dev(lax.rem(x + o // 4, 4), lax.rem(y + o % 4, 4), z, c)

    def sender(o):
        return 4 * lax.rem(y + 4 - o % 4, 4) + lax.rem(x + 4 - o // 4, 4)

    loads = [
        pltpu.make_async_copy(right_hbm, zbuf.at[z, pl.ds(0, TPD)], in_sem.at[0]),
        pltpu.make_async_copy(start_hbm, start_ref, in_sem.at[1]),
        pltpu.make_async_copy(diag_hbm, diag_ref, in_sem.at[2]),
        pltpu.make_async_copy(left_hbm, left_ref, in_sem.at[3]),
        pltpu.make_async_copy(shift_hbm, shift_ref, in_sem.at[4]),
        pltpu.make_async_copy(length_hbm, length_ref, in_sem.at[5]),
    ]
    for load in loads:
        load.start()
    barrier = pltpu.get_barrier_semaphore()
    ydevs = [dev(x, lax.rem(y + d, 4), z, c) for d in range(1, 4)]
    xdevs = [dev(lax.rem(x + d, 4), y, z, c) for d in range(1, 4)]
    partners = [up, down, other] + xdevs + ydevs
    partners += [dev(x, lax.rem(y + d, 4), z, 1 - c) for d in range(1, 4)]
    for p in partners:
        pl.semaphore_signal(barrier, inc=1, device_id=p, device_id_type=MESH)

    sub = lax.broadcasted_iota(jnp.int32, TILE, 0)
    for load in loads[3:]:
        load.wait()
    left_all[c, here] = jnp.zeros(TILE, F32)
    for t in range(TPD):
        left_all[c, here, :, t * ROWS : (t + 1) * ROWS] = left_ref[t]
    left_all[c, here, :, TPD * ROWS : TPD * ROWS + 1] = jnp.full((ROWS, 1), length_ref[0].astype(F32), F32)
    shift_all[c, y] = jnp.where(sub == 0, shift_ref[0], jnp.where(sub == 1, shift_ref[1], shift_ref[2]))
    live0 = jnp.where(sub < length_ref[0], 1.0, 0.0).astype(F32)
    for load in loads[1:3]:
        load.wait()
    for m in range(NBLK):
        gd[x, m % 16, m // 16, 0] = start_ref[:, m * BR : (m + 1) * BR] * live0
        gd[x, m % 16, m // 16, 1] = diag_ref[:, m * BR : (m + 1) * BR]
    loads[0].wait()
    pl.semaphore_wait(barrier, len(partners))

    kind = lax.rem(z - y + 4, 4)

    def is_kind(i, which):
        return lax.rem(kind + i + NZ, 4) == which

    def deliver(zz, u):
        nn = lax.rem(lax.div(zz, 4), 2)
        yd, cd = lax.rem(zz, 4), lax.div(zz, 8)
        if u < TPD:
            dst, sem = rbuf.at[nn, y, c, u], r_recv.at[nn, lax.rem(yd - y + 4, 4)]
        else:
            dst, sem = rbuf.at[nn, lax.rem(y + 2, 4), c, u - TPD], r_recv.at[nn, 2]
        stays = jnp.logical_and(yd == y, cd == c)

        @pl.when(stays)
        def _():
            pltpu.make_async_copy(zbuf.at[zz, u], dst, sem).start()

        @pl.when(jnp.logical_not(stays))
        def _():
            send(zbuf.at[zz, u], dst, r_send, sem, dev(x, yd, z, cd))

    def first_sends(u):
        send(zbuf.at[z, u], zbuf.at[z, u], z_send, z_plus.at[u, 0], up)
        send(zbuf.at[z, u], zbuf.at[z, u], z_send, z_minus.at[u, 0], down)

    @pl.when(is_kind(0, 2))
    def _():
        for t in range(TPD):
            send(zbuf.at[z, t], zbuf.at[z, TPD + t], opp_send, opp_recv.at[t], dev(x, lax.rem(y + 2, 4), z, c))

    @pl.when(jnp.logical_not(is_kind(0, 2)))
    def _():
        for t in range(TPD):
            first_sends(t)
            deliver(z, t)

    def half(k, cc):
        return gd.at[k, :, pl.ds(2 * cc, 2)]

    def send_rows(i):
        rows = gd.at[x, pl.ds(2 * i, 2), pl.ds(2 * c, 2)]
        for d in (2, 1, 3):
            send(rows, rows, x_send, x_recv.at[d - 1], dev(lax.rem(x + d, 4), y, z, c))

    for d in range(3):
        send(shift_all.at[c, y], shift_all.at[c, y], s_send.at[0], s_recv.at[0], ydevs[d])
        send(left_all.at[c, here], left_all.at[c, here], l_send.at[0], l_recv.at[0], xdevs[d])

    def send_opposite():
        @pl.when(is_kind(0, 0))
        def _():
            for u in range(TPD, 2 * TPD):
                wait(zbuf.at[z, u], opp_recv.at[u - TPD])
                first_sends(u)
                deliver(z, u)

    def ring_step(i, u):
        zp, zm = lax.rem(z + NZ - i, NZ), lax.rem(z + i, NZ)
        top, low = pl.ds(0, BR // 2), pl.ds(BR // 2, BR // 2)

        def has(j):
            return is_kind(j, 0) if u >= TPD else jnp.logical_not(is_kind(j, 2))

        if i < 8:

            @pl.when(has(-i))
            def _():
                wait(zbuf.at[zp, u], z_plus.at[u, i - 1])
                block = zbuf.at[zp, u] if i < 7 else zbuf.at[zp, u, top]
                send(block, block, z_send, z_plus.at[u, i], up)

            @pl.when(has(i))
            def _():
                wait(zbuf.at[zm, u], z_minus.at[u, i - 1])
                block = zbuf.at[zm, u] if i < 7 else zbuf.at[zm, u, low]
                send(block, block, z_send, z_minus.at[u, i], down)
                deliver(zm, u)

            @pl.when(has(-i))
            def _():
                deliver(zp, u)

        else:

            @pl.when(has(0))
            def _():
                wait(zbuf.at[zp, u, top], z_plus.at[u, 7])
                wait(zbuf.at[zp, u, low], z_minus.at[u, 7])
                deliver(zp, u)

    def pass_rows(d):
        k = lax.rem(x + 4 - d, 4)
        wait(half(k, c), x_recv.at[d - 1])
        send(half(k, c), half(k, c), x_send, x_core, other)

    def pass_left():
        wait(left_all.at[c, pl.ds(0, 3)], l_recv.at[0])
        row = left_all.at[c, pl.ds(4 * y, 4)]
        for d in range(3):
            send(row, row, l_send.at[1], l_recv.at[1], ydevs[d])

    def pass_small():
        wait(shift_all.at[c, pl.ds(0, 3)], s_recv.at[0])
        send(shift_all.at[c], shift_all.at[c], s_send.at[1], s_recv.at[1], other)
        wait(left_all.at[c, pl.ds(0, 12)], l_recv.at[1])
        send(left_all.at[c], left_all.at[c], l_send.at[2], l_recv.at[2], other)

    to_sm = pltpu.make_async_copy(shift_all, shift_sm, sm_sem)

    def take_small():
        wait(shift_all.at[1 - c], s_recv.at[1])
        to_sm.start()
        wait(left_all.at[1 - c], l_recv.at[2])
        for k in range(KS):
            length = jnp.broadcast_to(left_all[c, 4 * y + k][:, TPD * ROWS : TPD * ROWS + 1], TILE)
            mask[k] = jnp.where(sub.astype(F32) < length, 1.0, 0.0).astype(F32)

    def widen(first, count):
        def body(i, carry):
            cc, r = lax.div(i, 16), lax.rem(i, 16)
            yy, k = lax.div(r, 4), lax.rem(r, 4)
            tile = left_all[cc, r]
            for t in range(TPD):
                for j in range(ROWS):
                    lane = t * ROWS + j
                    left_wide[(yy * 2 + cc) * TPD + t, k, j] = jnp.broadcast_to(tile[:, lane : lane + 1], TILE)
            return carry

        lax.fori_loop(first, first + count, body, 0)

    def take_rows():
        wait(gd.at[pl.ds(0, 3), :, pl.ds(0, 2)], x_core)

    def vectors(first, count):
        def body(r, carry):
            for k in range(KS):
                for j in range(4):
                    g = gd[k, r, j, 0]
                    a = 1.0 / gd[k, r, j, 1]
                    b = g * a
                    v1[k, r, j] = g
                    v1[KS + k, r, j] = b
                    v1[2 * KS + k, r, j] = b * a
            return carry

        lax.fori_loop(first, first + count, body, 0)

    def mix(v, nk, first, count, step):
        rows = nk * ROWS

        def body(at, carry):
            for u in range(step):
                i = first + at * step + u
                yy, rest = lax.div(i, 2 * TPD), lax.rem(i, 2 * TPD)
                shift = shift_sm[lax.div(rest, TPD), yy, lax.rem(rest, TPD), 0]
                for nn in range(2):
                    m = 16 * (2 * c + nn) + here + shift
                    m = jnp.where(m >= NBLK, m - NBLK, m)
                    r, j4 = lax.rem(m, 16), lax.div(m, 16)
                    tiles = []
                    for k in range(nk):
                        src = v[k, r, j4]
                        total = None
                        for j in range(ROWS):
                            term = left_wide[i, k % KS, j] * src[j : j + 1, :]
                            total = term if total is None else total + term
                        tiles.append(total)
                    p = jnp.concatenate(tiles, axis=0)
                    hi = p.astype(BF16)
                    mixed[i, nn, 0:rows] = hi
                    mixed[i, nn, rows : 2 * rows] = (p - hi.astype(F32)).astype(BF16)
            return carry

        lax.fori_loop(0, count // step, body, 0)

    def terms_of(nn, yy, rows, cut):
        acc = None
        for q in range(2 * TPD):
            cc, t = q // TPD, q % TPD
            if cut:
                full = rbuf[nn, yy, cc, t]
                rh = full.astype(BF16)
                rl = (full - rh.astype(F32)).astype(BF16)
                r_hi[nn, yy, cc, t] = rh
                r_lo[nn, yy, cc, t] = rl
            else:
                rh = r_hi[nn, yy, cc, t]
                rl = r_lo[nn, yy, cc, t]
            i = yy * 2 * TPD + q
            both = jnp.dot(mixed[i, nn, 0 : 2 * rows], rh, preferred_element_type=F32)
            more = jnp.dot(mixed[i, nn, 0:rows], rl, preferred_element_type=F32)
            res = both[:rows] + both[rows:] + more
            acc = res if acc is None else acc + res
        return acc

    def product(v, nk):
        mix(v, nk, 0, TERMS, 4)
        for nn in range(2):
            acc = terms_of(nn, 0, nk * ROWS, False)
            for yy in range(1, 4):
                acc = acc + terms_of(nn, yy, nk * ROWS, False)
            y_sum[nn, pl.ds(0, nk)] = acc.reshape((nk,) + TILE)

    tasks = {i: [lambda i=i: send_rows(i)] for i in range(8)}
    tasks[2].append(pass_left)
    tasks[4].append(pass_small)
    tasks[6].append(take_small)
    for i in range(4):
        tasks.setdefault(i + 7, []).append(lambda i=i: widen(8 * i, 8))
    tasks[11] = [lambda: pass_rows(1)]
    tasks[12] = [lambda: pass_rows(3)]
    tasks[13] = [lambda: pass_rows(2)]
    tasks[14] = [take_rows, lambda: vectors(0, 4)]
    for i in range(15, 18):
        tasks[i] = [lambda i=i: vectors(4 * i - 56, 4)]
    tasks[17].append(to_sm.wait)
    for i in range(18, 24):
        tasks[i] = [lambda i=i: mix(v1, 3 * KS, 4 * i - 72, 4, 1)]
    for i in range(1, 9):
        for t in range(TPD):
            ring_step(i, t)
            for task in tasks.get((i - 1) * TPD + t, []):
                task()
        for t in range(TPD):
            if i == 1:
                continue
            ring_step(i - 1, TPD + t)
        if i == 1:
            send_opposite()
    for t in range(TPD):
        ring_step(8, TPD + t)

    for nn in range(2):
        for k in range(KS):
            j = 2 * c + nn
            inv[k, nn] = 1.0 / gd[k, here, j, 1]
            piece[G, k, nn] = v1[k, here, j]
            piece[B, k, nn] = v1[KS + k, here, j]
            piece[E, k, nn] = v1[2 * KS + k, here, j]

    def gather(phase, v):
        def at(r, cc):
            return v.at[:, r, pl.ds(2 * cc, 2)]

        def start(nn):
            half = v.at[:, here, pl.ds(2 * c + nn, 1)]
            for o in offsets:
                send(half, half, ag_send.at[phase, 0], ag_recv.at[phase, o], peer(o))
            send(half, half, ag_send.at[phase, 1], ag_core.at[phase], other)

        def pass_on(first, last):
            for o in offsets[::-1][first:last]:
                r = sender(o)
                wait(at(r, c), ag_recv.at[phase, o])
                send(at(r, c), at(r, c), ag_send.at[phase, 1], ag_core.at[phase], other)

        def finish():
            wait(v.at[:, :, pl.ds(0, 2)], ag_core.at[phase])

        def sent():
            wait(v.at[:, pl.ds(0, 15), pl.ds(0, 2)], ag_send.at[phase, 0])
            wait(v.at[:, :, pl.ds(0, 2)], ag_send.at[phase, 1])

        return start, pass_on, finish, sent

    def dots(g):
        def start(pairs):
            d_rows[g] = jnp.zeros((16, BR), F32)
            for r, (a, b) in enumerate(pairs):
                prod = (piece[a] * piece[b]).reshape((2 * KS,) + TILE)
                d_rows[g, r : r + 1, :] = jnp.sum(jnp.sum(prod, axis=0), axis=0, keepdims=True)
            total = jnp.broadcast_to(jnp.sum(d_rows[g], axis=1, keepdims=True), (16, BR))
            at_row = lax.broadcasted_iota(jnp.int32, (16, BR), 0) == lax.broadcasted_iota(jnp.int32, (16, BR), 1)
            dz[g, z] = jnp.sum(jnp.where(at_row, total, 0.0), axis=0, keepdims=True)
            for p in zdevs:
                send(dz.at[g, z], dz.at[g, z], dot_send.at[g, 0], dot_recv.at[g, 0], p)

        def plane():
            wait(dz.at[g, pl.ds(0, 15)], dot_recv.at[g, 0])
            dp[g, here] = jnp.sum(dz[g], axis=0)
            for o in offsets:
                send(dp.at[g, here], dp.at[g, here], dot_send.at[g, 1], dot_recv.at[g, 1], peer(o))

        def core():
            wait(dp.at[g, pl.ds(0, 15)], dot_recv.at[g, 1])
            dc[g, c] = jnp.sum(dp[g], axis=0)
            send(dc.at[g, c], dc.at[g, c], dot_send.at[g, 2], dot_recv.at[g, 2], other)

        def done(pairs):
            wait(dc.at[g, 1 - c], dot_recv.at[g, 2])
            total = dc[g, 0] + dc[g, 1]
            return {p: jnp.broadcast_to(total[:, r : r + 1], TILE) for r, p in enumerate(pairs)}

        def sent():
            wait(dz.at[g, pl.ds(0, 15)], dot_send.at[g, 0])
            wait(dp.at[g, pl.ds(0, 15)], dot_send.at[g, 1])
            wait(dc.at[g, c], dot_send.at[g, 2])

        return start, plane, core, done, sent

    spot = 4 * lax.rem(y, 2) + x
    cd = lax.div(y, 2)
    keeps = cd == c

    def exchange(i, src, got):
        def start():
            for k in range(KS):
                for nn in range(2):
                    stays = jnp.logical_and(jnp.logical_and(x == k, y == 2 * c + nn), keeps)

                    @pl.when(stays)
                    def _():
                        got[spot] = src[k, nn]

                    @pl.when(jnp.logical_not(stays))
                    def _():
                        where = dev(k, 2 * c + nn, z, cd)
                        send(src.at[k, nn], got.at[spot], out_send.at[i], out_recv.at[i], where)

        def arrived(sem):
            @pl.when(keeps)
            def _():
                wait(got.at[pl.ds(0, 7)], sem.at[i])

            @pl.when(jnp.logical_not(keeps))
            def _():
                wait(got, sem.at[i])

        return start, lambda: arrived(out_recv), lambda: arrived(out_send)

    ex_early, ex_t, ex_o = exchange(0, qs_src, qs_got), exchange(1, t_src, t_got), exchange(2, o_src, o_got)
    ag2, ag2b, ag3 = gather(0, v2), gather(1, v2b), gather(2, v3)
    early, late = dots(0), dots(1)

    apart = lax.rem(y + 8 * c - z + NZ, NZ)
    near = 1 - lax.div(lax.rem(apart + 9, NZ) + 9, NZ)
    for nn in (near, 1 - near):
        acc = None
        for d in (0, 1, 3, 2):
            yy = lax.rem(y - d + 4, 4)
            wait(rbuf.at[nn, yy], r_recv.at[nn, d])
            part = terms_of(nn, yy, 3 * KS * ROWS, True)
            acc = part if acc is None else acc + part
        acc = acc.reshape((3 * KS,) + TILE)
        for k in range(KS):
            h = acc[k] * mask[k]
            a = h * inv[k, nn]
            piece[H_, k, nn] = h
            piece[A_, k, nn] = a
            v2[k, here, 2 * c + nn] = a
            piece[AA, k, nn] = a * inv[k, nn]
            v2b[k, here, 2 * c + nn] = a * inv[k, nn]
            q = acc[KS + k] * mask[k]
            piece[Q, k, nn] = q
            qs_src[k, nn, 0] = q
            qs_src[k, nn, 1] = acc[2 * KS + k] * mask[k]
        ag2[0](nn)
    early[0](EARLY)
    ag2[1](0, 10)
    early[1]()
    ag2b[0](0)
    ag2b[0](1)
    ex_early[0]()
    ag2[1](10, 15)
    ag2[2]()

    product(v2, KS)
    early[2]()
    dot = early[3](EARLY)
    f1 = jnp.sqrt(CELLS / (dot[G, G] + EPS))
    r1 = f1 * f1 * dot[G, H_] / CELLS
    for nn in range(2):
        for k in range(KS):
            pp = y_sum[nn, k] * mask[k] - r1 * piece[Q, k, nn]
            piece[PP, k, nn] = pp
            piece[AP, k, nn] = pp * inv[k, nn]
            v3[k, here, 2 * c + nn] = pp * inv[k, nn]
        ag3[0](nn)
    late[0](LATE)
    ag2b[1](0, 15)
    ag2b[2]()
    product(v2b, KS)
    for nn in range(2):
        for k in range(KS):
            t_src[k, nn] = y_sum[nn, k] * mask[k]
    ex_t[0]()
    ag3[1](0, 10)
    late[1]()
    ag3[1](10, 15)
    ag3[2]()

    product(v3, KS)
    for nn in range(2):
        for k in range(KS):
            o_src[k, nn] = y_sum[nn, k] * mask[k]
    ex_o[0]()
    late[2]()
    dot.update(late[3](LATE))
    dot.update({(b, a): value for (a, b), value in dot.items()})

    c1 = f1 * f1 * (dot[G, A_] - r1 * dot[G, B]) / CELLS
    w = (-f1 * c1, -f1 * r1, f1)
    wy = (w[0], f1)
    x_x = [[dot[i, j] for j in (G, B, A_)] for i in (G, B, A_)]
    x_y = [[dot[G, H_], dot[G, PP]], [dot[G, A_], dot[B, PP]], [dot[A_, H_], dot[A_, PP]]]
    ax_y = [[dot[G, A_], dot[B, PP]], [dot[A_, B], dot[E, PP]], [dot[A_, A_], dot[AA, PP]]]
    ax_x = [
        [dot[G, B], dot[B, B], dot[A_, B]],
        [dot[B, B], dot[E, B], dot[E, A_]],
        [dot[A_, B], dot[E, A_], dot[AA, A_]],
    ]

    def along(weights, row):
        total = weights[0] * row[0]
        for weight, value in zip(weights[1:], row[1:], strict=True):
            total = total + weight * value
        return total

    def form(weights, m):
        return along(w, [along(weights, row) for row in m])

    def column(m, j):
        return [row[j] for row in m]

    uu, uk, uak, uau = form(w, x_x), form(wy, x_y), form(wy, ax_y), form(w, ax_x)
    gu, gk, uh = along(w, x_x[0]), along(wy, x_y[0]), along(w, column(x_y, 0))
    gak, gau, uah = along(wy, x_y[1]), along(w, x_x[1]), along(w, column(x_x, 2))
    f2 = jnp.sqrt(CELLS / (jnp.maximum(uu, 0.0) + EPS))
    b_ = f1 * f2 * (gk + uh) / (2.0 * CELLS)
    d_ = f2 * f2 * uk / CELLS
    h_ = (r1 - d_) / 2.0
    ritz = (r1 + d_) / 2.0 - jnp.sqrt(h_ * h_ + b_ * b_)
    big = jnp.maximum(jnp.abs(h_), jnp.abs(b_))
    safe = jnp.where(big > 0.0, big, 1.0)
    hs = jnp.where(big > 0.0, h_ / safe, 1.0)
    bs = b_ / safe
    rs = jnp.sqrt(hs * hs + bs * bs)
    larger = jnp.sqrt((rs + jnp.abs(hs)) / (2.0 * rs))
    smaller = jnp.abs(bs) / (2.0 * rs * larger)
    co = jnp.where(hs >= 0.0, larger, smaller)
    si = jnp.where(bs < 0.0, -1.0, 1.0) * jnp.where(hs >= 0.0, smaller, larger)
    n1, n2 = -si * f1, co * f2
    e1 = f1 * (n1 * (dot[G, A_] - ritz * dot[G, B]) + n2 * (gak - ritz * gau)) / CELLS
    e2 = f2 * (n1 * (uah - ritz * gau) + n2 * (uak - ritz * uau)) / CELLS
    t2 = {
        A_: n1 + n2 * w[0],
        B: -ritz * (n1 + n2 * w[0]),
        E: -ritz * n2 * w[1],
        AA: -ritz * n2 * w[2],
        AP: n2 * f1,
    }
    dot[A_, AP], dot[B, AP], dot[B, AA] = dot[AA, PP], dot[E, PP], dot[E, A_]
    dot.update({(b, a): value for (a, b), value in dot.items()})
    tt = jnp.zeros(TILE, F32)
    for i in t2:
        row = jnp.zeros(TILE, F32)
        for j in t2:
            row = row + t2[j] * dot[i, j]
        tt = tt + t2[i] * row
    square = tt - 2.0 * CELLS * (e1 * e1 + e2 * e2)
    square = square + e1 * e1 * f1 * f1 * dot[G, G] + e2 * e2 * f2 * f2 * uu + 2.0 * e1 * e2 * f1 * f2 * gu
    f3 = jnp.sqrt(CELLS / (jnp.maximum(square, 0.0) + EPS))
    coef = dict(t2)
    coef[G] = -e1 * f1 - e2 * f2 * w[0]
    coef[B] = coef[B] - e2 * f2 * w[1]
    coef[A_] = coef[A_] - e2 * f2 * w[2]
    coef = {i: f3 * value for i, value in coef.items()}
    coef_q = coef[B] + coef[A_] * r1
    for ex in (ex_early, ex_t, ex_o):
        ex[1]()
    for i in range(8):
        r = 8 * c + i
        a, ap, d = v2[x, r, y], v3[x, r, y], gd[x, r, y, 1]
        basis = coef[AP] * ap + coef[A_] * a + coef[AA] * v2b[x, r, y]
        basis = basis + coef[G] * v1[x, r, y] + coef[B] * v1[KS + x, r, y] + coef[E] * v1[2 * KS + x, r, y]
        image = coef[AP] * o_got[i] + (coef[A_] * ap + coef[G] * a) * d
        image = image + coef_q * qs_got[i, 0] + coef[E] * qs_got[i, 1] + coef[AA] * t_got[i]
        basis_ref[:, i * BR : (i + 1) * BR] = basis
        image_ref[:, i * BR : (i + 1) * BR] = image

    wait(zbuf.at[pl.ds(0, 15), pl.ds(0, TPD)], z_send)
    wait(zbuf.at[pl.ds(0, 12), pl.ds(0, TPD)], r_send)

    @pl.when(is_kind(0, 2))
    def _():
        wait(zbuf.at[0, pl.ds(0, TPD)], opp_send)

    wait(gd.at[pl.ds(0, 3)], x_send)
    wait(left_all.at[c, pl.ds(0, 3)], l_send.at[0])
    wait(left_all.at[c, pl.ds(0, 12)], l_send.at[1])
    wait(left_all.at[c], l_send.at[2])
    wait(shift_all.at[c, pl.ds(0, 3)], s_send.at[0])
    wait(shift_all.at[c], s_send.at[1])
    for ag in (ag2, ag2b, ag3):
        ag[3]()
    early[4]()
    late[4]()
    for ex in (ex_early, ex_t, ex_o):
        ex[2]()


def per_device(start_vector, precond_diag, left_env, right_env, right_shift, sector_length):
    vmem = pl.BlockSpec(memory_space=pltpu.VMEM)
    hbm = pl.BlockSpec(memory_space=pltpu.HBM)
    DMA = pltpu.SemaphoreType.DMA
    return pl.pallas_call(
        kernel,
        out_shape=[jax.ShapeDtypeStruct((ROWS, 1024), F32)] * 2,
        in_specs=[hbm] * 6,
        out_specs=[vmem, vmem],
        scratch_shapes=[
            pltpu.VMEM((ROWS, NBLK * BR), F32),
            pltpu.VMEM((ROWS, NBLK * BR), F32),
            pltpu.VMEM((TPD, ROWS, ROWS), F32),
            pltpu.SMEM((TPD,), jnp.int32),
            pltpu.SMEM((1,), jnp.int32),
            pltpu.VMEM((NZ, 2 * TPD, BR, BR), F32),
            pltpu.VMEM((2, 4, 2, TPD, BR, BR), F32),
            pltpu.VMEM((2, 4, 2, TPD, BR, BR), BF16),
            pltpu.VMEM((2, 4, 2, TPD, BR, BR), BF16),
            pltpu.VMEM((KS, 16, 4, 2) + TILE, F32),
            pltpu.VMEM((3 * KS, 16, 4) + TILE, F32),
            pltpu.VMEM((KS, 16, 4) + TILE, F32),
            pltpu.VMEM((KS, 16, 4) + TILE, F32),
            pltpu.VMEM((KS, 16, 4) + TILE, F32),
            pltpu.VMEM((TERMS, 2, 6 * KS * ROWS, BR), BF16),
            pltpu.VMEM((2, 3 * KS) + TILE, F32),
            pltpu.VMEM((9, KS, 2) + TILE, F32),
            pltpu.VMEM((KS, 2) + TILE, F32),
            pltpu.VMEM((2, 16) + TILE, F32),
            pltpu.VMEM((2, 4) + TILE, jnp.int32),
            pltpu.SMEM((2, 4) + TILE, jnp.int32),
            pltpu.VMEM((TERMS, KS, ROWS) + TILE, F32),
            pltpu.VMEM((KS,) + TILE, F32),
            pltpu.VMEM((2, 16, BR), F32),
            pltpu.VMEM((2, 16, 1, BR), F32),
            pltpu.VMEM((2, 16, 1, BR), F32),
            pltpu.VMEM((2, 2, 1, BR), F32),
            pltpu.VMEM((KS, 2, 2) + TILE, F32),
            pltpu.VMEM((8, 2) + TILE, F32),
            pltpu.VMEM((KS, 2) + TILE, F32),
            pltpu.VMEM((8,) + TILE, F32),
            pltpu.VMEM((KS, 2) + TILE, F32),
            pltpu.VMEM((8,) + TILE, F32),
            DMA((6,)),
            DMA,
            DMA((2 * TPD, 8)),
            DMA((2 * TPD, 8)),
            DMA,
            DMA((TPD,)),
            DMA,
            DMA((2, 4)),
            DMA,
            DMA((3,)),
            DMA,
            DMA((3,)),
            DMA((3,)),
            DMA((2,)),
            DMA((2,)),
            DMA,
            DMA((3, 2)),
            DMA((3, 16)),
            DMA((3,)),
            DMA((2, 3)),
            DMA((2, 3)),
            DMA((3,)),
            DMA((3,)),
        ],
        compiler_params=pltpu.CompilerParams(
            collective_id=0, has_side_effects=True, vmem_limit_bytes=60 * 1024 * 1024
        ),
        cost_estimate=pl.CostEstimate(flops=600_000_000, bytes_accessed=2_000_000, transcendentals=0),
    )(start_vector, precond_diag, left_env, right_env, right_shift, sector_length)


def solution(mesh):
    placed = (
        P("sec", None),
        P("sec", None),
        P("mpo", "sec", None),
        P("mpo", "sec", None),
        P("mpo"),
        P("sec"),
    )
    return jax.shard_map(
        per_device,
        mesh=mesh,
        in_specs=placed,
        out_specs=(P("sec", "mpo"), P("sec", "mpo")),
        check_vma=False,
    )
```

```python
import jax
import jax.numpy as jnp
from jax import lax
from jax.experimental import pallas as pl
from jax.experimental.pallas import tpu as pltpu
from jax.sharding import PartitionSpec as P

MESH = pl.DeviceIdType.MESH
F32 = jnp.float32
BF16 = jnp.bfloat16

NZ = 16
ROWS, BR, NBLK = 8, 128, 64
TPD = 3
TERMS = 24
KS = 4
CELLS = float(512 * 8192)
EPS = 1e-6
TILE = (ROWS, BR)

G, B, E, H_, Q, A_, AA, PP, AP = range(9)
EARLY = [
    (G, G), (G, H_), (G, B), (G, A_), (B, B), (A_, B), (A_, A_), (A_, H_),
    (E, B), (E, A_), (AA, A_), (E, E), (E, AA), (AA, AA),
]
LATE = [(G, PP), (B, PP), (A_, PP), (E, PP), (AA, PP), (E, AP), (AA, AP), (AP, AP)]


def kernel(
    start_hbm,
    diag_hbm,
    left_hbm,
    right_hbm,
    shift_hbm,
    length_hbm,
    basis_ref,
    image_ref,
    start_ref,
    diag_ref,
    left_ref,
    shift_ref,
    length_ref,
    zbuf,
    rbuf,
    r_hi,
    r_lo,
    gd,
    v1,
    v2,
    v2b,
    v3,
    mixed,
    y_sum,
    piece,
    inv,
    left_all,
    shift_all,
    shift_sm,
    left_wide,
    mask,
    d_rows,
    dz,
    dp,
    qs_src,
    qs_got,
    t_src,
    t_got,
    o_src,
    o_got,
    in_sem,
    z_send,
    z_plus,
    z_minus,
    opp_send,
    opp_recv,
    r_send,
    r_recv,
    x_send,
    x_recv,
    x_core,
    l_send,
    l_recv,
    s_send,
    s_recv,
    sm_sem,
    ag_send,
    ag_recv,
    ag_core,
    dot_send,
    dot_recv,
    out_send,
    out_recv,
):
    sec = lax.axis_index("sec")
    mpo = lax.axis_index("mpo")
    z, x = lax.div(sec, 4), lax.rem(sec, 4)
    y, c = lax.div(mpo, 2), lax.rem(mpo, 2)
    here = 4 * y + x

    def dev(xx, yy, zz, cc):
        return (zz * 4 + xx, yy * 2 + cc)

    def send(src, dst, send_sem, recv_sem, where):
        pltpu.make_async_remote_copy(
            src_ref=src,
            dst_ref=dst,
            send_sem=send_sem,
            recv_sem=recv_sem,
            device_id=where,
            device_id_type=MESH,
        ).start()

    def wait(ref, sem):
        pltpu.make_async_copy(ref, ref, sem).wait()

    up = dev(x, y, lax.rem(z + 1, NZ), c)
    down = dev(x, y, lax.rem(z + NZ - 1, NZ), c)
    other = dev(x, y, z, 1 - c)
    zdevs = [dev(x, y, lax.rem(z + d, NZ), c) for d in range(1, NZ)]
    offsets = sorted(range(1, 16), key=lambda o: -(min(o // 4, 4 - o // 4) + min(o % 4, 4 - o % 4)))

    def peer(o, core=c):
        return dev(lax.rem(x + o // 4, 4), lax.rem(y + o % 4, 4), z, core)

    def sender(o):
        return 4 * lax.rem(y + 4 - o % 4, 4) + lax.rem(x + 4 - o // 4, 4)

    loads = [
        pltpu.make_async_copy(right_hbm, zbuf.at[z, pl.ds(0, TPD)], in_sem.at[0]),
        pltpu.make_async_copy(start_hbm, start_ref, in_sem.at[1]),
        pltpu.make_async_copy(diag_hbm, diag_ref, in_sem.at[2]),
        pltpu.make_async_copy(left_hbm, left_ref, in_sem.at[3]),
        pltpu.make_async_copy(shift_hbm, shift_ref, in_sem.at[4]),
        pltpu.make_async_copy(length_hbm, length_ref, in_sem.at[5]),
    ]
    for load in loads:
        load.start()
    barrier = pltpu.get_barrier_semaphore()
    ydevs = [dev(x, lax.rem(y + d, 4), z, c) for d in range(1, 4)]
    xdevs = [dev(lax.rem(x + d, 4), y, z, c) for d in range(1, 4)]
    partners = [up, down, other] + xdevs + ydevs
    partners += [dev(x, lax.rem(y + d, 4), z, 1 - c) for d in range(1, 4)]
    for p in partners:
        pl.semaphore_signal(barrier, inc=1, device_id=p, device_id_type=MESH)

    sub = lax.broadcasted_iota(jnp.int32, TILE, 0)
    for load in loads[3:]:
        load.wait()
    left_all[c, here] = jnp.zeros(TILE, F32)
    for t in range(TPD):
        left_all[c, here, :, t * ROWS : (t + 1) * ROWS] = left_ref[t]
    left_all[c, here, :, TPD * ROWS : TPD * ROWS + 1] = jnp.full((ROWS, 1), length_ref[0].astype(F32), F32)
    shift_all[c, y] = jnp.where(sub == 0, shift_ref[0], jnp.where(sub == 1, shift_ref[1], shift_ref[2]))
    live0 = jnp.where(sub < length_ref[0], 1.0, 0.0).astype(F32)
    for load in loads[1:3]:
        load.wait()
    for m in range(NBLK):
        gd[x, m % 16, m // 16, 0] = start_ref[:, m * BR : (m + 1) * BR] * live0
        gd[x, m % 16, m // 16, 1] = diag_ref[:, m * BR : (m + 1) * BR]
    loads[0].wait()
    pl.semaphore_wait(barrier, len(partners))

    kind = lax.rem(z - y + 4, 4)

    def is_kind(i, which):
        return lax.rem(kind + i + NZ, 4) == which

    def deliver(zz, u):
        nn = lax.rem(lax.div(zz, 4), 2)
        yd, cd = lax.rem(zz, 4), lax.div(zz, 8)
        if u < TPD:
            dst, sem = rbuf.at[nn, y, c, u], r_recv.at[nn, lax.rem(yd - y + 4, 4)]
        else:
            dst, sem = rbuf.at[nn, lax.rem(y + 2, 4), c, u - TPD], r_recv.at[nn, 2]
        stays = jnp.logical_and(yd == y, cd == c)

        @pl.when(stays)
        def _():
            pltpu.make_async_copy(zbuf.at[zz, u], dst, sem).start()

        @pl.when(jnp.logical_not(stays))
        def _():
            send(zbuf.at[zz, u], dst, r_send, sem, dev(x, yd, z, cd))

    def first_sends(u):
        send(zbuf.at[z, u], zbuf.at[z, u], z_send, z_plus.at[u, 0], up)
        send(zbuf.at[z, u], zbuf.at[z, u], z_send, z_minus.at[u, 0], down)

    @pl.when(is_kind(0, 2))
    def _():
        for t in range(TPD):
            send(zbuf.at[z, t], zbuf.at[z, TPD + t], opp_send, opp_recv.at[t], dev(x, lax.rem(y + 2, 4), z, c))

    @pl.when(jnp.logical_not(is_kind(0, 2)))
    def _():
        for t in range(TPD):
            first_sends(t)
            deliver(z, t)

    def half(k, cc):
        return gd.at[k, :, pl.ds(2 * cc, 2)]

    def send_rows(i):
        rows = gd.at[x, pl.ds(2 * i, 2), pl.ds(2 * c, 2)]
        for d in (2, 1, 3):
            send(rows, rows, x_send, x_recv.at[d - 1], dev(lax.rem(x + d, 4), y, z, c))

    for d in range(3):
        send(shift_all.at[c, y], shift_all.at[c, y], s_send.at[0], s_recv.at[0], ydevs[d])
        send(left_all.at[c, here], left_all.at[c, here], l_send.at[0], l_recv.at[0], xdevs[d])

    def send_opposite():
        @pl.when(is_kind(0, 0))
        def _():
            for u in range(TPD, 2 * TPD):
                wait(zbuf.at[z, u], opp_recv.at[u - TPD])
                first_sends(u)
                deliver(z, u)

    def ring_step(i, u):
        zp, zm = lax.rem(z + NZ - i, NZ), lax.rem(z + i, NZ)
        top, low = pl.ds(0, BR // 2), pl.ds(BR // 2, BR // 2)

        def has(j):
            return is_kind(j, 0) if u >= TPD else jnp.logical_not(is_kind(j, 2))

        if i < 8:

            @pl.when(has(-i))
            def _():
                wait(zbuf.at[zp, u], z_plus.at[u, i - 1])
                block = zbuf.at[zp, u] if i < 7 else zbuf.at[zp, u, top]
                send(block, block, z_send, z_plus.at[u, i], up)

            @pl.when(has(i))
            def _():
                wait(zbuf.at[zm, u], z_minus.at[u, i - 1])
                block = zbuf.at[zm, u] if i < 7 else zbuf.at[zm, u, low]
                send(block, block, z_send, z_minus.at[u, i], down)
                deliver(zm, u)

            @pl.when(has(-i))
            def _():
                deliver(zp, u)

        else:

            @pl.when(has(0))
            def _():
                wait(zbuf.at[zp, u, top], z_plus.at[u, 7])
                wait(zbuf.at[zp, u, low], z_minus.at[u, 7])
                deliver(zp, u)

    def pass_rows(d):
        k = lax.rem(x + 4 - d, 4)
        wait(half(k, c), x_recv.at[d - 1])
        send(half(k, c), half(k, c), x_send, x_core, other)

    def pass_left():
        wait(left_all.at[c, pl.ds(0, 3)], l_recv.at[0])
        row = left_all.at[c, pl.ds(4 * y, 4)]
        for d in range(3):
            send(row, row, l_send.at[1], l_recv.at[1], ydevs[d])

    def pass_small():
        wait(shift_all.at[c, pl.ds(0, 3)], s_recv.at[0])
        send(shift_all.at[c], shift_all.at[c], s_send.at[1], s_recv.at[1], other)
        wait(left_all.at[c, pl.ds(0, 12)], l_recv.at[1])
        send(left_all.at[c], left_all.at[c], l_send.at[2], l_recv.at[2], other)

    to_sm = pltpu.make_async_copy(shift_all, shift_sm, sm_sem)

    def take_small():
        wait(shift_all.at[1 - c], s_recv.at[1])
        to_sm.start()
        wait(left_all.at[1 - c], l_recv.at[2])
        for k in range(KS):
            length = jnp.broadcast_to(left_all[c, 4 * y + k][:, TPD * ROWS : TPD * ROWS + 1], TILE)
            mask[k] = jnp.where(sub.astype(F32) < length, 1.0, 0.0).astype(F32)

    def widen(first, count):
        def body(i, carry):
            cc, r = lax.div(i, 16), lax.rem(i, 16)
            yy, k = lax.div(r, 4), lax.rem(r, 4)
            tile = left_all[cc, r]
            for t in range(TPD):
                for j in range(ROWS):
                    lane = t * ROWS + j
                    left_wide[(yy * 2 + cc) * TPD + t, k, j] = jnp.broadcast_to(tile[:, lane : lane + 1], TILE)
            return carry

        lax.fori_loop(first, first + count, body, 0)

    def take_rows():
        wait(gd.at[pl.ds(0, 3), :, pl.ds(0, 2)], x_core)

    def vectors(first, count):
        def body(r, carry):
            for k in range(KS):
                for j in range(4):
                    g = gd[k, r, j, 0]
                    a = 1.0 / gd[k, r, j, 1]
                    b = g * a
                    v1[k, r, j] = g
                    v1[KS + k, r, j] = b
                    v1[2 * KS + k, r, j] = b * a
            return carry

        lax.fori_loop(first, first + count, body, 0)

    def mix(v, nk, first, count, step):
        rows = nk * ROWS

        def body(at, carry):
            for u in range(step):
                i = first + at * step + u
                yy, rest = lax.div(i, 2 * TPD), lax.rem(i, 2 * TPD)
                shift = shift_sm[lax.div(rest, TPD), yy, lax.rem(rest, TPD), 0]
                for nn in range(2):
                    m = 16 * (2 * c + nn) + here + shift
                    m = jnp.where(m >= NBLK, m - NBLK, m)
                    r, j4 = lax.rem(m, 16), lax.div(m, 16)
                    tiles = []
                    for k in range(nk):
                        src = v[k, r, j4]
                        total = None
                        for j in range(ROWS):
                            term = left_wide[i, k % KS, j] * src[j : j + 1, :]
                            total = term if total is None else total + term
                        tiles.append(total)
                    p = jnp.concatenate(tiles, axis=0)
                    hi = p.astype(BF16)
                    mixed[i, nn, 0:rows] = hi
                    mixed[i, nn, rows : 2 * rows] = (p - hi.astype(F32)).astype(BF16)
            return carry

        lax.fori_loop(0, count // step, body, 0)

    def terms_of(nn, yy, rows, cut):
        acc = None
        for q in range(2 * TPD):
            cc, t = q // TPD, q % TPD
            if cut:
                full = rbuf[nn, yy, cc, t]
                rh = full.astype(BF16)
                rl = (full - rh.astype(F32)).astype(BF16)
                r_hi[nn, yy, cc, t] = rh
                r_lo[nn, yy, cc, t] = rl
            else:
                rh = r_hi[nn, yy, cc, t]
                rl = r_lo[nn, yy, cc, t]
            i = yy * 2 * TPD + q
            both = jnp.dot(mixed[i, nn, 0 : 2 * rows], rh, preferred_element_type=F32)
            more = jnp.dot(mixed[i, nn, 0:rows], rl, preferred_element_type=F32)
            res = both[:rows] + both[rows:] + more
            acc = res if acc is None else acc + res
        return acc

    def product(v, nk):
        mix(v, nk, 0, TERMS, 4)
        for nn in range(2):
            acc = terms_of(nn, 0, nk * ROWS, False)
            for yy in range(1, 4):
                acc = acc + terms_of(nn, yy, nk * ROWS, False)
            y_sum[nn, pl.ds(0, nk)] = acc.reshape((nk,) + TILE)

    tasks = {i: [lambda i=i: send_rows(i)] for i in range(8)}
    tasks[2].append(pass_left)
    tasks[4].append(pass_small)
    tasks[6].append(take_small)
    for i in range(4):
        tasks.setdefault(i + 7, []).append(lambda i=i: widen(8 * i, 8))
    tasks[11] = [lambda: pass_rows(1)]
    tasks[12] = [lambda: pass_rows(3)]
    tasks[13] = [lambda: pass_rows(2)]
    tasks[14] = [take_rows, lambda: vectors(0, 4)]
    for i in range(15, 18):
        tasks[i] = [lambda i=i: vectors(4 * i - 56, 4)]
    tasks[17].append(to_sm.wait)
    for i in range(18, 24):
        tasks[i] = [lambda i=i: mix(v1, 3 * KS, 4 * i - 72, 4, 1)]
    for i in range(1, 9):
        for t in range(TPD):
            ring_step(i, t)
            for task in tasks.get((i - 1) * TPD + t, []):
                task()
        for t in range(TPD):
            if i == 1:
                continue
            ring_step(i - 1, TPD + t)
        if i == 1:
            send_opposite()
    for t in range(TPD):
        ring_step(8, TPD + t)

    for nn in range(2):
        for k in range(KS):
            j = 2 * c + nn
            inv[k, nn] = 1.0 / gd[k, here, j, 1]
            piece[G, k, nn] = v1[k, here, j]
            piece[B, k, nn] = v1[KS + k, here, j]
            piece[E, k, nn] = v1[2 * KS + k, here, j]

    def gather(phase, v):
        def at(r, cc):
            return v.at[:, r, pl.ds(2 * cc, 2)]

        def start(nn=None):
            own = at(here, c) if nn is None else v.at[:, here, pl.ds(2 * c + nn, 1)]
            for o in offsets:
                send(own, own, ag_send.at[phase, 0], ag_recv.at[phase, o], peer(o))
            send(own, own, ag_send.at[phase, 1], ag_core.at[phase], other)

        def pass_on(first, last):
            for o in offsets[::-1][first:last]:
                r = sender(o)
                wait(at(r, c), ag_recv.at[phase, o])
                send(at(r, c), at(r, c), ag_send.at[phase, 1], ag_core.at[phase], other)

        def finish():
            wait(v.at[:, :, pl.ds(0, 2)], ag_core.at[phase])

        def sent():
            wait(v.at[:, pl.ds(0, 15), pl.ds(0, 2)], ag_send.at[phase, 0])
            wait(v.at[:, :, pl.ds(0, 2)], ag_send.at[phase, 1])

        return start, pass_on, finish, sent

    def dots(g):
        def start(pairs):
            d_rows[g] = jnp.zeros((16, BR), F32)
            for r, (a, b) in enumerate(pairs):
                prod = (piece[a] * piece[b]).reshape((2 * KS,) + TILE)
                d_rows[g, r : r + 1, :] = jnp.sum(jnp.sum(prod, axis=0), axis=0, keepdims=True)
            total = jnp.broadcast_to(jnp.sum(d_rows[g], axis=1, keepdims=True), (16, BR))
            at_row = lax.broadcasted_iota(jnp.int32, (16, BR), 0) == lax.broadcasted_iota(jnp.int32, (16, BR), 1)
            dz[g, z] = jnp.sum(jnp.where(at_row, total, 0.0), axis=0, keepdims=True)
            for p in zdevs:
                send(dz.at[g, z], dz.at[g, z], dot_send.at[g, 0], dot_recv.at[g, 0], p)

        def plane():
            wait(dz.at[g, pl.ds(0, 15)], dot_recv.at[g, 0])
            own = dp.at[g, 16 * c + here]
            dp[g, 16 * c + here] = jnp.sum(dz[g], axis=0)
            for o in offsets:
                send(own, own, dot_send.at[g, 1], dot_recv.at[g, 1], peer(o))
                send(own, own, dot_send.at[g, 1], dot_recv.at[g, 1], peer(o, 1 - c))
            send(own, own, dot_send.at[g, 1], dot_recv.at[g, 1], other)

        def done(pairs):
            wait(dp.at[g, pl.ds(0, 31)], dot_recv.at[g, 1])
            total = jnp.sum(dp[g], axis=0)
            return {p: jnp.broadcast_to(total[:, r : r + 1], TILE) for r, p in enumerate(pairs)}

        def sent():
            wait(dz.at[g, pl.ds(0, 15)], dot_send.at[g, 0])
            wait(dp.at[g, pl.ds(0, 31)], dot_send.at[g, 1])

        return start, plane, done, sent

    spot = 4 * lax.rem(y, 2) + x
    cd = lax.div(y, 2)
    keeps = cd == c

    def exchange(i, src, got):
        def start():
            for k in range(KS):
                for nn in range(2):
                    stays = jnp.logical_and(jnp.logical_and(x == k, y == 2 * c + nn), keeps)

                    @pl.when(stays)
                    def _():
                        got[spot] = src[k, nn]

                    @pl.when(jnp.logical_not(stays))
                    def _():
                        where = dev(k, 2 * c + nn, z, cd)
                        send(src.at[k, nn], got.at[spot], out_send.at[i], out_recv.at[i], where)

        def arrived(sem):
            @pl.when(keeps)
            def _():
                wait(got.at[pl.ds(0, 7)], sem.at[i])

            @pl.when(jnp.logical_not(keeps))
            def _():
                wait(got, sem.at[i])

        return start, lambda: arrived(out_recv), lambda: arrived(out_send)

    ex_early, ex_t, ex_o = exchange(0, qs_src, qs_got), exchange(1, t_src, t_got), exchange(2, o_src, o_got)
    ag2, ag2b, ag3 = gather(0, v2), gather(1, v2b), gather(2, v3)
    early, late = dots(0), dots(1)

    apart = lax.rem(y + 8 * c - z + NZ, NZ)
    near = 1 - lax.div(lax.rem(apart + 9, NZ) + 9, NZ)
    for nn in (near, 1 - near):
        acc = None
        for d in (0, 1, 3, 2):
            yy = lax.rem(y - d + 4, 4)
            wait(rbuf.at[nn, yy], r_recv.at[nn, d])
            part = terms_of(nn, yy, 3 * KS * ROWS, True)
            acc = part if acc is None else acc + part
        acc = acc.reshape((3 * KS,) + TILE)
        for k in range(KS):
            h = acc[k] * mask[k]
            a = h * inv[k, nn]
            piece[H_, k, nn] = h
            piece[A_, k, nn] = a
            v2[k, here, 2 * c + nn] = a
            piece[AA, k, nn] = a * inv[k, nn]
            v2b[k, here, 2 * c + nn] = a * inv[k, nn]
            q = acc[KS + k] * mask[k]
            piece[Q, k, nn] = q
            qs_src[k, nn, 0] = q
            qs_src[k, nn, 1] = acc[2 * KS + k] * mask[k]
        ag2[0](nn)
    early[0](EARLY)
    ag2[1](0, 10)
    early[1]()
    ag2b[0]()
    ex_early[0]()
    ag2[1](10, 15)
    ag2[2]()

    product(v2, KS)
    dot = early[2](EARLY)
    f1 = jnp.sqrt(CELLS / (dot[G, G] + EPS))
    r1 = f1 * f1 * dot[G, H_] / CELLS
    for nn in range(2):
        for k in range(KS):
            pp = y_sum[nn, k] * mask[k] - r1 * piece[Q, k, nn]
            piece[PP, k, nn] = pp
            piece[AP, k, nn] = pp * inv[k, nn]
            v3[k, here, 2 * c + nn] = pp * inv[k, nn]
    ag3[0]()
    late[0](LATE)
    ag2b[1](0, 15)
    ag2b[2]()
    product(v2b, KS)
    for nn in range(2):
        for k in range(KS):
            t_src[k, nn] = y_sum[nn, k] * mask[k]
    ex_t[0]()
    ag3[1](0, 10)
    late[1]()
    ag3[1](10, 15)
    ag3[2]()

    product(v3, KS)
    for nn in range(2):
        for k in range(KS):
            o_src[k, nn] = y_sum[nn, k] * mask[k]
    ex_o[0]()
    dot.update(late[2](LATE))
    dot.update({(b, a): value for (a, b), value in dot.items()})

    c1 = f1 * f1 * (dot[G, A_] - r1 * dot[G, B]) / CELLS
    w = (-f1 * c1, -f1 * r1, f1)
    wy = (w[0], f1)
    x_x = [[dot[i, j] for j in (G, B, A_)] for i in (G, B, A_)]
    x_y = [[dot[G, H_], dot[G, PP]], [dot[G, A_], dot[B, PP]], [dot[A_, H_], dot[A_, PP]]]
    ax_y = [[dot[G, A_], dot[B, PP]], [dot[A_, B], dot[E, PP]], [dot[A_, A_], dot[AA, PP]]]
    ax_x = [
        [dot[G, B], dot[B, B], dot[A_, B]],
        [dot[B, B], dot[E, B], dot[E, A_]],
        [dot[A_, B], dot[E, A_], dot[AA, A_]],
    ]

    def along(weights, row):
        total = weights[0] * row[0]
        for weight, value in zip(weights[1:], row[1:], strict=True):
            total = total + weight * value
        return total

    def form(weights, m):
        return along(w, [along(weights, row) for row in m])

    def column(m, j):
        return [row[j] for row in m]

    uu, uk, uak, uau = form(w, x_x), form(wy, x_y), form(wy, ax_y), form(w, ax_x)
    gu, gk, uh = along(w, x_x[0]), along(wy, x_y[0]), along(w, column(x_y, 0))
    gak, gau, uah = along(wy, x_y[1]), along(w, x_x[1]), along(w, column(x_x, 2))
    f2 = jnp.sqrt(CELLS / (jnp.maximum(uu, 0.0) + EPS))
    b_ = f1 * f2 * (gk + uh) / (2.0 * CELLS)
    d_ = f2 * f2 * uk / CELLS
    h_ = (r1 - d_) / 2.0
    ritz = (r1 + d_) / 2.0 - jnp.sqrt(h_ * h_ + b_ * b_)
    big = jnp.maximum(jnp.abs(h_), jnp.abs(b_))
    safe = jnp.where(big > 0.0, big, 1.0)
    hs = jnp.where(big > 0.0, h_ / safe, 1.0)
    bs = b_ / safe
    rs = jnp.sqrt(hs * hs + bs * bs)
    larger = jnp.sqrt((rs + jnp.abs(hs)) / (2.0 * rs))
    smaller = jnp.abs(bs) / (2.0 * rs * larger)
    co = jnp.where(hs >= 0.0, larger, smaller)
    si = jnp.where(bs < 0.0, -1.0, 1.0) * jnp.where(hs >= 0.0, smaller, larger)
    n1, n2 = -si * f1, co * f2
    e1 = f1 * (n1 * (dot[G, A_] - ritz * dot[G, B]) + n2 * (gak - ritz * gau)) / CELLS
    e2 = f2 * (n1 * (uah - ritz * gau) + n2 * (uak - ritz * uau)) / CELLS
    t2 = {
        A_: n1 + n2 * w[0],
        B: -ritz * (n1 + n2 * w[0]),
        E: -ritz * n2 * w[1],
        AA: -ritz * n2 * w[2],
        AP: n2 * f1,
    }
    dot[A_, AP], dot[B, AP], dot[B, AA] = dot[AA, PP], dot[E, PP], dot[E, A_]
    dot.update({(b, a): value for (a, b), value in dot.items()})
    tt = jnp.zeros(TILE, F32)
    for i in t2:
        row = jnp.zeros(TILE, F32)
        for j in t2:
            row = row + t2[j] * dot[i, j]
        tt = tt + t2[i] * row
    square = tt - 2.0 * CELLS * (e1 * e1 + e2 * e2)
    square = square + e1 * e1 * f1 * f1 * dot[G, G] + e2 * e2 * f2 * f2 * uu + 2.0 * e1 * e2 * f1 * f2 * gu
    f3 = jnp.sqrt(CELLS / (jnp.maximum(square, 0.0) + EPS))
    coef = dict(t2)
    coef[G] = -e1 * f1 - e2 * f2 * w[0]
    coef[B] = coef[B] - e2 * f2 * w[1]
    coef[A_] = coef[A_] - e2 * f2 * w[2]
    coef = {i: f3 * value for i, value in coef.items()}
    coef_q = coef[B] + coef[A_] * r1
    for ex in (ex_early, ex_t, ex_o):
        ex[1]()
    for i in range(8):
        r = 8 * c + i
        a, ap, d = v2[x, r, y], v3[x, r, y], gd[x, r, y, 1]
        basis = coef[AP] * ap + coef[A_] * a + coef[AA] * v2b[x, r, y]
        basis = basis + coef[G] * v1[x, r, y] + coef[B] * v1[KS + x, r, y] + coef[E] * v1[2 * KS + x, r, y]
        image = coef[AP] * o_got[i] + (coef[A_] * ap + coef[G] * a) * d
        image = image + coef_q * qs_got[i, 0] + coef[E] * qs_got[i, 1] + coef[AA] * t_got[i]
        basis_ref[:, i * BR : (i + 1) * BR] = basis
        image_ref[:, i * BR : (i + 1) * BR] = image

    wait(zbuf.at[pl.ds(0, 15), pl.ds(0, TPD)], z_send)
    wait(zbuf.at[pl.ds(0, 12), pl.ds(0, TPD)], r_send)

    @pl.when(is_kind(0, 2))
    def _():
        wait(zbuf.at[0, pl.ds(0, TPD)], opp_send)

    wait(gd.at[pl.ds(0, 3)], x_send)
    wait(left_all.at[c, pl.ds(0, 3)], l_send.at[0])
    wait(left_all.at[c, pl.ds(0, 12)], l_send.at[1])
    wait(left_all.at[c], l_send.at[2])
    wait(shift_all.at[c, pl.ds(0, 3)], s_send.at[0])
    wait(shift_all.at[c], s_send.at[1])
    for ag in (ag2, ag2b, ag3):
        ag[3]()
    early[3]()
    late[3]()
    for ex in (ex_early, ex_t, ex_o):
        ex[2]()


def per_device(start_vector, precond_diag, left_env, right_env, right_shift, sector_length):
    vmem = pl.BlockSpec(memory_space=pltpu.VMEM)
    hbm = pl.BlockSpec(memory_space=pltpu.HBM)
    DMA = pltpu.SemaphoreType.DMA
    return pl.pallas_call(
        kernel,
        out_shape=[jax.ShapeDtypeStruct((ROWS, 1024), F32)] * 2,
        in_specs=[hbm] * 6,
        out_specs=[vmem, vmem],
        scratch_shapes=[
            pltpu.VMEM((ROWS, NBLK * BR), F32),
            pltpu.VMEM((ROWS, NBLK * BR), F32),
            pltpu.VMEM((TPD, ROWS, ROWS), F32),
            pltpu.SMEM((TPD,), jnp.int32),
            pltpu.SMEM((1,), jnp.int32),
            pltpu.VMEM((NZ, 2 * TPD, BR, BR), F32),
            pltpu.VMEM((2, 4, 2, TPD, BR, BR), F32),
            pltpu.VMEM((2, 4, 2, TPD, BR, BR), BF16),
            pltpu.VMEM((2, 4, 2, TPD, BR, BR), BF16),
            pltpu.VMEM((KS, 16, 4, 2) + TILE, F32),
            pltpu.VMEM((3 * KS, 16, 4) + TILE, F32),
            pltpu.VMEM((KS, 16, 4) + TILE, F32),
            pltpu.VMEM((KS, 16, 4) + TILE, F32),
            pltpu.VMEM((KS, 16, 4) + TILE, F32),
            pltpu.VMEM((TERMS, 2, 6 * KS * ROWS, BR), BF16),
            pltpu.VMEM((2, 3 * KS) + TILE, F32),
            pltpu.VMEM((9, KS, 2) + TILE, F32),
            pltpu.VMEM((KS, 2) + TILE, F32),
            pltpu.VMEM((2, 16) + TILE, F32),
            pltpu.VMEM((2, 4) + TILE, jnp.int32),
            pltpu.SMEM((2, 4) + TILE, jnp.int32),
            pltpu.VMEM((TERMS, KS, ROWS) + TILE, F32),
            pltpu.VMEM((KS,) + TILE, F32),
            pltpu.VMEM((2, 16, BR), F32),
            pltpu.VMEM((2, 16, 1, BR), F32),
            pltpu.VMEM((2, 32, 1, BR), F32),
            pltpu.VMEM((KS, 2, 2) + TILE, F32),
            pltpu.VMEM((8, 2) + TILE, F32),
            pltpu.VMEM((KS, 2) + TILE, F32),
            pltpu.VMEM((8,) + TILE, F32),
            pltpu.VMEM((KS, 2) + TILE, F32),
            pltpu.VMEM((8,) + TILE, F32),
            DMA((6,)),
            DMA,
            DMA((2 * TPD, 8)),
            DMA((2 * TPD, 8)),
            DMA,
            DMA((TPD,)),
            DMA,
            DMA((2, 4)),
            DMA,
            DMA((3,)),
            DMA,
            DMA((3,)),
            DMA((3,)),
            DMA((2,)),
            DMA((2,)),
            DMA,
            DMA((3, 2)),
            DMA((3, 16)),
            DMA((3,)),
            DMA((2, 2)),
            DMA((2, 2)),
            DMA((3,)),
            DMA((3,)),
        ],
        compiler_params=pltpu.CompilerParams(
            collective_id=0, has_side_effects=True, vmem_limit_bytes=60 * 1024 * 1024
        ),
        cost_estimate=pl.CostEstimate(flops=600_000_000, bytes_accessed=2_000_000, transcendentals=0),
    )(start_vector, precond_diag, left_env, right_env, right_shift, sector_length)


def solution(mesh):
    placed = (
        P("sec", None),
        P("sec", None),
        P("mpo", "sec", None),
        P("mpo", "sec", None),
        P("mpo"),
        P("sec"),
    )
    return jax.shard_map(
        per_device,
        mesh=mesh,
        in_specs=placed,
        out_specs=(P("sec", "mpo"), P("sec", "mpo")),
        check_vma=False,
    )
```

```python
import jax
import jax.numpy as jnp
from jax import lax
from jax.experimental import pallas as pl
from jax.experimental.pallas import tpu as pltpu
from jax.sharding import PartitionSpec as P

MESH = pl.DeviceIdType.MESH
F32 = jnp.float32
BF16 = jnp.bfloat16

NZ = 16
ROWS, BR, NBLK = 8, 128, 64
TPD = 3
TERMS = 24
KS = 4
CELLS = float(512 * 8192)
EPS = 1e-6
TILE = (ROWS, BR)

G, B, E, H_, Q, A_, AA, PP, AP = range(9)
EARLY = [
    (G, G), (G, H_), (G, B), (G, A_), (B, B), (A_, B), (A_, A_), (A_, H_),
    (E, B), (E, A_), (AA, A_), (E, E), (E, AA), (AA, AA),
]
LATE = [(G, PP), (B, PP), (A_, PP), (E, PP), (AA, PP), (E, AP), (AA, AP), (AP, AP)]


def kernel(
    start_hbm,
    diag_hbm,
    left_hbm,
    right_hbm,
    shift_hbm,
    length_hbm,
    basis_ref,
    image_ref,
    start_ref,
    diag_ref,
    left_ref,
    shift_ref,
    length_ref,
    zbuf,
    rbuf,
    r_hi,
    r_lo,
    gd,
    v1,
    v2,
    v2b,
    v3,
    mixed,
    y_sum,
    piece,
    inv,
    left_all,
    shift_all,
    shift_sm,
    left_wide,
    mask,
    d_rows,
    dz,
    dp,
    qs_src,
    qs_got,
    t_src,
    t_got,
    o_src,
    o_got,
    in_sem,
    z_send,
    z_plus,
    z_minus,
    opp_send,
    opp_recv,
    r_send,
    r_recv,
    x_send,
    x_recv,
    x_core,
    l_send,
    l_recv,
    s_send,
    s_recv,
    sm_sem,
    ag_send,
    ag_recv,
    ag_core,
    dot_send,
    dot_recv,
    out_send,
    out_recv,
):
    sec = lax.axis_index("sec")
    mpo = lax.axis_index("mpo")
    z, x = lax.div(sec, 4), lax.rem(sec, 4)
    y, c = lax.div(mpo, 2), lax.rem(mpo, 2)
    here = 4 * y + x

    def dev(xx, yy, zz, cc):
        return (zz * 4 + xx, yy * 2 + cc)

    def send(src, dst, send_sem, recv_sem, where):
        pltpu.make_async_remote_copy(
            src_ref=src,
            dst_ref=dst,
            send_sem=send_sem,
            recv_sem=recv_sem,
            device_id=where,
            device_id_type=MESH,
        ).start()

    def wait(ref, sem):
        pltpu.make_async_copy(ref, ref, sem).wait()

    up = dev(x, y, lax.rem(z + 1, NZ), c)
    down = dev(x, y, lax.rem(z + NZ - 1, NZ), c)
    other = dev(x, y, z, 1 - c)
    zdevs = [dev(x, y, lax.rem(z + d, NZ), c) for d in range(1, NZ)]
    offsets = sorted(range(1, 16), key=lambda o: -(min(o // 4, 4 - o // 4) + min(o % 4, 4 - o % 4)))

    def peer(o, core=c):
        return dev(lax.rem(x + o // 4, 4), lax.rem(y + o % 4, 4), z, core)

    def sender(o):
        return 4 * lax.rem(y + 4 - o % 4, 4) + lax.rem(x + 4 - o // 4, 4)

    loads = [
        pltpu.make_async_copy(right_hbm, zbuf.at[z, pl.ds(0, TPD)], in_sem.at[0]),
        pltpu.make_async_copy(start_hbm, start_ref, in_sem.at[1]),
        pltpu.make_async_copy(diag_hbm, diag_ref, in_sem.at[2]),
        pltpu.make_async_copy(left_hbm, left_ref, in_sem.at[3]),
        pltpu.make_async_copy(shift_hbm, shift_ref, in_sem.at[4]),
        pltpu.make_async_copy(length_hbm, length_ref, in_sem.at[5]),
    ]
    for load in loads:
        load.start()
    barrier = pltpu.get_barrier_semaphore()
    ydevs = [dev(x, lax.rem(y + d, 4), z, c) for d in range(1, 4)]
    xdevs = [dev(lax.rem(x + d, 4), y, z, c) for d in range(1, 4)]
    partners = [up, down, other] + xdevs + ydevs
    partners += [dev(x, lax.rem(y + d, 4), z, 1 - c) for d in range(1, 4)]
    for p in partners:
        pl.semaphore_signal(barrier, inc=1, device_id=p, device_id_type=MESH)

    sub = lax.broadcasted_iota(jnp.int32, TILE, 0)
    for load in loads[3:]:
        load.wait()
    left_all[c, here] = jnp.zeros(TILE, F32)
    for t in range(TPD):
        left_all[c, here, :, t * ROWS : (t + 1) * ROWS] = left_ref[t]
    left_all[c, here, :, TPD * ROWS : TPD * ROWS + 1] = jnp.full((ROWS, 1), length_ref[0].astype(F32), F32)
    shift_all[c, y] = jnp.where(sub == 0, shift_ref[0], jnp.where(sub == 1, shift_ref[1], shift_ref[2]))
    live0 = jnp.where(sub < length_ref[0], 1.0, 0.0).astype(F32)
    for load in loads[1:3]:
        load.wait()
    for m in range(NBLK):
        gd[x, m % 16, m // 16, 0] = start_ref[:, m * BR : (m + 1) * BR] * live0
        gd[x, m % 16, m // 16, 1] = diag_ref[:, m * BR : (m + 1) * BR]
    loads[0].wait()
    pl.semaphore_wait(barrier, len(partners))

    kind = lax.rem(z - y + 4, 4)

    def is_kind(i, which):
        return lax.rem(kind + i + NZ, 4) == which

    def deliver(zz, u):
        nn = lax.rem(lax.div(zz, 4), 2)
        yd, cd = lax.rem(zz, 4), lax.div(zz, 8)
        if u < TPD:
            dst, sem = rbuf.at[nn, y, c, u], r_recv.at[nn, lax.rem(yd - y + 4, 4)]
        else:
            dst, sem = rbuf.at[nn, lax.rem(y + 2, 4), c, u - TPD], r_recv.at[nn, 2]
        stays = jnp.logical_and(yd == y, cd == c)

        @pl.when(stays)
        def _():
            pltpu.make_async_copy(zbuf.at[zz, u], dst, sem).start()

        @pl.when(jnp.logical_not(stays))
        def _():
            send(zbuf.at[zz, u], dst, r_send, sem, dev(x, yd, z, cd))

    def first_sends(u):
        send(zbuf.at[z, u], zbuf.at[z, u], z_send, z_plus.at[u, 0], up)
        send(zbuf.at[z, u], zbuf.at[z, u], z_send, z_minus.at[u, 0], down)

    @pl.when(is_kind(0, 2))
    def _():
        for t in range(TPD):
            send(zbuf.at[z, t], zbuf.at[z, TPD + t], opp_send, opp_recv.at[t], dev(x, lax.rem(y + 2, 4), z, c))

    @pl.when(jnp.logical_not(is_kind(0, 2)))
    def _():
        for t in range(TPD):
            first_sends(t)
            deliver(z, t)

    def half(k, cc):
        return gd.at[k, :, pl.ds(2 * cc, 2)]

    def send_rows(i):
        rows = gd.at[x, pl.ds(2 * i, 2), pl.ds(2 * c, 2)]
        for d in (2, 1, 3):
            send(rows, rows, x_send, x_recv.at[d - 1], dev(lax.rem(x + d, 4), y, z, c))

    for d in range(3):
        send(shift_all.at[c, y], shift_all.at[c, y], s_send.at[0], s_recv.at[0], ydevs[d])
        send(left_all.at[c, here], left_all.at[c, here], l_send.at[0], l_recv.at[0], xdevs[d])

    def send_opposite():
        @pl.when(is_kind(0, 0))
        def _():
            for u in range(TPD, 2 * TPD):
                wait(zbuf.at[z, u], opp_recv.at[u - TPD])
                first_sends(u)
                deliver(z, u)

    def ring_step(i, u):
        zp, zm = lax.rem(z + NZ - i, NZ), lax.rem(z + i, NZ)
        top, low = pl.ds(0, BR // 2), pl.ds(BR // 2, BR // 2)

        def has(j):
            return is_kind(j, 0) if u >= TPD else jnp.logical_not(is_kind(j, 2))

        if i < 8:

            @pl.when(has(-i))
            def _():
                wait(zbuf.at[zp, u], z_plus.at[u, i - 1])
                block = zbuf.at[zp, u] if i < 7 else zbuf.at[zp, u, top]
                send(block, block, z_send, z_plus.at[u, i], up)

            @pl.when(has(i))
            def _():
                wait(zbuf.at[zm, u], z_minus.at[u, i - 1])
                block = zbuf.at[zm, u] if i < 7 else zbuf.at[zm, u, low]
                send(block, block, z_send, z_minus.at[u, i], down)
                deliver(zm, u)

            @pl.when(has(-i))
            def _():
                deliver(zp, u)

        else:

            @pl.when(has(0))
            def _():
                wait(zbuf.at[zp, u, top], z_plus.at[u, 7])
                wait(zbuf.at[zp, u, low], z_minus.at[u, 7])
                deliver(zp, u)

    def pass_rows(d):
        k = lax.rem(x + 4 - d, 4)
        wait(half(k, c), x_recv.at[d - 1])
        send(half(k, c), half(k, c), x_send, x_core, other)

    def pass_left():
        wait(left_all.at[c, pl.ds(0, 3)], l_recv.at[0])
        row = left_all.at[c, pl.ds(4 * y, 4)]
        for d in range(3):
            send(row, row, l_send.at[1], l_recv.at[1], ydevs[d])

    def pass_small():
        wait(shift_all.at[c, pl.ds(0, 3)], s_recv.at[0])
        send(shift_all.at[c], shift_all.at[c], s_send.at[1], s_recv.at[1], other)
        wait(left_all.at[c, pl.ds(0, 12)], l_recv.at[1])
        send(left_all.at[c], left_all.at[c], l_send.at[2], l_recv.at[2], other)

    to_sm = pltpu.make_async_copy(shift_all, shift_sm, sm_sem)

    def take_small():
        wait(shift_all.at[1 - c], s_recv.at[1])
        to_sm.start()
        wait(left_all.at[1 - c], l_recv.at[2])
        for k in range(KS):
            length = jnp.broadcast_to(left_all[c, 4 * y + k][:, TPD * ROWS : TPD * ROWS + 1], TILE)
            mask[k] = jnp.where(sub.astype(F32) < length, 1.0, 0.0).astype(F32)

    def widen(first, count):
        def body(i, carry):
            cc, r = lax.div(i, 16), lax.rem(i, 16)
            yy, k = lax.div(r, 4), lax.rem(r, 4)
            tile = left_all[cc, r]
            for t in range(TPD):
                for j in range(ROWS):
                    lane = t * ROWS + j
                    left_wide[(yy * 2 + cc) * TPD + t, k, j] = jnp.broadcast_to(tile[:, lane : lane + 1], TILE)
            return carry

        lax.fori_loop(first, first + count, body, 0)

    def take_rows():
        wait(gd.at[pl.ds(0, 3), :, pl.ds(0, 2)], x_core)

    def vectors(first, count):
        def body(r, carry):
            for k in range(KS):
                for j in range(4):
                    g = gd[k, r, j, 0]
                    a = 1.0 / gd[k, r, j, 1]
                    b = g * a
                    v1[k, r, j] = g
                    v1[KS + k, r, j] = b
                    v1[2 * KS + k, r, j] = b * a
            return carry

        lax.fori_loop(first, first + count, body, 0)

    def mix(v, nk, first, count, step):
        rows = nk * ROWS

        def body(at, carry):
            for u in range(step):
                i = first + at * step + u
                yy, rest = lax.div(i, 2 * TPD), lax.rem(i, 2 * TPD)
                shift = shift_sm[lax.div(rest, TPD), yy, lax.rem(rest, TPD), 0]
                for nn in range(2):
                    m = 16 * (2 * c + nn) + here + shift
                    m = jnp.where(m >= NBLK, m - NBLK, m)
                    r, j4 = lax.rem(m, 16), lax.div(m, 16)
                    tiles = []
                    for k in range(nk):
                        src = v[k, r, j4]
                        total = None
                        for j in range(ROWS):
                            term = left_wide[i, k % KS, j] * src[j : j + 1, :]
                            total = term if total is None else total + term
                        tiles.append(total)
                    p = jnp.concatenate(tiles, axis=0)
                    hi = p.astype(BF16)
                    mixed[i, nn, 0:rows] = hi
                    mixed[i, nn, rows : 2 * rows] = (p - hi.astype(F32)).astype(BF16)
            return carry

        lax.fori_loop(0, count // step, body, 0)

    def terms_of(nn, yy, rows, cut):
        acc = None
        for q in range(2 * TPD):
            cc, t = q // TPD, q % TPD
            if cut:
                full = rbuf[nn, yy, cc, t]
                rh = full.astype(BF16)
                rl = (full - rh.astype(F32)).astype(BF16)
                r_hi[nn, yy, cc, t] = rh
                r_lo[nn, yy, cc, t] = rl
            else:
                rh = r_hi[nn, yy, cc, t]
                rl = r_lo[nn, yy, cc, t]
            i = yy * 2 * TPD + q
            both = jnp.dot(mixed[i, nn, 0 : 2 * rows], rh, preferred_element_type=F32)
            more = jnp.dot(mixed[i, nn, 0:rows], rl, preferred_element_type=F32)
            res = both[:rows] + both[rows:] + more
            acc = res if acc is None else acc + res
        return acc

    def product(v, nk, after=None):
        mix(v, nk, 0, TERMS, 4)
        for nn in range(2):
            acc = terms_of(nn, 0, nk * ROWS, False)
            for yy in range(1, 4):
                acc = acc + terms_of(nn, yy, nk * ROWS, False)
            y_sum[nn, pl.ds(0, nk)] = acc.reshape((nk,) + TILE)
            if after is not None:
                after(nn)

    tasks = {i: [lambda i=i: send_rows(i)] for i in range(8)}
    tasks[2].append(pass_left)
    tasks[4].append(pass_small)
    tasks[6].append(take_small)
    for i in range(4):
        tasks.setdefault(i + 7, []).append(lambda i=i: widen(8 * i, 8))
    tasks[11] = [lambda: pass_rows(1)]
    tasks[12] = [lambda: pass_rows(3)]
    tasks[13] = [lambda: pass_rows(2)]
    tasks[14] = [take_rows, lambda: vectors(0, 4)]
    for i in range(15, 18):
        tasks[i] = [lambda i=i: vectors(4 * i - 56, 4)]
    tasks[17].append(to_sm.wait)
    for i in range(18, 24):
        tasks[i] = [lambda i=i: mix(v1, 3 * KS, 4 * i - 72, 4, 1)]
    for i in range(1, 9):
        for t in range(TPD):
            ring_step(i, t)
            for task in tasks.get((i - 1) * TPD + t, []):
                task()
        for t in range(TPD):
            if i == 1:
                continue
            ring_step(i - 1, TPD + t)
        if i == 1:
            send_opposite()
    for t in range(TPD):
        ring_step(8, TPD + t)

    for nn in range(2):
        for k in range(KS):
            j = 2 * c + nn
            inv[k, nn] = 1.0 / gd[k, here, j, 1]
            piece[G, k, nn] = v1[k, here, j]
            piece[B, k, nn] = v1[KS + k, here, j]
            piece[E, k, nn] = v1[2 * KS + k, here, j]

    def gather(phase, v):
        def at(r, cc):
            return v.at[:, r, pl.ds(2 * cc, 2)]

        def start(nn=None):
            own = at(here, c) if nn is None else v.at[:, here, pl.ds(2 * c + nn, 1)]
            for o in offsets:
                send(own, own, ag_send.at[phase, 0], ag_recv.at[phase, o], peer(o))
            send(own, own, ag_send.at[phase, 1], ag_core.at[phase], other)

        def pass_on(first, last):
            for o in offsets[::-1][first:last]:
                r = sender(o)
                wait(at(r, c), ag_recv.at[phase, o])
                send(at(r, c), at(r, c), ag_send.at[phase, 1], ag_core.at[phase], other)

        def finish():
            wait(v.at[:, :, pl.ds(0, 2)], ag_core.at[phase])

        def sent():
            wait(v.at[:, pl.ds(0, 15), pl.ds(0, 2)], ag_send.at[phase, 0])
            wait(v.at[:, :, pl.ds(0, 2)], ag_send.at[phase, 1])

        return start, pass_on, finish, sent

    def dots(g):
        def start(pairs):
            d_rows[g] = jnp.zeros((16, BR), F32)
            for r, (a, b) in enumerate(pairs):
                prod = (piece[a] * piece[b]).reshape((2 * KS,) + TILE)
                d_rows[g, r : r + 1, :] = jnp.sum(jnp.sum(prod, axis=0), axis=0, keepdims=True)
            total = jnp.broadcast_to(jnp.sum(d_rows[g], axis=1, keepdims=True), (16, BR))
            at_row = lax.broadcasted_iota(jnp.int32, (16, BR), 0) == lax.broadcasted_iota(jnp.int32, (16, BR), 1)
            dz[g, z] = jnp.sum(jnp.where(at_row, total, 0.0), axis=0, keepdims=True)
            for p in zdevs:
                send(dz.at[g, z], dz.at[g, z], dot_send.at[g, 0], dot_recv.at[g, 0], p)

        def plane():
            wait(dz.at[g, pl.ds(0, 15)], dot_recv.at[g, 0])
            own = dp.at[g, 16 * c + here]
            dp[g, 16 * c + here] = jnp.sum(dz[g], axis=0)
            for o in offsets:
                send(own, own, dot_send.at[g, 1], dot_recv.at[g, 1], peer(o))
                send(own, own, dot_send.at[g, 1], dot_recv.at[g, 1], peer(o, 1 - c))
            send(own, own, dot_send.at[g, 1], dot_recv.at[g, 1], other)

        def done(pairs):
            wait(dp.at[g, pl.ds(0, 31)], dot_recv.at[g, 1])
            total = jnp.sum(dp[g], axis=0)
            return {p: jnp.broadcast_to(total[:, r : r + 1], TILE) for r, p in enumerate(pairs)}

        def sent():
            wait(dz.at[g, pl.ds(0, 15)], dot_send.at[g, 0])
            wait(dp.at[g, pl.ds(0, 31)], dot_send.at[g, 1])

        return start, plane, done, sent

    spot = 4 * lax.rem(y, 2) + x
    cd = lax.div(y, 2)
    keeps = cd == c

    def exchange(i, src, got):
        def start(blocks=(0, 1)):
            for k in range(KS):
                for nn in blocks:
                    stays = jnp.logical_and(jnp.logical_and(x == k, y == 2 * c + nn), keeps)

                    @pl.when(stays)
                    def _():
                        got[spot] = src[k, nn]

                    @pl.when(jnp.logical_not(stays))
                    def _():
                        where = dev(k, 2 * c + nn, z, cd)
                        send(src.at[k, nn], got.at[spot], out_send.at[i], out_recv.at[i], where)

        def arrived(sem):
            @pl.when(keeps)
            def _():
                wait(got.at[pl.ds(0, 7)], sem.at[i])

            @pl.when(jnp.logical_not(keeps))
            def _():
                wait(got, sem.at[i])

        return start, lambda: arrived(out_recv), lambda: arrived(out_send)

    ex_early, ex_t, ex_o = exchange(0, qs_src, qs_got), exchange(1, t_src, t_got), exchange(2, o_src, o_got)
    ag2, ag2b, ag3 = gather(0, v2), gather(1, v2b), gather(2, v3)
    early, late = dots(0), dots(1)

    apart = lax.rem(y + 8 * c - z + NZ, NZ)
    near = 1 - lax.div(lax.rem(apart + 9, NZ) + 9, NZ)
    for nn in (near, 1 - near):
        acc = None
        for d in (0, 1, 3, 2):
            yy = lax.rem(y - d + 4, 4)
            wait(rbuf.at[nn, yy], r_recv.at[nn, d])
            part = terms_of(nn, yy, 3 * KS * ROWS, True)
            acc = part if acc is None else acc + part
        acc = acc.reshape((3 * KS,) + TILE)
        for k in range(KS):
            h = acc[k] * mask[k]
            a = h * inv[k, nn]
            piece[H_, k, nn] = h
            piece[A_, k, nn] = a
            v2[k, here, 2 * c + nn] = a
            piece[AA, k, nn] = a * inv[k, nn]
            v2b[k, here, 2 * c + nn] = a * inv[k, nn]
            q = acc[KS + k] * mask[k]
            piece[Q, k, nn] = q
            qs_src[k, nn, 0] = q
            qs_src[k, nn, 1] = acc[2 * KS + k] * mask[k]
        ag2[0](nn)
    early[0](EARLY)
    ag2[1](0, 10)
    early[1]()
    ag2b[0]()
    ex_early[0]()
    ag2[1](10, 15)
    ag2[2]()

    product(v2, KS)
    dot = early[2](EARLY)
    f1 = jnp.sqrt(CELLS / (dot[G, G] + EPS))
    r1 = f1 * f1 * dot[G, H_] / CELLS
    for nn in range(2):
        for k in range(KS):
            pp = y_sum[nn, k] * mask[k] - r1 * piece[Q, k, nn]
            piece[PP, k, nn] = pp
            piece[AP, k, nn] = pp * inv[k, nn]
            v3[k, here, 2 * c + nn] = pp * inv[k, nn]
    ag3[0]()
    late[0](LATE)
    ag2b[1](0, 15)
    ag2b[2]()
    product(v2b, KS)
    for nn in range(2):
        for k in range(KS):
            t_src[k, nn] = y_sum[nn, k] * mask[k]
    ex_t[0]()
    ag3[1](0, 10)
    late[1]()
    ag3[1](10, 15)
    ag3[2]()

    def hand_over(nn):
        for k in range(KS):
            o_src[k, nn] = y_sum[nn, k] * mask[k]
        ex_o[0]((nn,))

    product(v3, KS, hand_over)
    dot.update(late[2](LATE))
    dot.update({(b, a): value for (a, b), value in dot.items()})

    c1 = f1 * f1 * (dot[G, A_] - r1 * dot[G, B]) / CELLS
    w = (-f1 * c1, -f1 * r1, f1)
    wy = (w[0], f1)
    x_x = [[dot[i, j] for j in (G, B, A_)] for i in (G, B, A_)]
    x_y = [[dot[G, H_], dot[G, PP]], [dot[G, A_], dot[B, PP]], [dot[A_, H_], dot[A_, PP]]]
    ax_y = [[dot[G, A_], dot[B, PP]], [dot[A_, B], dot[E, PP]], [dot[A_, A_], dot[AA, PP]]]
    ax_x = [
        [dot[G, B], dot[B, B], dot[A_, B]],
        [dot[B, B], dot[E, B], dot[E, A_]],
        [dot[A_, B], dot[E, A_], dot[AA, A_]],
    ]

    def along(weights, row):
        total = weights[0] * row[0]
        for weight, value in zip(weights[1:], row[1:], strict=True):
            total = total + weight * value
        return total

    def form(weights, m):
        return along(w, [along(weights, row) for row in m])

    def column(m, j):
        return [row[j] for row in m]

    uu, uk, uak, uau = form(w, x_x), form(wy, x_y), form(wy, ax_y), form(w, ax_x)
    gu, gk, uh = along(w, x_x[0]), along(wy, x_y[0]), along(w, column(x_y, 0))
    gak, gau, uah = along(wy, x_y[1]), along(w, x_x[1]), along(w, column(x_x, 2))
    f2 = jnp.sqrt(CELLS / (jnp.maximum(uu, 0.0) + EPS))
    b_ = f1 * f2 * (gk + uh) / (2.0 * CELLS)
    d_ = f2 * f2 * uk / CELLS
    h_ = (r1 - d_) / 2.0
    ritz = (r1 + d_) / 2.0 - jnp.sqrt(h_ * h_ + b_ * b_)
    big = jnp.maximum(jnp.abs(h_), jnp.abs(b_))
    safe = jnp.where(big > 0.0, big, 1.0)
    hs = jnp.where(big > 0.0, h_ / safe, 1.0)
    bs = b_ / safe
    rs = jnp.sqrt(hs * hs + bs * bs)
    larger = jnp.sqrt((rs + jnp.abs(hs)) / (2.0 * rs))
    smaller = jnp.abs(bs) / (2.0 * rs * larger)
    co = jnp.where(hs >= 0.0, larger, smaller)
    si = jnp.where(bs < 0.0, -1.0, 1.0) * jnp.where(hs >= 0.0, smaller, larger)
    n1, n2 = -si * f1, co * f2
    e1 = f1 * (n1 * (dot[G, A_] - ritz * dot[G, B]) + n2 * (gak - ritz * gau)) / CELLS
    e2 = f2 * (n1 * (uah - ritz * gau) + n2 * (uak - ritz * uau)) / CELLS
    t2 = {
        A_: n1 + n2 * w[0],
        B: -ritz * (n1 + n2 * w[0]),
        E: -ritz * n2 * w[1],
        AA: -ritz * n2 * w[2],
        AP: n2 * f1,
    }
    dot[A_, AP], dot[B, AP], dot[B, AA] = dot[AA, PP], dot[E, PP], dot[E, A_]
    dot.update({(b, a): value for (a, b), value in dot.items()})
    tt = jnp.zeros(TILE, F32)
    for i in t2:
        row = jnp.zeros(TILE, F32)
        for j in t2:
            row = row + t2[j] * dot[i, j]
        tt = tt + t2[i] * row
    square = tt - 2.0 * CELLS * (e1 * e1 + e2 * e2)
    square = square + e1 * e1 * f1 * f1 * dot[G, G] + e2 * e2 * f2 * f2 * uu + 2.0 * e1 * e2 * f1 * f2 * gu
    f3 = jnp.sqrt(CELLS / (jnp.maximum(square, 0.0) + EPS))
    coef = dict(t2)
    coef[G] = -e1 * f1 - e2 * f2 * w[0]
    coef[B] = coef[B] - e2 * f2 * w[1]
    coef[A_] = coef[A_] - e2 * f2 * w[2]
    coef = {i: f3 * value for i, value in coef.items()}
    coef_q = coef[B] + coef[A_] * r1
    for ex in (ex_early, ex_t, ex_o):
        ex[1]()
    for i in range(8):
        r = 8 * c + i
        a, ap, d = v2[x, r, y], v3[x, r, y], gd[x, r, y, 1]
        basis = coef[AP] * ap + coef[A_] * a + coef[AA] * v2b[x, r, y]
        basis = basis + coef[G] * v1[x, r, y] + coef[B] * v1[KS + x, r, y] + coef[E] * v1[2 * KS + x, r, y]
        image = coef[AP] * o_got[i] + (coef[A_] * ap + coef[G] * a) * d
        image = image + coef_q * qs_got[i, 0] + coef[E] * qs_got[i, 1] + coef[AA] * t_got[i]
        basis_ref[:, i * BR : (i + 1) * BR] = basis
        image_ref[:, i * BR : (i + 1) * BR] = image

    wait(zbuf.at[pl.ds(0, 15), pl.ds(0, TPD)], z_send)
    wait(zbuf.at[pl.ds(0, 12), pl.ds(0, TPD)], r_send)

    @pl.when(is_kind(0, 2))
    def _():
        wait(zbuf.at[0, pl.ds(0, TPD)], opp_send)

    wait(gd.at[pl.ds(0, 3)], x_send)
    wait(left_all.at[c, pl.ds(0, 3)], l_send.at[0])
    wait(left_all.at[c, pl.ds(0, 12)], l_send.at[1])
    wait(left_all.at[c], l_send.at[2])
    wait(shift_all.at[c, pl.ds(0, 3)], s_send.at[0])
    wait(shift_all.at[c], s_send.at[1])
    for ag in (ag2, ag2b, ag3):
        ag[3]()
    early[3]()
    late[3]()
    for ex in (ex_early, ex_t, ex_o):
        ex[2]()


def per_device(start_vector, precond_diag, left_env, right_env, right_shift, sector_length):
    vmem = pl.BlockSpec(memory_space=pltpu.VMEM)
    hbm = pl.BlockSpec(memory_space=pltpu.HBM)
    DMA = pltpu.SemaphoreType.DMA
    return pl.pallas_call(
        kernel,
        out_shape=[jax.ShapeDtypeStruct((ROWS, 1024), F32)] * 2,
        in_specs=[hbm] * 6,
        out_specs=[vmem, vmem],
        scratch_shapes=[
            pltpu.VMEM((ROWS, NBLK * BR), F32),
            pltpu.VMEM((ROWS, NBLK * BR), F32),
            pltpu.VMEM((TPD, ROWS, ROWS), F32),
            pltpu.SMEM((TPD,), jnp.int32),
            pltpu.SMEM((1,), jnp.int32),
            pltpu.VMEM((NZ, 2 * TPD, BR, BR), F32),
            pltpu.VMEM((2, 4, 2, TPD, BR, BR), F32),
            pltpu.VMEM((2, 4, 2, TPD, BR, BR), BF16),
            pltpu.VMEM((2, 4, 2, TPD, BR, BR), BF16),
            pltpu.VMEM((KS, 16, 4, 2) + TILE, F32),
            pltpu.VMEM((3 * KS, 16, 4) + TILE, F32),
            pltpu.VMEM((KS, 16, 4) + TILE, F32),
            pltpu.VMEM((KS, 16, 4) + TILE, F32),
            pltpu.VMEM((KS, 16, 4) + TILE, F32),
            pltpu.VMEM((TERMS, 2, 6 * KS * ROWS, BR), BF16),
            pltpu.VMEM((2, 3 * KS) + TILE, F32),
            pltpu.VMEM((9, KS, 2) + TILE, F32),
            pltpu.VMEM((KS, 2) + TILE, F32),
            pltpu.VMEM((2, 16) + TILE, F32),
            pltpu.VMEM((2, 4) + TILE, jnp.int32),
            pltpu.SMEM((2, 4) + TILE, jnp.int32),
            pltpu.VMEM((TERMS, KS, ROWS) + TILE, F32),
            pltpu.VMEM((KS,) + TILE, F32),
            pltpu.VMEM((2, 16, BR), F32),
            pltpu.VMEM((2, 16, 1, BR), F32),
            pltpu.VMEM((2, 32, 1, BR), F32),
            pltpu.VMEM((KS, 2, 2) + TILE, F32),
            pltpu.VMEM((8, 2) + TILE, F32),
            pltpu.VMEM((KS, 2) + TILE, F32),
            pltpu.VMEM((8,) + TILE, F32),
            pltpu.VMEM((KS, 2) + TILE, F32),
            pltpu.VMEM((8,) + TILE, F32),
            DMA((6,)),
            DMA,
            DMA((2 * TPD, 8)),
            DMA((2 * TPD, 8)),
            DMA,
            DMA((TPD,)),
            DMA,
            DMA((2, 4)),
            DMA,
            DMA((3,)),
            DMA,
            DMA((3,)),
            DMA((3,)),
            DMA((2,)),
            DMA((2,)),
            DMA,
            DMA((3, 2)),
            DMA((3, 16)),
            DMA((3,)),
            DMA((2, 2)),
            DMA((2, 2)),
            DMA((3,)),
            DMA((3,)),
        ],
        compiler_params=pltpu.CompilerParams(
            collective_id=0, has_side_effects=True, vmem_limit_bytes=60 * 1024 * 1024
        ),
        cost_estimate=pl.CostEstimate(flops=600_000_000, bytes_accessed=2_000_000, transcendentals=0),
    )(start_vector, precond_diag, left_env, right_env, right_shift, sector_length)


def solution(mesh):
    placed = (
        P("sec", None),
        P("sec", None),
        P("mpo", "sec", None),
        P("mpo", "sec", None),
        P("mpo"),
        P("sec"),
    )
    return jax.shard_map(
        per_device,
        mesh=mesh,
        in_specs=placed,
        out_specs=(P("sec", "mpo"), P("sec", "mpo")),
        check_vma=False,
    )
```
